32 devices in a mesh: orbit: 2 (over y), lon: 4 (over z), lat: 4 (over x, core).
Axes of the slice: x: 2, y: 2, z: 4, core: 2. Of those that a mesh axis runs over, the one named last changes fastest.
Arguments:
- kernel: float32 [20, 131072], P(None, ('orbit', 'lon', 'lat')), may hold values from 0.2 to 1.2
- residual: float32 [131072], P(('orbit', 'lon', 'lat')), may hold values from -6 to 6
- owner_block: int32 [131072, 1], P(('orbit', 'lon', 'lat')), may hold values from 0 to 15; in each aligned block of 4096 rows (0 to 4095, 4096 to 8191, ...) at most 1024 rows name the same one
- column: int32 [131072], P(('orbit', 'lon', 'lat')), may hold values from 0 to 1023
- time_step: int32 [131072], P(('orbit', 'lon', 'lat')), may hold values from 0 to 7
- horizontal: float32 [4, 72, 32, 512], P(None, None, 'lon', 'lat'), may hold values from 0.04 to 0.22
- vertical: float32 [71, 32, 512], P(None, 'lon', 'lat'), may hold values from 0.02 to 0.24
Outputs:
- adjoint_state: float32 [72, 32, 512], P(None, 'lon', 'lat')
- flux_gradient: float32 [32, 512], P('lon', 'lat')
The draws below stay inside these ranges and needn't reach their ends.
Inputs may be any that keep to these rules, and one draw needn't show every extreme that they name: `owner_block`: among the soundings of one device no block is named more than 1024 times, and in some device's soundings one block is named exactly 1024 times.
All inputs are finite; a program needn't handle non-finite values.
Results may differ from the reference program's by a relative error of at most 0.0001.
Values sent between devices are 32-bit elements; how exact they have to be, the bound alone decides.
A program may use at most 128 MiB of HBM per device.

```python
import math
import jax
import jax.numpy as jnp
import numpy as np
from jax import lax

LEV = 72
KLEV = 20
STEPS = 8
CLON = 8
CLAT = 128
S_DEV = 4096
OWNERS = 16
CAP = 1024
SOUNDINGS = 131072
NLON = 32
NLAT = 512
CCOL = 1024
N_LAT = 4


def touch_ends(array, stream_key, smallest, largest):
    place = [jax.random.randint(jax.random.fold_in(stream_key, axis), (), 0, length) for axis, length in enumerate(array.shape)]
    widest = array.shape.index(max(array.shape))
    next_to = place[:widest] + [(place[widest] + 1) % array.shape[widest]] + place[widest + 1:]
    return array.at[tuple(place)].set(smallest).at[tuple(next_to)].set(largest)


def block_levels(own_key, dims, shards, smallest, top_value):
    level = 1.0
    for position, blocks in shards:
        steps = jax.random.uniform(jax.random.fold_in(jax.random.fold_in(own_key, 6), position), (blocks,), jnp.float32, smallest / len(shards), top_value / len(shards))
        level = level * jnp.repeat(jnp.exp(steps), dims[position] // blocks).reshape((-1,) + (1,) * (len(dims) - 1 - position))
    return level


def assign_block(key, own, number, rows, count, top, bound, slope):
    order = jax.random.permutation(key, count)
    heavy_load, ordinary = shares(count, rows * top, bound, slope, True), shares(count, rows * top, bound, slope, False)
    places = jnp.arange(count)

    def named(sizes, turn):
        used = int((sizes > 0).sum())
        fixed = max(1, used // 4)
        moved = fixed + (places - fixed + turn * (used - fixed)) % max(1, count - fixed)
        return jnp.zeros((count,), jnp.int32).at[order[jnp.where(places < fixed, places, moved)]].set(jnp.asarray(sizes, jnp.int32))

    sizes = jnp.where(number % 4 == 0, named(heavy_load, number // 4), named(ordinary, number - number // 4 - 1))
    mixed = jax.random.permutation(jax.random.fold_in(own, 3), count)
    source_of, taker = mixed[0:count // 2 * 2:2], mixed[1:count // 2 * 2:2]
    margin = jnp.minimum(sizes[source_of] - 1, bound - sizes[taker]) // 2
    margin = jnp.where((source_of == order[0]) | (taker == order[0]) | (sizes[taker] == 0), 0, jnp.maximum(margin, 0))
    moved = jax.random.randint(jax.random.fold_in(own, 4), (count // 2,), 0, 1 << 20) % (margin + 1)
    sizes = sizes.at[source_of].add(-moved).at[taker].add(moved)
    members = jnp.searchsorted(jnp.cumsum(sizes), jnp.arange(rows * top), side="right").astype(jnp.int32)
    grid = members.reshape(top, rows).T
    grid = grid[jax.random.permutation(jax.random.fold_in(own, 1), rows)]
    turn = jax.random.randint(jax.random.fold_in(own, 2), (rows, 1), 0, top)
    return jnp.take_along_axis(grid, (jnp.arange(top)[None, :] + turn) % top, axis=1)


def shares(amount, total, reach, skew, full):
    portions = [(1 << 20) // math.isqrt(rank ** skew) + 1 for rank in range(1, amount + 1)]
    largest = reach if full else min(reach, max(-(-total // amount), total * portions[0] // sum(portions)))
    least = 1 if total - largest >= amount - 1 else 0
    counts, spare = [largest] + [least] * (amount - 1), total - largest - least * (amount - 1)
    while spare > 0:
        free = [i for i in range(1, amount) if counts[i] < largest] or [i for i in range(1, amount) if counts[i] < reach]
        mass, budget = sum([portions[i] for i in free]), spare
        for i in free:
            addition = min(reach - counts[i], max(1, budget * portions[i] // mass), spare)
            counts[i] = counts[i] + addition
            spare = spare - addition
    return np.array(counts)


def centred(key, shape, width, limit, pieces=(), kind=jnp.bfloat16):
    array = jax.random.normal(key, shape, jnp.float32) * width
    if len(pieces) > 0:
        array = block_levels(key, shape, pieces, -0.22, 0.18) * array
    return jnp.clip(array, min=-limit, max=limit).astype(kind)


def setup_inputs(seed: int = 0) -> dict:
    streams_of = jax.random.split(jax.random.key(seed), 8)
    kernel = jnp.clip(0.2 + 1 * jax.random.uniform(streams_of[0], (KLEV, SOUNDINGS), jnp.float32) ** block_levels(streams_of[0], (KLEV, SOUNDINGS), ((1, 32),), -0.2, 0.2), 0.2, 1.2)
    residual = centred(streams_of[1], (SOUNDINGS,), 1.0, 6.0, ((0, 32),), jnp.float32)
    owner_block_keys = jax.random.split(jax.random.fold_in(streams_of[2], 1), SOUNDINGS // S_DEV)
    owner_block_turns = jax.random.permutation(jax.random.fold_in(streams_of[2], 3), SOUNDINGS // S_DEV)
    owner_block = jax.vmap(lambda own, number: assign_block(jax.random.fold_in(streams_of[2], 2), own, number, S_DEV, OWNERS, 1, CAP, 2))(owner_block_keys, owner_block_turns).reshape((SOUNDINGS, 1))
    column = touch_ends(jax.random.randint(streams_of[3], (SOUNDINGS,), 0, CCOL), jax.random.fold_in(streams_of[3], 1), 0, CCOL - 1).astype(jnp.int32)
    time_step = touch_ends(jax.random.randint(streams_of[4], (SOUNDINGS,), 0, STEPS), jax.random.fold_in(streams_of[4], 1), 0, STEPS - 1).astype(jnp.int32)
    horizontal = jnp.clip(0.04 + 0.18 * jax.random.uniform(streams_of[5], (4, LEV, NLON, NLAT), jnp.float32) ** block_levels(streams_of[5], (4, LEV, NLON, NLAT), ((2, 4), (3, 4)), -0.2, 0.2), 0.04, 0.22)
    vertical = jnp.clip(0.02 + 0.22 * jax.random.uniform(streams_of[6], (LEV - 1, NLON, NLAT), jnp.float32) ** block_levels(streams_of[6], (LEV - 1, NLON, NLAT), ((1, 4), (2, 4)), -0.2, 0.2), 0.02, 0.24)
    return {"kernel": kernel, "residual": residual, "owner_block": owner_block, "column": column, "time_step": time_step, "horizontal": horizontal, "vertical": vertical}


def level_map(levels, kernel_levels):
    heights = jnp.arange(levels, dtype=jnp.float32)
    centre = jnp.clip((heights + 0.5) * kernel_levels / levels - 0.5, 0.0, kernel_levels - 1.0)
    knots = jnp.arange(kernel_levels, dtype=jnp.float32)
    return jnp.maximum(0.0, 1.0 - jnp.abs(centre[:, None] - knots[None, :]))


def reference(kernel, residual, owner_block, column, time_step, horizontal, vertical):
    columns = NLON * NLAT
    owner_ids = owner_block[:, 0]
    longitude = (owner_ids // N_LAT) * CLON + column // CLAT
    latitude = (owner_ids % N_LAT) * CLAT + column % CLAT
    segment = (time_step * columns + longitude * NLAT + latitude).astype(jnp.int32)
    weighted = kernel * residual[None, :]
    binned = jnp.zeros((KLEV, STEPS * columns), jnp.float32).at[:, segment].add(weighted)
    binned = binned.reshape(KLEV, STEPS, columns)
    interp = level_map(LEV, KLEV)
    diagonal_part = 1.0 - horizontal[0] - horizontal[1] - horizontal[2] - horizontal[3]
    adjoint = jnp.zeros((LEV, NLON, NLAT), jnp.float32)
    flux_total = jnp.zeros((NLON, NLAT), jnp.float32)
    for step_index in range(STEPS - 1, -1, -1):
        forcing = jnp.dot(interp, binned[:, step_index, :], precision=lax.Precision.HIGHEST)
        forced = adjoint + forcing.reshape(LEV, NLON, NLAT)
        up_flux = vertical * (forced[1:] - forced[:-1])
        mixed = forced + jnp.pad(up_flux, ((0, 1), (0, 0), (0, 0))) - jnp.pad(up_flux, ((1, 0), (0, 0), (0, 0)))
        terms = horizontal * mixed[None]
        east_term = jnp.roll(terms[0], 1, axis=1)
        west_term = jnp.roll(terms[1], -1, axis=1)
        north_term = jnp.pad(terms[2][:, :, :-1], ((0, 0), (0, 0), (1, 0)))
        south_term = jnp.pad(terms[3][:, :, 1:], ((0, 0), (0, 0), (0, 1)))
        adjoint = diagonal_part * mixed + east_term + west_term + north_term + south_term
        flux_total = flux_total + adjoint[0]
    return adjoint, flux_total
```

```python
import functools

import jax
import jax.numpy as jnp
import numpy as np
from jax import lax
from jax.experimental import pallas as pl
from jax.experimental.pallas import tpu as pltpu
from jax.sharding import PartitionSpec as P

STEPS = 8
CLON = 8
CLAT = 128
CELLS = CLON * CLAT
ROWS = 24
CHUNK = 256
F32 = jnp.float32
BF16 = jnp.bfloat16
VMEM_LIMIT = 48 * 1024 * 1024
NT = (((1,), (1,)), ((), ()))


def level_weights(levels, kernel_levels):
    one = np.float32
    heights = np.arange(levels, dtype=np.float32)
    centre = np.clip((heights + one(0.5)) * one(kernel_levels) / one(levels) - one(0.5),
                     one(0), one(kernel_levels - 1))
    knots = np.arange(kernel_levels, dtype=np.float32)
    return np.maximum(one(0), one(1) - np.abs(centre[:, None] - knots[None, :]))


def split(values):
    high = values.astype(BF16)
    return high, (values - high.astype(F32)).astype(BF16)


def pack_kernel(owners, kernel_hbm, residual_hbm, owner_hbm, column_hbm, time_hbm, out_ref,
                kernel_ref, residual_ref, owner_ref, column_ref, time_ref, own_ref, data_ref,
                place_ref, left_ref, sorted_ref, sem):
    levels, count = kernel_hbm.shape
    slot_rows = out_ref.shape[2]
    chunks = count // CHUNK
    loads = [pltpu.make_async_copy(source, target, sem.at[i]) for i, (source, target) in enumerate(
        ((owner_hbm, owner_ref), (column_hbm, column_ref), (time_hbm, time_ref),
         (residual_hbm, residual_ref), (kernel_hbm, kernel_ref)))]
    for load in loads:
        load.start()
    heights = sorted_ref.shape[1]
    filled = count // CLAT
    sorted_ref[:, filled:, :] = jnp.zeros((ROWS, heights - filled, CLAT), F32)
    earlier = (lax.broadcasted_iota(jnp.int32, (CHUNK, CHUNK), 0)
               < lax.broadcasted_iota(jnp.int32, (CHUNK, CHUNK), 1)).astype(F32).astype(BF16)
    names = lax.broadcasted_iota(jnp.int32, (owners, CHUNK), 0)
    ones = jnp.ones((CHUNK, CLAT), F32).astype(BF16)
    before = (lax.broadcasted_iota(jnp.int32, (owners, owners), 1)
              < lax.broadcasted_iota(jnp.int32, (owners, owners), 0)).astype(F32)

    loads[0].wait()
    for c in range(chunks):
        own_ref[c * owners:(c + 1) * owners] = (
            owner_ref[:, c * CHUNK:(c + 1) * CHUNK] == names).astype(F32).astype(BF16)
    inside = jnp.dot(own_ref[...], earlier, preferred_element_type=F32)
    counts = jnp.dot(own_ref[...], ones, preferred_element_type=F32)
    parts = [counts[c * owners:(c + 1) * owners] for c in range(chunks)]
    totals = functools.reduce(lambda x, y: x + y, parts)
    starts = jnp.dot(before, totals, precision=lax.Precision.HIGHEST, preferred_element_type=F32)
    carry = starts
    for c in range(chunks):
        own = own_ref[c * owners:(c + 1) * owners].astype(F32)
        wide = jnp.concatenate([carry] * (CHUNK // CLAT), axis=1)
        place_ref[:, c * CHUNK:(c + 1) * CHUNK] = jnp.sum(
            own * (inside[c * owners:(c + 1) * owners] + wide), axis=0,
            keepdims=True).astype(jnp.int32)
        carry = carry + parts[c]

    for load in loads[1:]:
        load.wait()
    high, low = split(kernel_ref[...] * residual_ref[...])
    seg_high = (time_ref[...] * CLON + column_ref[...] // CLAT).astype(F32)
    seg_low = (column_ref[...] % CLAT).astype(F32)
    spare = jnp.zeros((ROWS - levels - 1, count), F32)
    data_ref[...] = jnp.concatenate(
        [high.astype(F32), seg_high * float(CLAT), spare, low.astype(F32), seg_low, spare],
        axis=0).astype(BF16)

    groups = count // CHUNK
    span = min(count, 4 * CHUNK)
    inner = lax.broadcasted_iota(jnp.int32, (CHUNK, span), 0).astype(F32).astype(BF16)
    none = jnp.zeros((2 * ROWS, span), BF16)
    total = None
    for c in range(count // span):
        here = slice(c * span, (c + 1) * span)
        place = place_ref[:, here]
        outer = jnp.broadcast_to((place // CHUNK).astype(F32), (2 * ROWS, span)).astype(BF16)
        offset = jnp.broadcast_to((place % CHUNK).astype(F32), (CHUNK, span)).astype(BF16)
        data = data_ref[:, here]
        for g in range(groups):
            left_ref[g * 2 * ROWS:(g + 1) * 2 * ROWS] = jnp.where(
                outer == jnp.asarray(g, BF16), data, none)
        chosen = jnp.where(offset == inner, jnp.ones((), BF16), jnp.zeros((), BF16))
        got = lax.dot_general(left_ref[...], chosen, NT, preferred_element_type=F32)
        total = got if total is None else total + got
    for g in range(groups):
        both = total[2 * ROWS * g:2 * ROWS * g + ROWS] + total[2 * ROWS * g + ROWS:2 * ROWS * (g + 1)]
        for p in range(CHUNK // CLAT):
            sorted_ref[:, g * (CHUNK // CLAT) + p, :] = both[:, p * CLAT:(p + 1) * CLAT]

    shape = (levels + 1, slot_rows, CLAT)
    lane = lax.broadcasted_iota(jnp.int32, shape, 2)
    slot = (lax.broadcasted_iota(jnp.int32, (1, slot_rows, CLAT), 1) * CLAT
            + lax.broadcasted_iota(jnp.int32, (1, slot_rows, CLAT), 2))
    first = [jnp.max(starts[o:o + 1]).astype(jnp.int32) for o in range(owners)] + [count]
    for o in range(owners):
        row, shift = first[o] // CLAT, lax.rem(first[o], CLAT)
        back = lax.rem(CLAT - shift, CLAT)
        one = pltpu.roll(sorted_ref[0:levels + 1, pl.ds(row, slot_rows), :], back, 2)
        two = pltpu.roll(sorted_ref[0:levels + 1, pl.ds(row + 1, slot_rows), :], back, 2)
        run = jnp.where(lane < CLAT - shift, one, two)
        out_ref[o, 0:levels] = run[0:levels]
        out_ref[o, levels:] = jnp.where(slot < first[o + 1] - first[o], run[levels:], -1.0)


def pack(kernel, residual, owner_block, column, time_step, owners, capacity):
    levels, count = kernel.shape
    slot_rows = capacity // CLAT
    heights = -(-(count // CLAT + slot_rows + 1) // 8) * 8
    row = pltpu.VMEM((1, count), jnp.int32)
    chunks = count // CHUNK
    return pl.pallas_call(
        functools.partial(pack_kernel, owners),
        out_shape=jax.ShapeDtypeStruct((owners, levels + 1, slot_rows, CLAT), F32),
        in_specs=[pl.BlockSpec(memory_space=pltpu.HBM)] * 5,
        out_specs=pl.BlockSpec(memory_space=pltpu.VMEM),
        scratch_shapes=[
            pltpu.VMEM(kernel.shape, F32),
            pltpu.VMEM((1, count), F32),
            row, row, row,
            pltpu.VMEM((chunks * owners, CHUNK), BF16),
            pltpu.VMEM((2 * ROWS, count), BF16),
            row,
            pltpu.VMEM((2 * ROWS * chunks, min(count, 4 * CHUNK)), BF16),
            pltpu.VMEM((ROWS, heights, CLAT), F32),
            pltpu.SemaphoreType.DMA((5,)),
        ],
        compiler_params=pltpu.CompilerParams(vmem_limit_bytes=VMEM_LIMIT),
    )(kernel, residual.reshape(1, count), owner_block.reshape(1, count),
      column.reshape(1, count), time_step.reshape(1, count))


def bin_kernel(levels, lons, lats, slots_ref, out_ref, got_ref, total_ref, left_ref, chosen_ref, send_sem, recv_sem):
    owners, _, slot_rows, _ = slots_ref.shape
    lon, lat = lax.axis_index("lon"), lax.axis_index("lat")
    mesh_id = pl.DeviceIdType.MESH

    def peer(d):
        return lax.rem(lon + d // lats, lons), lax.rem(lat + lax.rem(d, lats), lats)

    def slot_copy(d):
        to_lon, to_lat = peer(d)
        return pltpu.make_async_remote_copy(
            src_ref=slots_ref.at[to_lon * lats + to_lat], dst_ref=got_ref.at[d],
            send_sem=send_sem.at[d], recv_sem=recv_sem.at[d],
            device_id={"lon": to_lon, "lat": to_lat}, device_id_type=mesh_id)

    barrier = pltpu.get_barrier_semaphore()

    def greet(d, _):
        to_lon, to_lat = peer(d)
        pl.semaphore_signal(barrier, inc=1, device_id={"lon": to_lon, "lat": to_lat},
                            device_id_type=mesh_id)
        return 0

    lax.fori_loop(1, owners, greet, 0)
    pl.semaphore_wait(barrier, owners - 1)

    def turn(i):
        return jnp.where(lax.rem(i, 2) == 1, (i + 1) // 2, lax.rem(owners - i // 2, owners))

    def begin(i, _):
        slot_copy(turn(i)).start()
        return 0

    lax.fori_loop(1, owners, begin, 0)
    total_ref[...] = jnp.zeros_like(total_ref)
    got_ref[0] = slots_ref[lon * lats + lat]

    def collect(i, _):
        d = turn(i)

        @pl.when(i > 0)
        def _():
            slot_copy(d).wait_recv()

        rows = jnp.concatenate([got_ref[d, :, i, :] for i in range(slot_rows)], axis=1)
        width = rows.shape[1]
        segment = rows[levels:levels + 1].astype(jnp.int32)
        values = rows[0:levels]
        high = values.astype(BF16).astype(F32)
        spare = jnp.zeros((ROWS - levels, width), F32)
        data = jnp.concatenate([high, spare, values - high, spare], axis=0).astype(BF16)
        step = jnp.broadcast_to((segment >> 10).astype(F32), data.shape).astype(BF16)
        for j in range(STEPS):
            left_ref[j * 2 * ROWS:(j + 1) * 2 * ROWS] = jnp.where(
                step == jnp.asarray(j, BF16), data, jnp.zeros(data.shape, BF16))
        lane = lax.broadcasted_iota(jnp.int32, (CLAT, width), 0).astype(F32).astype(BF16)
        for i in range(CLON):
            key = jnp.where(((segment >> 7) & (CLON - 1)) == i, segment & (CLAT - 1), -1).astype(F32)
            key = jnp.broadcast_to(key, (CLAT, width)).astype(BF16)
            chosen_ref[i * CLAT:(i + 1) * CLAT] = jnp.where(
                key == lane, jnp.ones((), BF16), jnp.zeros((), BF16))
        total_ref[...] += lax.dot_general(
            left_ref[...], chosen_ref[...], NT, preferred_element_type=F32)
        return 0

    lax.fori_loop(0, owners, collect, 0)
    for j in range(STEPS):
        top = j * 2 * ROWS
        part = total_ref[top:top + levels] + total_ref[top + ROWS:top + ROWS + levels]
        for i in range(CLON):
            out_ref[j, :, i, :] = part[:, i * CLAT:(i + 1) * CLAT]

    def finish(d, _):
        slot_copy(d).wait_send()
        return 0

    lax.fori_loop(1, owners, finish, 0)


def bin_soundings(slots, levels):
    lons, lats = lax.axis_size("lon"), lax.axis_size("lat")
    vmem = pl.BlockSpec(memory_space=pltpu.VMEM)
    return pl.pallas_call(
        functools.partial(bin_kernel, levels, lons, lats),
        out_shape=jax.ShapeDtypeStruct((STEPS, levels, CLON, CLAT), F32),
        in_specs=[vmem],
        out_specs=vmem,
        scratch_shapes=[
            pltpu.VMEM(slots.shape, F32),
            pltpu.VMEM((2 * STEPS * ROWS, CELLS), F32),
            pltpu.VMEM((2 * STEPS * ROWS, slots.shape[2] * CLAT), BF16),
            pltpu.VMEM((CELLS, slots.shape[2] * CLAT), BF16),
            pltpu.SemaphoreType.DMA((lons * lats,)),
            pltpu.SemaphoreType.DMA((lons * lats,)),
        ],
        compiler_params=pltpu.CompilerParams(
            collective_id=1, has_side_effects=True, vmem_limit_bytes=VMEM_LIMIT),
    )(slots)


def steps_kernel(orbits, lons, lats, weights, bins_ref, horizontal_ref, vertical_ref,
                 adjoint_ref, flux_ref, other_ref, forced_ref, mixed_ref, diagonal_ref, weight_ref,
                 edge_ref, lon_out, lon_in, lat_out, lat_in,
                 orbit_send, orbit_recv, edge_send, edge_recv):
    levels = adjoint_ref.shape[0]
    lon, lat, orbit = lax.axis_index("lon"), lax.axis_index("lat"), lax.axis_index("orbit")
    east, west = lax.rem(lon + 1, lons), lax.rem(lon + lons - 1, lons)
    partner = 1 - orbit
    mesh_id = pl.DeviceIdType.MESH
    barrier = pltpu.get_barrier_semaphore()
    pl.semaphore_signal(barrier, inc=1, device_id={"lon": east}, device_id_type=mesh_id)
    pl.semaphore_signal(barrier, inc=1, device_id={"lon": west}, device_id_type=mesh_id)
    pl.semaphore_signal(barrier, inc=1, device_id={"orbit": partner}, device_id_type=mesh_id)

    @pl.when(lat < lats - 1)
    def _():
        pl.semaphore_signal(barrier, inc=1, device_id={"lat": lat + 1}, device_id_type=mesh_id)

    @pl.when(lat > 0)
    def _():
        pl.semaphore_signal(barrier, inc=1, device_id={"lat": lat - 1}, device_id_type=mesh_id)

    peers = 3 + jnp.where(lat > 0, 1, 0) + jnp.where(lat < lats - 1, 1, 0)
    pl.semaphore_wait(barrier, peers)

    def orbit_copy(j):
        return pltpu.make_async_remote_copy(
            src_ref=bins_ref.at[j], dst_ref=other_ref.at[j],
            send_sem=orbit_send.at[j], recv_sem=orbit_recv.at[j],
            device_id={"orbit": partner}, device_id_type=mesh_id)

    def edge_copy(t, side):
        out, into = (lon_out, lon_in) if side < 2 else (lat_out, lat_in)
        device = ({"lon": east}, {"lon": west}, {"lat": lat + 1}, {"lat": lat - 1})[side]
        return pltpu.make_async_remote_copy(
            src_ref=out.at[side % 2, t], dst_ref=into.at[side % 2, t],
            send_sem=edge_send.at[side, t], recv_sem=edge_recv.at[side, t],
            device_id=device, device_id_type=mesh_id)

    def begin(t, _):
        orbit_copy(STEPS - 1 - t).start()
        return 0

    lax.fori_loop(0, STEPS, begin, 0)

    @pl.when(lat == 0)
    def _():
        lat_in[0] = jnp.zeros(lat_in.shape[1:], F32)

    @pl.when(lat == lats - 1)
    def _():
        lat_in[1] = jnp.zeros(lat_in.shape[1:], F32)

    part = (8, CLON, CLAT)
    lane = lax.broadcasted_iota(jnp.int32, part, 2)
    sub = lax.broadcasted_iota(jnp.int32, part, 1)
    level = lax.broadcasted_iota(jnp.int32, part, 0)
    chunks = range(0, levels, 8)
    pairs = CLAT // 2

    def gather_edge(total, values, side, first):
        column = values[:, :, CLAT - 1:CLAT] if side == 0 else values[:, :, 0:1]
        where = (2 * first - side) % CLAT
        place = (where + 2 * level) & (CLAT - 1)
        mine = jnp.sum(jnp.where(lane == place, jnp.broadcast_to(column, part), 0.0), axis=0)
        group = first // pairs
        total[group] = mine if total[group] is None else total[group] + mine

    groups = lat_in.shape[2]
    edge_weight = [[None] * groups, [None] * groups]
    for a in chunks:
        here = slice(a, a + 8)
        h = [horizontal_ref[d, here] for d in range(4)]
        diagonal_ref[here] = 1.0 - h[0] - h[1] - h[2] - h[3]
        weight_ref[0, here] = jnp.where(sub == 0, 0.0, pltpu.roll(h[0], 1, 1))
        weight_ref[1, here] = jnp.where(sub == CLON - 1, 0.0, pltpu.roll(h[1], CLON - 1, 1))
        weight_ref[2, here] = jnp.where(lane == 0, 0.0, pltpu.roll(h[2], 1, 2))
        weight_ref[3, here] = jnp.where(lane == CLAT - 1, 0.0, pltpu.roll(h[3], CLAT - 1, 2))
        gather_edge(edge_weight[0], h[2], 0, a)
        gather_edge(edge_weight[1], h[3], 1, a)
    for side in range(2):
        for g in range(groups):
            edge_ref[side, g] = edge_weight[side][g]

    def force(bins, a):
        forcing = []
        for l in range(a, a + 8):
            parts = [bins[k:k + 1] * float(weights[l, k]) for k in np.nonzero(weights[l])[0]]
            forcing.append(functools.reduce(lambda x, y: x + y, parts))
        return jnp.concatenate(forcing, axis=0)

    orbit_copy(STEPS - 1).wait_recv()
    bins = bins_ref[STEPS - 1] + other_ref[STEPS - 1]
    for a in chunks:
        forced_ref[a:a + 8] = force(bins, a)
    flux_ref[...] = jnp.zeros_like(flux_ref)
    none = jnp.zeros((1, CLON, CLAT), F32)

    def advance(t, _):
        edges = [[None] * groups, [None] * groups]
        for a in chunks:
            low, high = max(a - 1, 0), min(a + 9, levels)
            forced = forced_ref[low:high]
            up = vertical_ref[low:high - 1] * (forced[1:] - forced[:-1])
            if a == 0:
                up = jnp.concatenate([none, up], axis=0)
            if a + 8 == levels:
                up = jnp.concatenate([up, none], axis=0)
            mixed = forced_ref[a:a + 8] + up[1:] - up[:-1]
            mixed_ref[a:a + 8] = mixed
            gather_edge(edges[0], mixed, 0, a)
            gather_edge(edges[1], mixed, 1, a)
        lon_out[0, t] = horizontal_ref[0, :, CLON - 1, :] * mixed_ref[:, CLON - 1, :]
        edge_copy(t, 0).start()
        lon_out[1, t] = horizontal_ref[1, :, 0, :] * mixed_ref[:, 0, :]
        edge_copy(t, 1).start()
        for side in range(2):
            for g in range(groups):
                lat_out[side, t, g] = edge_ref[side, g] * edges[side][g]

        @pl.when(lat < lats - 1)
        def _():
            edge_copy(t, 2).start()

        @pl.when(lat > 0)
        def _():
            edge_copy(t, 3).start()

        for a in chunks:
            here = slice(a, a + 8)
            mixed = mixed_ref[here]
            adjoint_ref[here] = (diagonal_ref[here] * mixed
                                 + weight_ref[0, here] * pltpu.roll(mixed, 1, 1)
                                 + weight_ref[1, here] * pltpu.roll(mixed, CLON - 1, 1)
                                 + weight_ref[2, here] * pltpu.roll(mixed, 1, 2)
                                 + weight_ref[3, here] * pltpu.roll(mixed, CLAT - 1, 2))

        j = jnp.maximum(STEPS - 2 - t, 0)

        @pl.when(t < STEPS - 1)
        def _():
            orbit_copy(j).wait_recv()

        @pl.when(lat > 0)
        def _():
            edge_copy(t, 2).wait_recv()

        @pl.when(lat < lats - 1)
        def _():
            edge_copy(t, 3).wait_recv()

        edge_copy(t, 0).wait_recv()
        edge_copy(t, 1).wait_recv()
        adjoint_ref[:, 0, :] = adjoint_ref[:, 0, :] + lon_in[0, t]
        adjoint_ref[:, CLON - 1, :] = adjoint_ref[:, CLON - 1, :] + lon_in[1, t]
        bins = bins_ref[j] + other_ref[j]
        sides = [lat_in[0, t, g] + lat_in[1, t, g] for g in range(groups)]
        outer = (lane == 0) | (lane == CLAT - 1)
        for a in chunks:
            near = jnp.stack([pltpu.roll(sides[l // pairs], -2 * l % CLAT, 1)
                              for l in range(a, a + 8)])
            result = adjoint_ref[a:a + 8] + jnp.where(outer, near, 0.0)
            adjoint_ref[a:a + 8] = result
            forced_ref[a:a + 8] = result + force(bins, a)
            if a == 0:
                flux_ref[...] += result[0]
        return 0

    lax.fori_loop(0, STEPS, advance, 0)

    def finish(t, _):
        orbit_copy(t).wait_send()
        edge_copy(t, 0).wait_send()
        edge_copy(t, 1).wait_send()

        @pl.when(lat < lats - 1)
        def _():
            edge_copy(t, 2).wait_send()

        @pl.when(lat > 0)
        def _():
            edge_copy(t, 3).wait_send()

        return 0

    lax.fori_loop(0, STEPS, finish, 0)


def transport(bins, horizontal, vertical):
    levels = horizontal.shape[1]
    kernel_levels = bins.shape[1]
    orbits, lons, lats = (lax.axis_size(name) for name in ("orbit", "lon", "lat"))
    vmem = pl.BlockSpec(memory_space=pltpu.VMEM)
    block = (levels, CLON, CLAT)
    groups = -(-2 * levels // CLAT)
    return pl.pallas_call(
        functools.partial(steps_kernel, orbits, lons, lats, level_weights(levels, kernel_levels)),
        out_shape=(jax.ShapeDtypeStruct(block, F32), jax.ShapeDtypeStruct((CLON, CLAT), F32)),
        in_specs=[vmem] * 3,
        out_specs=(vmem, vmem),
        scratch_shapes=[
            pltpu.VMEM(bins.shape, F32),
            pltpu.VMEM(block, F32),
            pltpu.VMEM(block, F32),
            pltpu.VMEM(block, F32),
            pltpu.VMEM((4,) + block, F32),
            pltpu.VMEM((2, groups, CLON, CLAT), F32),
            pltpu.VMEM((2, STEPS, levels, CLAT), F32),
            pltpu.VMEM((2, STEPS, levels, CLAT), F32),
            pltpu.VMEM((2, STEPS, groups, CLON, CLAT), F32),
            pltpu.VMEM((2, STEPS, groups, CLON, CLAT), F32),
            pltpu.SemaphoreType.DMA((STEPS,)),
            pltpu.SemaphoreType.DMA((STEPS,)),
            pltpu.SemaphoreType.DMA((4, STEPS)),
            pltpu.SemaphoreType.DMA((4, STEPS)),
        ],
        compiler_params=pltpu.CompilerParams(
            collective_id=0, has_side_effects=True, vmem_limit_bytes=VMEM_LIMIT),
    )(bins, horizontal, vertical)


def per_device(kernel, residual, owner_block, column, time_step, horizontal, vertical):
    owners = lax.axis_size("lon") * lax.axis_size("lat")
    capacity = 4 * kernel.shape[1] // owners
    slots = pack(kernel, residual, owner_block, column, time_step, owners, capacity)
    return transport(bin_soundings(slots, kernel.shape[0]), horizontal, vertical)


def solution(mesh):
    placed = (
        P(None, ("orbit", "lon", "lat")),
        P(("orbit", "lon", "lat")),
        P(("orbit", "lon", "lat"), None),
        P(("orbit", "lon", "lat")),
        P(("orbit", "lon", "lat")),
        P(None, None, "lon", "lat"),
        P(None, "lon", "lat"),
    )
    return jax.shard_map(
        per_device,
        mesh=mesh,
        in_specs=placed,
        out_specs=(P(None, "lon", "lat"), P("lon", "lat")),
        check_vma=False,
    )
```

```python
import functools

import jax
import jax.numpy as jnp
import numpy as np
from jax import lax
from jax.experimental import pallas as pl
from jax.experimental.pallas import tpu as pltpu
from jax.sharding import PartitionSpec as P

STEPS = 8
CLON = 8
CLAT = 128
CELLS = CLON * CLAT
ROWS = 24
CHUNK = 256
F32 = jnp.float32
BF16 = jnp.bfloat16
VMEM_LIMIT = 48 * 1024 * 1024
NT = (((1,), (1,)), ((), ()))


def level_weights(levels, kernel_levels):
    one = np.float32
    heights = np.arange(levels, dtype=np.float32)
    centre = np.clip((heights + one(0.5)) * one(kernel_levels) / one(levels) - one(0.5),
                     one(0), one(kernel_levels - 1))
    knots = np.arange(kernel_levels, dtype=np.float32)
    return np.maximum(one(0), one(1) - np.abs(centre[:, None] - knots[None, :]))


def split(values):
    high = values.astype(BF16)
    return high, (values - high.astype(F32)).astype(BF16)


def pack_kernel(owners, kernel_hbm, residual_hbm, owner_hbm, column_hbm, time_hbm, out_ref,
                kernel_ref, residual_ref, owner_ref, column_ref, time_ref, own_ref, data_ref,
                place_ref, left_ref, sorted_ref, sem):
    levels, count = kernel_hbm.shape
    slot_rows = out_ref.shape[2]
    chunks = count // CHUNK
    loads = [pltpu.make_async_copy(source, target, sem.at[i]) for i, (source, target) in enumerate(
        ((owner_hbm, owner_ref), (column_hbm, column_ref), (time_hbm, time_ref),
         (residual_hbm, residual_ref), (kernel_hbm, kernel_ref)))]
    for load in loads:
        load.start()
    heights = sorted_ref.shape[1]
    filled = count // CLAT
    sorted_ref[:, filled:, :] = jnp.zeros((ROWS, heights - filled, CLAT), F32)
    earlier = (lax.broadcasted_iota(jnp.int32, (CHUNK, CHUNK), 0)
               < lax.broadcasted_iota(jnp.int32, (CHUNK, CHUNK), 1)).astype(F32).astype(BF16)
    names = lax.broadcasted_iota(jnp.int32, (owners, CHUNK), 0)
    ones = jnp.ones((CHUNK, CLAT), F32).astype(BF16)
    before = (lax.broadcasted_iota(jnp.int32, (owners, owners), 1)
              < lax.broadcasted_iota(jnp.int32, (owners, owners), 0)).astype(F32)

    loads[0].wait()
    for c in range(chunks):
        own_ref[c * owners:(c + 1) * owners] = (
            owner_ref[:, c * CHUNK:(c + 1) * CHUNK] == names).astype(F32).astype(BF16)
    inside = jnp.dot(own_ref[...], earlier, preferred_element_type=F32)
    counts = jnp.dot(own_ref[...], ones, preferred_element_type=F32)
    parts = [counts[c * owners:(c + 1) * owners] for c in range(chunks)]
    totals = functools.reduce(lambda x, y: x + y, parts)
    starts = jnp.dot(before, totals, precision=lax.Precision.HIGHEST, preferred_element_type=F32)
    carry = starts
    for c in range(chunks):
        own = own_ref[c * owners:(c + 1) * owners].astype(F32)
        wide = jnp.concatenate([carry] * (CHUNK // CLAT), axis=1)
        place_ref[:, c * CHUNK:(c + 1) * CHUNK] = jnp.sum(
            own * (inside[c * owners:(c + 1) * owners] + wide), axis=0,
            keepdims=True).astype(jnp.int32)
        carry = carry + parts[c]

    for load in loads[1:]:
        load.wait()
    high, low = split(kernel_ref[...] * residual_ref[...])
    seg_high = (time_ref[...] * CLON + column_ref[...] // CLAT).astype(F32)
    seg_low = (column_ref[...] % CLAT).astype(F32)
    spare = jnp.zeros((ROWS - levels - 1, count), F32)
    data_ref[...] = jnp.concatenate(
        [high.astype(F32), seg_high * float(CLAT), spare, low.astype(F32), seg_low, spare],
        axis=0).astype(BF16)

    groups = count // CHUNK
    span = min(count, 4 * CHUNK)
    inner = lax.broadcasted_iota(jnp.int32, (CHUNK, span), 0).astype(F32).astype(BF16)
    none = jnp.zeros((2 * ROWS, span), BF16)
    total = None
    for c in range(count // span):
        here = slice(c * span, (c + 1) * span)
        place = place_ref[:, here]
        outer = jnp.broadcast_to((place // CHUNK).astype(F32), (2 * ROWS, span)).astype(BF16)
        offset = jnp.broadcast_to((place % CHUNK).astype(F32), (CHUNK, span)).astype(BF16)
        data = data_ref[:, here]
        for g in range(groups):
            left_ref[g * 2 * ROWS:(g + 1) * 2 * ROWS] = jnp.where(
                outer == jnp.asarray(g, BF16), data, none)
        chosen = jnp.where(offset == inner, jnp.ones((), BF16), jnp.zeros((), BF16))
        got = lax.dot_general(left_ref[...], chosen, NT, preferred_element_type=F32)
        total = got if total is None else total + got
    for g in range(groups):
        both = total[2 * ROWS * g:2 * ROWS * g + ROWS] + total[2 * ROWS * g + ROWS:2 * ROWS * (g + 1)]
        for p in range(CHUNK // CLAT):
            sorted_ref[:, g * (CHUNK // CLAT) + p, :] = both[:, p * CLAT:(p + 1) * CLAT]

    shape = (levels + 1, slot_rows, CLAT)
    lane = lax.broadcasted_iota(jnp.int32, shape, 2)
    slot = (lax.broadcasted_iota(jnp.int32, (1, slot_rows, CLAT), 1) * CLAT
            + lax.broadcasted_iota(jnp.int32, (1, slot_rows, CLAT), 2))
    first = [jnp.max(starts[o:o + 1]).astype(jnp.int32) for o in range(owners)] + [count]
    for o in range(owners):
        row, shift = first[o] // CLAT, lax.rem(first[o], CLAT)
        back = lax.rem(CLAT - shift, CLAT)
        one = pltpu.roll(sorted_ref[0:levels + 1, pl.ds(row, slot_rows), :], back, 2)
        two = pltpu.roll(sorted_ref[0:levels + 1, pl.ds(row + 1, slot_rows), :], back, 2)
        run = jnp.where(lane < CLAT - shift, one, two)
        out_ref[o, 0:levels] = run[0:levels]
        out_ref[o, levels:] = jnp.where(slot < first[o + 1] - first[o], run[levels:], -1.0)


def pack(kernel, residual, owner_block, column, time_step, owners, capacity):
    levels, count = kernel.shape
    slot_rows = capacity // CLAT
    heights = -(-(count // CLAT + slot_rows + 1) // 8) * 8
    row = pltpu.VMEM((1, count), jnp.int32)
    chunks = count // CHUNK
    return pl.pallas_call(
        functools.partial(pack_kernel, owners),
        out_shape=jax.ShapeDtypeStruct((owners, levels + 1, slot_rows, CLAT), F32),
        in_specs=[pl.BlockSpec(memory_space=pltpu.HBM)] * 5,
        out_specs=pl.BlockSpec(memory_space=pltpu.VMEM),
        scratch_shapes=[
            pltpu.VMEM(kernel.shape, F32),
            pltpu.VMEM((1, count), F32),
            row, row, row,
            pltpu.VMEM((chunks * owners, CHUNK), BF16),
            pltpu.VMEM((2 * ROWS, count), BF16),
            row,
            pltpu.VMEM((2 * ROWS * chunks, min(count, 4 * CHUNK)), BF16),
            pltpu.VMEM((ROWS, heights, CLAT), F32),
            pltpu.SemaphoreType.DMA((5,)),
        ],
        compiler_params=pltpu.CompilerParams(vmem_limit_bytes=VMEM_LIMIT),
    )(*(pltpu.with_memory_space_constraint(x, pltpu.HBM) for x in (
        kernel, residual.reshape(1, count), owner_block.reshape(1, count),
        column.reshape(1, count), time_step.reshape(1, count))))


def bin_kernel(levels, lons, lats, slots_ref, out_ref, got_ref, total_ref, left_ref, chosen_ref, send_sem, recv_sem):
    owners, _, slot_rows, _ = slots_ref.shape
    lon, lat = lax.axis_index("lon"), lax.axis_index("lat")
    mesh_id = pl.DeviceIdType.MESH

    def peer(d):
        return lax.rem(lon + d // lats, lons), lax.rem(lat + lax.rem(d, lats), lats)

    def slot_copy(d):
        to_lon, to_lat = peer(d)
        return pltpu.make_async_remote_copy(
            src_ref=slots_ref.at[to_lon * lats + to_lat], dst_ref=got_ref.at[d],
            send_sem=send_sem.at[d], recv_sem=recv_sem.at[d],
            device_id={"lon": to_lon, "lat": to_lat}, device_id_type=mesh_id)

    barrier = pltpu.get_barrier_semaphore()

    def greet(d, _):
        to_lon, to_lat = peer(d)
        pl.semaphore_signal(barrier, inc=1, device_id={"lon": to_lon, "lat": to_lat},
                            device_id_type=mesh_id)
        return 0

    lax.fori_loop(1, owners, greet, 0)
    pl.semaphore_wait(barrier, owners - 1)

    def turn(i):
        return jnp.where(lax.rem(i, 2) == 1, (i + 1) // 2, lax.rem(owners - i // 2, owners))

    def begin(i, _):
        slot_copy(turn(i)).start()
        return 0

    lax.fori_loop(1, owners, begin, 0)
    total_ref[...] = jnp.zeros_like(total_ref)
    got_ref[0] = slots_ref[lon * lats + lat]

    def collect(i, _):
        d = turn(i)

        @pl.when(i > 0)
        def _():
            slot_copy(d).wait_recv()

        rows = jnp.concatenate([got_ref[d, :, i, :] for i in range(slot_rows)], axis=1)
        width = rows.shape[1]
        segment = rows[levels:levels + 1].astype(jnp.int32)
        values = rows[0:levels]
        high = values.astype(BF16).astype(F32)
        spare = jnp.zeros((ROWS - levels, width), F32)
        data = jnp.concatenate([high, spare, values - high, spare], axis=0).astype(BF16)
        step = jnp.broadcast_to((segment >> 10).astype(F32), data.shape).astype(BF16)
        for j in range(STEPS):
            left_ref[j * 2 * ROWS:(j + 1) * 2 * ROWS] = jnp.where(
                step == jnp.asarray(j, BF16), data, jnp.zeros(data.shape, BF16))
        lane = lax.broadcasted_iota(jnp.int32, (CLAT, width), 0).astype(F32).astype(BF16)
        for i in range(CLON):
            key = jnp.where(((segment >> 7) & (CLON - 1)) == i, segment & (CLAT - 1), -1).astype(F32)
            key = jnp.broadcast_to(key, (CLAT, width)).astype(BF16)
            chosen_ref[i * CLAT:(i + 1) * CLAT] = jnp.where(
                key == lane, jnp.ones((), BF16), jnp.zeros((), BF16))
        total_ref[...] += lax.dot_general(
            left_ref[...], chosen_ref[...], NT, preferred_element_type=F32)
        return 0

    lax.fori_loop(0, owners, collect, 0)
    for j in range(STEPS):
        top = j * 2 * ROWS
        part = total_ref[top:top + levels] + total_ref[top + ROWS:top + ROWS + levels]
        for i in range(CLON):
            out_ref[j, :, i, :] = part[:, i * CLAT:(i + 1) * CLAT]

    def finish(d, _):
        slot_copy(d).wait_send()
        return 0

    lax.fori_loop(1, owners, finish, 0)


def bin_soundings(slots, levels):
    lons, lats = lax.axis_size("lon"), lax.axis_size("lat")
    vmem = pl.BlockSpec(memory_space=pltpu.VMEM)
    return pl.pallas_call(
        functools.partial(bin_kernel, levels, lons, lats),
        out_shape=jax.ShapeDtypeStruct((STEPS, levels, CLON, CLAT), F32),
        in_specs=[vmem],
        out_specs=vmem,
        scratch_shapes=[
            pltpu.VMEM(slots.shape, F32),
            pltpu.VMEM((2 * STEPS * ROWS, CELLS), F32),
            pltpu.VMEM((2 * STEPS * ROWS, slots.shape[2] * CLAT), BF16),
            pltpu.VMEM((CELLS, slots.shape[2] * CLAT), BF16),
            pltpu.SemaphoreType.DMA((lons * lats,)),
            pltpu.SemaphoreType.DMA((lons * lats,)),
        ],
        compiler_params=pltpu.CompilerParams(
            collective_id=1, has_side_effects=True, vmem_limit_bytes=VMEM_LIMIT),
    )(slots)


def steps_kernel(orbits, lons, lats, weights, bins_ref, horizontal_ref, vertical_ref,
                 adjoint_ref, flux_ref, other_ref, forced_ref, mixed_ref, diagonal_ref, weight_ref,
                 first_ref, second_ref, halo_ref, pack_ref, lon_out, lon_in, lat_out, lat_in,
                 diag_out, diag_in, orbit_send, orbit_recv, lon_send, lon_recv, lat_send, lat_recv,
                 diag_send, diag_recv):
    levels = adjoint_ref.shape[0]
    lon, lat, orbit = lax.axis_index("lon"), lax.axis_index("lat"), lax.axis_index("orbit")
    east, west = lax.rem(lon + 1, lons), lax.rem(lon + lons - 1, lons)
    partner = 1 - orbit
    mesh_id = pl.DeviceIdType.MESH
    pairs = STEPS // 2
    last = CLON - 1
    below, above = lat < lats - 1, lat > 0
    barrier = pltpu.get_barrier_semaphore()

    def greet(device):
        pl.semaphore_signal(barrier, inc=1, device_id=device, device_id_type=mesh_id)

    greet({"lon": east})
    greet({"lon": west})
    greet({"orbit": partner})

    @pl.when(below)
    def _():
        greet({"lat": lat + 1})
        greet({"lon": east, "lat": lat + 1})
        greet({"lon": west, "lat": lat + 1})

    @pl.when(above)
    def _():
        greet({"lat": lat - 1})
        greet({"lon": east, "lat": lat - 1})
        greet({"lon": west, "lat": lat - 1})

    pl.semaphore_wait(barrier, 3 + jnp.where(above, 3, 0) + jnp.where(below, 3, 0))

    def orbit_copy(j):
        return pltpu.make_async_remote_copy(
            src_ref=bins_ref.at[j], dst_ref=other_ref.at[j],
            send_sem=orbit_send.at[j], recv_sem=orbit_recv.at[j],
            device_id={"orbit": partner}, device_id_type=mesh_id)

    def lon_copy(p, side):
        return pltpu.make_async_remote_copy(
            src_ref=lon_out.at[side, p], dst_ref=lon_in.at[side, p],
            send_sem=lon_send.at[side, p], recv_sem=lon_recv.at[side, p],
            device_id={"lon": (east, west)[side]}, device_id_type=mesh_id)

    def lat_copy(p, side):
        return pltpu.make_async_remote_copy(
            src_ref=lat_out.at[side, p], dst_ref=lat_in.at[side, p],
            send_sem=lat_send.at[side, p], recv_sem=lat_recv.at[side, p],
            device_id={"lat": (lat + 1, lat - 1)[side]}, device_id_type=mesh_id)

    def diag_copy(p, side, turn):
        return pltpu.make_async_remote_copy(
            src_ref=diag_out.at[side, p], dst_ref=diag_in.at[side, turn, p],
            send_sem=diag_send.at[side, turn, p], recv_sem=diag_recv.at[side, turn, p],
            device_id={"lon": (east, west)[turn], "lat": (lat + 1, lat - 1)[side]},
            device_id_type=mesh_id)

    towards = (below, above)
    comes = (above, below)

    def begin(t, _):
        orbit_copy(STEPS - 1 - t).start()
        return 0

    lax.fori_loop(0, STEPS, begin, 0)

    for side in range(2):
        @pl.when(jnp.logical_not(comes[side]))
        def _():
            lat_in[side] = jnp.zeros(lat_in.shape[1:], F32)
            diag_in[side] = jnp.zeros(diag_in.shape[1:], F32)

    part = (8, CLON, CLAT)
    lane = lax.broadcasted_iota(jnp.int32, part, 2)
    sub = lax.broadcasted_iota(jnp.int32, part, 1)
    level = lax.broadcasted_iota(jnp.int32, part, 0)
    chunks = range(0, levels, 8)
    ends = (CLAT - 1, 0)

    def collect(total, values, side, first):
        column = jnp.broadcast_to(values[:, :, ends[side]:ends[side] + 1], part)
        mine = jnp.sum(jnp.where(lane == first + level, column, 0.0), axis=0)
        return mine if total is None else total + mine

    none = jnp.zeros((1, CLON, CLAT), F32)
    packs = [[None] * 3, [None] * 3]
    for a in chunks:
        here = slice(a, a + 8)
        h = [horizontal_ref[d, here] for d in range(4)]
        v = (jnp.concatenate([vertical_ref[a:levels - 1], none], axis=0) if a + 8 == levels
             else vertical_ref[here])
        mingled = jnp.where(sub == last, h[0], h[1])
        for side in range(2):
            for i, values in enumerate((v, h[2 + side], mingled)):
                packs[side][i] = collect(packs[side][i], values, side, a)
        diagonal_ref[here] = 1.0 - h[0] - h[1] - h[2] - h[3]
        weight_ref[0, here] = jnp.where(sub == 0, 0.0, pltpu.roll(h[0], 1, 1))
        weight_ref[1, here] = jnp.where(sub == last, 0.0, pltpu.roll(h[1], last, 1))
        weight_ref[2, here] = jnp.where(lane == 0, 0.0, pltpu.roll(h[2], 1, 2))
        weight_ref[3, here] = jnp.where(lane == CLAT - 1, 0.0, pltpu.roll(h[3], CLAT - 1, 2))
    for side in range(2):
        edge = (last, 0)[side]
        lon_out[side, pairs, 0, 0:levels - 1] = vertical_ref[:, edge, :]
        lon_out[side, pairs, 0, levels - 1:] = jnp.zeros((1, CLAT), F32)
        lon_out[side, pairs, 1] = horizontal_ref[side, :, edge, :]
        lat_out[side, pairs, 0] = packs[side][0]
        lat_out[side, pairs, 1] = packs[side][1]
        pack_ref[side, 0] = packs[side][1]
        pack_ref[side, 1] = packs[side][2]
        lon_copy(pairs, side).start()

        @pl.when(towards[side])
        def _():
            lat_copy(pairs, side).start()

    def force(j, target_ref):
        bins = bins_ref[j] + other_ref[j]
        for a in chunks:
            forcing = []
            for l in range(a, a + 8):
                parts = [bins[k:k + 1] * float(weights[l, k]) for k in np.nonzero(weights[l])[0]]
                forcing.append(functools.reduce(lambda x, y: x + y, parts))
            target_ref[a:a + 8] = jnp.concatenate(forcing, axis=0)

    orbit_copy(STEPS - 1).wait_recv()
    force(STEPS - 1, forced_ref)
    orbit_copy(STEPS - 2).wait_recv()
    force(STEPS - 2, second_ref)
    flux_ref[...] = jnp.zeros_like(flux_ref)
    halo_ref[...] = jnp.zeros_like(halo_ref)

    def mix(packed):
        for a in chunks:
            low, high = max(a - 1, 0), min(a + 9, levels)
            forced = forced_ref[low:high]
            up = vertical_ref[low:high - 1] * (forced[1:] - forced[:-1])
            if a == 0:
                up = jnp.concatenate([none, up], axis=0)
            if a + 8 == levels:
                up = jnp.concatenate([up, none], axis=0)
            mixed = forced_ref[a:a + 8] + up[1:] - up[:-1]
            mixed_ref[a:a + 8] = mixed
            if packed is not None:
                for side in range(2):
                    packed[side] = collect(packed[side], mixed, side, a)

    def stencil(a):
        here = slice(a, a + 8)
        mixed = mixed_ref[here]
        return (diagonal_ref[here] * mixed
                + weight_ref[0, here] * pltpu.roll(mixed, 1, 1)
                + weight_ref[1, here] * pltpu.roll(mixed, last, 1)
                + weight_ref[2, here] * pltpu.roll(mixed, 1, 2)
                + weight_ref[3, here] * pltpu.roll(mixed, CLAT - 1, 2))

    def near(rows, a):
        north = jnp.stack([pltpu.roll(rows[0], -l % CLAT, 1) for l in range(a, a + 8)])
        south = jnp.stack([pltpu.roll(rows[1], CLAT - 1 - l, 1) for l in range(a, a + 8)])
        return jnp.where(lane == 0, north, jnp.where(lane == CLAT - 1, south, 0.0))

    wide = (levels, CLAT)
    wide_lane = lax.broadcasted_iota(jnp.int32, wide, 1)
    wide_level = lax.broadcasted_iota(jnp.int32, wide, 0)
    flat_sub = lax.broadcasted_iota(jnp.int32, (CLON, CLAT), 0)
    blank = jnp.zeros((1, CLAT), F32)

    def upright(row):
        return jnp.sum(jnp.where(wide_lane == wide_level, jnp.broadcast_to(row, wide), 0.0),
                       axis=1, keepdims=True)

    def advance(p, _):
        packed = [None, None]
        mix(packed)
        shed = []
        for side in range(2):
            edge, inner = ((last, last - 1), (0, 1))[side]
            mixed = mixed_ref[:, edge, :]
            out = horizontal_ref[side, :, edge, :] * mixed
            lon_out[side, p, 0] = out
            lon_out[side, p, 1] = (
                diagonal_ref[:, edge, :] * mixed
                + weight_ref[side, :, edge, :] * mixed_ref[:, inner, :]
                + weight_ref[2, :, edge, :] * pltpu.roll(mixed, 1, 1)
                + weight_ref[3, :, edge, :] * pltpu.roll(mixed, CLAT - 1, 1)
                + second_ref[:, edge, :])
            lon_copy(p, side).start()
        for side in range(2):
            out = pack_ref[side, 0] * packed[side]
            shed.append(out)
            lat_out[side, p, 0] = out
            diag_out[side, p, 0] = out
            diag_out[side, p, 1] = pack_ref[side, 1] * packed[side]

            @pl.when(towards[side])
            def _():
                diag_copy(p, side, 0).start()
                diag_copy(p, side, 1).start()

        partial = [None, None]
        for a in chunks:
            here = slice(a, a + 8)
            local = stencil(a)
            if a == 0:
                flux_ref[...] += local[0]
            local = local + second_ref[here]
            forced_ref[here] = local
            for side in range(2):
                partial[side] = collect(partial[side], local, side, a)
        for side in range(2):
            lat_out[side, p, 1] = partial[side]

            @pl.when(towards[side])
            def _():
                lat_copy(p, side).start()

        @pl.when(p < pairs - 1)
        def _():
            j = jnp.maximum(STEPS - 3 - 2 * p, 1)
            orbit_copy(j).wait_recv()
            force(j, first_ref)
            orbit_copy(j - 1).wait_recv()
            force(j - 1, second_ref)

        @pl.when(p == 0)
        def _():
            for side in range(2):
                lon_copy(pairs, side).wait_recv()

                @pl.when(comes[side])
                def _():
                    lat_copy(pairs, side).wait_recv()

        for side in range(2):
            @pl.when(comes[side])
            def _():
                lat_copy(p, side).wait_recv()
                diag_copy(p, side, 0).wait_recv()
                diag_copy(p, side, 1).wait_recv()

        for side in range(2):
            lon_copy(p, side).wait_recv()
            edge = (0, last)[side]
            halo_ref[0, :, edge, :] = lon_in[side, p, 0]

            far = (last, 0)[side]
            corner = [upright(diag_in[i, side, p, 0, far:far + 1, :]) for i in range(2)]
            beside = (lon_in[side, p, 1] + lon_out[1 - side, p, 0]
                      + jnp.where(wide_lane == 0, corner[0], 0.0)
                      + jnp.where(wide_lane == CLAT - 1, corner[1], 0.0))
            up = lon_in[side, pairs, 0, 0:levels - 1] * (beside[1:] - beside[:-1])
            mixed = (beside + jnp.concatenate([up, blank], axis=0)
                     - jnp.concatenate([blank, up], axis=0))
            halo_ref[1, :, edge, :] = lon_in[side, pairs, 1] * mixed

        rows, later = [], []
        for side in range(2):
            rows.append(lat_in[side, p, 0])
            beside = (lat_in[side, p, 1] + shed[1 - side]
                      + jnp.where(flat_sub == 0, pltpu.roll(diag_in[side, 0, p, 1], 1, 0), 0.0)
                      + jnp.where(flat_sub == last, pltpu.roll(diag_in[side, 1, p, 1], last, 0), 0.0))
            up = lat_in[side, pairs, 0] * (pltpu.roll(beside, CLAT - 1, 1) - beside)
            mixed = beside + up - pltpu.roll(up, 1, 1)
            later.append(lat_in[side, pairs, 1] * mixed)

        for a in chunks:
            here = slice(a, a + 8)
            more = halo_ref[0, here] + near(rows, a)
            if a == 0:
                flux_ref[...] += more[0]
            forced_ref[here] += more
        mix(None)
        for a in chunks:
            here = slice(a, a + 8)
            result = stencil(a) + (halo_ref[1, here] + near(later, a))
            if a == 0:
                flux_ref[...] += result[0]
            adjoint_ref[here] = result
            forced_ref[here] = result + first_ref[here]
        return 0

    first_ref[...] = jnp.zeros_like(first_ref)
    lax.fori_loop(0, pairs, advance, 0)

    def finish(p, _):
        for side in range(2):
            lon_copy(p, side).wait_send()

            @pl.when(towards[side])
            def _():
                lat_copy(p, side).wait_send()

            @pl.when(towards[side] & (p < pairs))
            def _():
                diag_copy(p, side, 0).wait_send()
                diag_copy(p, side, 1).wait_send()
        return 0

    lax.fori_loop(0, pairs + 1, finish, 0)

    def done(t, _):
        orbit_copy(t).wait_send()
        return 0

    lax.fori_loop(0, STEPS, done, 0)


def transport(bins, horizontal, vertical):
    levels = horizontal.shape[1]
    kernel_levels = bins.shape[1]
    orbits, lons, lats = (lax.axis_size(name) for name in ("orbit", "lon", "lat"))
    vmem = pl.BlockSpec(memory_space=pltpu.VMEM)
    block = (levels, CLON, CLAT)
    turns = STEPS // 2 + 1
    flat = (CLON, CLAT)
    return pl.pallas_call(
        functools.partial(steps_kernel, orbits, lons, lats, level_weights(levels, kernel_levels)),
        out_shape=(jax.ShapeDtypeStruct(block, F32), jax.ShapeDtypeStruct((CLON, CLAT), F32)),
        in_specs=[vmem] * 3,
        out_specs=(vmem, vmem),
        scratch_shapes=[
            pltpu.VMEM(bins.shape, F32),
            pltpu.VMEM(block, F32),
            pltpu.VMEM(block, F32),
            pltpu.VMEM(block, F32),
            pltpu.VMEM((4,) + block, F32),
            pltpu.VMEM(block, F32),
            pltpu.VMEM(block, F32),
            pltpu.VMEM((2,) + block, F32),
            pltpu.VMEM((2, 2) + flat, F32),
            pltpu.VMEM((2, turns, 2, levels, CLAT), F32),
            pltpu.VMEM((2, turns, 2, levels, CLAT), F32),
            pltpu.VMEM((2, turns, 2) + flat, F32),
            pltpu.VMEM((2, turns, 2) + flat, F32),
            pltpu.VMEM((2, turns, 2) + flat, F32),
            pltpu.VMEM((2, 2, turns, 2) + flat, F32),
            pltpu.SemaphoreType.DMA((STEPS,)),
            pltpu.SemaphoreType.DMA((STEPS,)),
            pltpu.SemaphoreType.DMA((2, turns)),
            pltpu.SemaphoreType.DMA((2, turns)),
            pltpu.SemaphoreType.DMA((2, turns)),
            pltpu.SemaphoreType.DMA((2, turns)),
            pltpu.SemaphoreType.DMA((2, 2, turns)),
            pltpu.SemaphoreType.DMA((2, 2, turns)),
        ],
        compiler_params=pltpu.CompilerParams(
            collective_id=0, has_side_effects=True, vmem_limit_bytes=VMEM_LIMIT),
    )(bins, horizontal, vertical)


def per_device(kernel, residual, owner_block, column, time_step, horizontal, vertical):
    owners = lax.axis_size("lon") * lax.axis_size("lat")
    capacity = 4 * kernel.shape[1] // owners
    slots = pack(kernel, residual, owner_block, column, time_step, owners, capacity)
    return transport(bin_soundings(slots, kernel.shape[0]), horizontal, vertical)


def solution(mesh):
    placed = (
        P(None, ("orbit", "lon", "lat")),
        P(("orbit", "lon", "lat")),
        P(("orbit", "lon", "lat"), None),
        P(("orbit", "lon", "lat")),
        P(("orbit", "lon", "lat")),
        P(None, None, "lon", "lat"),
        P(None, "lon", "lat"),
    )
    return jax.shard_map(
        per_device,
        mesh=mesh,
        in_specs=placed,
        out_specs=(P(None, "lon", "lat"), P("lon", "lat")),
        check_vma=False,
    )
```

```python
import functools

import jax
import jax.numpy as jnp
import numpy as np
from jax import lax
from jax.experimental import pallas as pl
from jax.experimental.pallas import tpu as pltpu
from jax.sharding import PartitionSpec as P

STEPS = 8
CLON = 8
CLAT = 128
CELLS = CLON * CLAT
ROWS = 24
CHUNK = 256
F32 = jnp.float32
BF16 = jnp.bfloat16
VMEM_LIMIT = 48 * 1024 * 1024
NT = (((1,), (1,)), ((), ()))


def level_weights(levels, kernel_levels):
    one = np.float32
    heights = np.arange(levels, dtype=np.float32)
    centre = np.clip((heights + one(0.5)) * one(kernel_levels) / one(levels) - one(0.5),
                     one(0), one(kernel_levels - 1))
    knots = np.arange(kernel_levels, dtype=np.float32)
    return np.maximum(one(0), one(1) - np.abs(centre[:, None] - knots[None, :]))


def split(values):
    high = values.astype(BF16)
    return high, (values - high.astype(F32)).astype(BF16)


def pack_kernel(owners, kernel_hbm, residual_hbm, owner_hbm, column_hbm, time_hbm, out_ref,
                kernel_ref, residual_ref, owner_ref, column_ref, time_ref, own_ref, data_ref,
                place_ref, left_ref, sorted_ref, sem):
    levels, count = kernel_hbm.shape
    slot_rows = out_ref.shape[2]
    chunks = count // CHUNK
    loads = [pltpu.make_async_copy(source, target, sem.at[i]) for i, (source, target) in enumerate(
        ((owner_hbm, owner_ref), (column_hbm, column_ref), (time_hbm, time_ref),
         (residual_hbm, residual_ref), (kernel_hbm, kernel_ref)))]
    for load in loads:
        load.start()
    heights = sorted_ref.shape[1]
    filled = count // CLAT
    sorted_ref[:, filled:, :] = jnp.zeros((ROWS, heights - filled, CLAT), F32)
    earlier = (lax.broadcasted_iota(jnp.int32, (CHUNK, CHUNK), 0)
               < lax.broadcasted_iota(jnp.int32, (CHUNK, CHUNK), 1)).astype(F32).astype(BF16)
    names = lax.broadcasted_iota(jnp.int32, (owners, CHUNK), 0)
    ones = jnp.ones((CHUNK, CLAT), F32).astype(BF16)
    before = (lax.broadcasted_iota(jnp.int32, (owners, owners), 1)
              < lax.broadcasted_iota(jnp.int32, (owners, owners), 0)).astype(F32)

    loads[0].wait()
    for c in range(chunks):
        own_ref[c * owners:(c + 1) * owners] = (
            owner_ref[:, c * CHUNK:(c + 1) * CHUNK] == names).astype(F32).astype(BF16)
    inside = jnp.dot(own_ref[...], earlier, preferred_element_type=F32)
    counts = jnp.dot(own_ref[...], ones, preferred_element_type=F32)
    parts = [counts[c * owners:(c + 1) * owners] for c in range(chunks)]
    totals = functools.reduce(lambda x, y: x + y, parts)
    starts = jnp.dot(before, totals, precision=lax.Precision.HIGHEST, preferred_element_type=F32)
    carry = starts
    for c in range(chunks):
        own = own_ref[c * owners:(c + 1) * owners].astype(F32)
        wide = jnp.concatenate([carry] * (CHUNK // CLAT), axis=1)
        place_ref[:, c * CHUNK:(c + 1) * CHUNK] = jnp.sum(
            own * (inside[c * owners:(c + 1) * owners] + wide), axis=0,
            keepdims=True).astype(jnp.int32)
        carry = carry + parts[c]

    for load in loads[1:]:
        load.wait()
    high, low = split(kernel_ref[...] * residual_ref[...])
    seg_high = (time_ref[...] * CLON + column_ref[...] // CLAT).astype(F32)
    seg_low = (column_ref[...] % CLAT).astype(F32)
    spare = jnp.zeros((ROWS - levels - 1, count), F32)
    data_ref[...] = jnp.concatenate(
        [high.astype(F32), seg_high * float(CLAT), spare, low.astype(F32), seg_low, spare],
        axis=0).astype(BF16)

    groups = count // CHUNK
    span = min(count, 4 * CHUNK)
    inner = lax.broadcasted_iota(jnp.int32, (CHUNK, span), 0).astype(F32).astype(BF16)
    none = jnp.zeros((2 * ROWS, span), BF16)
    total = None
    for c in range(count // span):
        here = slice(c * span, (c + 1) * span)
        place = place_ref[:, here]
        outer = jnp.broadcast_to((place // CHUNK).astype(F32), (2 * ROWS, span)).astype(BF16)
        offset = jnp.broadcast_to((place % CHUNK).astype(F32), (CHUNK, span)).astype(BF16)
        data = data_ref[:, here]
        for g in range(groups):
            left_ref[g * 2 * ROWS:(g + 1) * 2 * ROWS] = jnp.where(
                outer == jnp.asarray(g, BF16), data, none)
        chosen = jnp.where(offset == inner, jnp.ones((), BF16), jnp.zeros((), BF16))
        got = lax.dot_general(left_ref[...], chosen, NT, preferred_element_type=F32)
        total = got if total is None else total + got
    for g in range(groups):
        both = total[2 * ROWS * g:2 * ROWS * g + ROWS] + total[2 * ROWS * g + ROWS:2 * ROWS * (g + 1)]
        for p in range(CHUNK // CLAT):
            sorted_ref[:, g * (CHUNK // CLAT) + p, :] = both[:, p * CLAT:(p + 1) * CLAT]

    shape = (levels + 1, slot_rows, CLAT)
    lane = lax.broadcasted_iota(jnp.int32, shape, 2)
    slot = (lax.broadcasted_iota(jnp.int32, (1, slot_rows, CLAT), 1) * CLAT
            + lax.broadcasted_iota(jnp.int32, (1, slot_rows, CLAT), 2))
    first = [jnp.max(starts[o:o + 1]).astype(jnp.int32) for o in range(owners)] + [count]
    for o in range(owners):
        row, shift = first[o] // CLAT, lax.rem(first[o], CLAT)
        back = lax.rem(CLAT - shift, CLAT)
        one = pltpu.roll(sorted_ref[0:levels + 1, pl.ds(row, slot_rows), :], back, 2)
        two = pltpu.roll(sorted_ref[0:levels + 1, pl.ds(row + 1, slot_rows), :], back, 2)
        run = jnp.where(lane < CLAT - shift, one, two)
        out_ref[o, 0:levels] = run[0:levels]
        out_ref[o, levels:] = jnp.where(slot < first[o + 1] - first[o], run[levels:], -1.0)


def pack(kernel, residual, owner_block, column, time_step, owners, capacity):
    levels, count = kernel.shape
    slot_rows = capacity // CLAT
    heights = -(-(count // CLAT + slot_rows + 1) // 8) * 8
    row = pltpu.VMEM((1, count), jnp.int32)
    chunks = count // CHUNK
    return pl.pallas_call(
        functools.partial(pack_kernel, owners),
        out_shape=jax.ShapeDtypeStruct((owners, levels + 1, slot_rows, CLAT), F32),
        in_specs=[pl.BlockSpec(memory_space=pltpu.HBM)] * 5,
        out_specs=pl.BlockSpec(memory_space=pltpu.VMEM),
        scratch_shapes=[
            pltpu.VMEM(kernel.shape, F32),
            pltpu.VMEM((1, count), F32),
            row, row, row,
            pltpu.VMEM((chunks * owners, CHUNK), BF16),
            pltpu.VMEM((2 * ROWS, count), BF16),
            row,
            pltpu.VMEM((2 * ROWS * chunks, min(count, 4 * CHUNK)), BF16),
            pltpu.VMEM((ROWS, heights, CLAT), F32),
            pltpu.SemaphoreType.DMA((5,)),
        ],
        compiler_params=pltpu.CompilerParams(vmem_limit_bytes=VMEM_LIMIT),
    )(*(pltpu.with_memory_space_constraint(x, pltpu.HBM) for x in (
        kernel, residual.reshape(1, count), owner_block.reshape(1, count),
        column.reshape(1, count), time_step.reshape(1, count))))


def bin_kernel(levels, lons, lats, slots_ref, out_ref, got_ref, total_ref, left_ref, chosen_ref, send_sem, recv_sem):
    owners, _, slot_rows, _ = slots_ref.shape
    lon, lat = lax.axis_index("lon"), lax.axis_index("lat")
    mesh_id = pl.DeviceIdType.MESH

    def peer(d):
        return lax.rem(lon + d // lats, lons), lax.rem(lat + lax.rem(d, lats), lats)

    def slot_copy(d):
        to_lon, to_lat = peer(d)
        return pltpu.make_async_remote_copy(
            src_ref=slots_ref.at[to_lon * lats + to_lat], dst_ref=got_ref.at[d],
            send_sem=send_sem.at[d], recv_sem=recv_sem.at[d],
            device_id={"lon": to_lon, "lat": to_lat}, device_id_type=mesh_id)

    barrier = pltpu.get_barrier_semaphore()

    def greet(d, _):
        to_lon, to_lat = peer(d)
        pl.semaphore_signal(barrier, inc=1, device_id={"lon": to_lon, "lat": to_lat},
                            device_id_type=mesh_id)
        return 0

    lax.fori_loop(1, owners, greet, 0)
    pl.semaphore_wait(barrier, owners - 1)

    middle = lons // 2

    def turn(i):
        ring = lax.rem(i + lons * lats - 1, owners) // lats
        offset = middle + (ring + 1) // 2 * jnp.where(lax.rem(ring, 2) == 1, -1, 1)
        other = offset * lats + lax.rem(i + lats - 1, lats)
        return jnp.where(i == 0, 0, jnp.where(i <= owners - lats, other, i - owners + lats))

    def begin(i, _):
        slot_copy(turn(i)).start()
        return 0

    lax.fori_loop(1, owners, begin, 0)
    total_ref[...] = jnp.zeros_like(total_ref)
    got_ref[0] = slots_ref[lon * lats + lat]

    def collect(i, _):
        d = turn(i)

        @pl.when(i > 0)
        def _():
            slot_copy(d).wait_recv()

        rows = jnp.concatenate([got_ref[d, :, i, :] for i in range(slot_rows)], axis=1)
        width = rows.shape[1]
        segment = rows[levels:levels + 1].astype(jnp.int32)
        values = rows[0:levels]
        high = values.astype(BF16).astype(F32)
        spare = jnp.zeros((ROWS - levels, width), F32)
        data = jnp.concatenate([high, spare, values - high, spare], axis=0).astype(BF16)
        step = jnp.broadcast_to((segment >> 10).astype(F32), data.shape).astype(BF16)
        for j in range(STEPS):
            left_ref[j * 2 * ROWS:(j + 1) * 2 * ROWS] = jnp.where(
                step == jnp.asarray(j, BF16), data, jnp.zeros(data.shape, BF16))
        lane = lax.broadcasted_iota(jnp.int32, (CLAT, width), 0).astype(F32).astype(BF16)
        for i in range(CLON):
            key = jnp.where(((segment >> 7) & (CLON - 1)) == i, segment & (CLAT - 1), -1).astype(F32)
            key = jnp.broadcast_to(key, (CLAT, width)).astype(BF16)
            chosen_ref[i * CLAT:(i + 1) * CLAT] = jnp.where(
                key == lane, jnp.ones((), BF16), jnp.zeros((), BF16))
        total_ref[...] += lax.dot_general(
            left_ref[...], chosen_ref[...], NT, preferred_element_type=F32)
        return 0

    lax.fori_loop(0, owners, collect, 0)
    for j in range(STEPS):
        top = j * 2 * ROWS
        part = total_ref[top:top + levels] + total_ref[top + ROWS:top + ROWS + levels]
        for i in range(CLON):
            out_ref[j, :, i, :] = part[:, i * CLAT:(i + 1) * CLAT]

    def finish(d, _):
        slot_copy(d).wait_send()
        return 0

    lax.fori_loop(1, owners, finish, 0)


def bin_soundings(slots, levels):
    lons, lats = lax.axis_size("lon"), lax.axis_size("lat")
    vmem = pl.BlockSpec(memory_space=pltpu.VMEM)
    return pl.pallas_call(
        functools.partial(bin_kernel, levels, lons, lats),
        out_shape=jax.ShapeDtypeStruct((STEPS, levels, CLON, CLAT), F32),
        in_specs=[vmem],
        out_specs=vmem,
        scratch_shapes=[
            pltpu.VMEM(slots.shape, F32),
            pltpu.VMEM((2 * STEPS * ROWS, CELLS), F32),
            pltpu.VMEM((2 * STEPS * ROWS, slots.shape[2] * CLAT), BF16),
            pltpu.VMEM((CELLS, slots.shape[2] * CLAT), BF16),
            pltpu.SemaphoreType.DMA((lons * lats,)),
            pltpu.SemaphoreType.DMA((lons * lats,)),
        ],
        compiler_params=pltpu.CompilerParams(
            collective_id=1, has_side_effects=True, vmem_limit_bytes=VMEM_LIMIT),
    )(slots)


def steps_kernel(orbits, lons, lats, weights, bins_ref, horizontal_ref, vertical_ref,
                 adjoint_ref, flux_ref, other_ref, forced_ref, mixed_ref, diagonal_ref, weight_ref,
                 first_ref, second_ref, halo_ref, pack_ref, lon_out, lon_in, lat_out, lat_in,
                 diag_out, diag_in, orbit_send, orbit_recv, lon_send, lon_recv, lat_send, lat_recv,
                 diag_send, diag_recv):
    levels = adjoint_ref.shape[0]
    lon, lat, orbit = lax.axis_index("lon"), lax.axis_index("lat"), lax.axis_index("orbit")
    east, west = lax.rem(lon + 1, lons), lax.rem(lon + lons - 1, lons)
    partner = 1 - orbit
    mesh_id = pl.DeviceIdType.MESH
    pairs = STEPS // 2
    last = CLON - 1
    below, above = lat < lats - 1, lat > 0
    barrier = pltpu.get_barrier_semaphore()

    def greet(device):
        pl.semaphore_signal(barrier, inc=1, device_id=device, device_id_type=mesh_id)

    greet({"lon": east})
    greet({"lon": west})
    greet({"orbit": partner})

    @pl.when(below)
    def _():
        greet({"lat": lat + 1})
        greet({"lon": east, "lat": lat + 1})
        greet({"lon": west, "lat": lat + 1})

    @pl.when(above)
    def _():
        greet({"lat": lat - 1})
        greet({"lon": east, "lat": lat - 1})
        greet({"lon": west, "lat": lat - 1})

    pl.semaphore_wait(barrier, 3 + jnp.where(above, 3, 0) + jnp.where(below, 3, 0))

    def orbit_copy(j):
        return pltpu.make_async_remote_copy(
            src_ref=bins_ref.at[j], dst_ref=other_ref.at[j],
            send_sem=orbit_send.at[j], recv_sem=orbit_recv.at[j],
            device_id={"orbit": partner}, device_id_type=mesh_id)

    def lon_copy(p, side):
        return pltpu.make_async_remote_copy(
            src_ref=lon_out.at[side, p], dst_ref=lon_in.at[side, p],
            send_sem=lon_send.at[side, p], recv_sem=lon_recv.at[side, p],
            device_id={"lon": (east, west)[side]}, device_id_type=mesh_id)

    def lat_copy(p, side):
        return pltpu.make_async_remote_copy(
            src_ref=lat_out.at[side, p], dst_ref=lat_in.at[side, p],
            send_sem=lat_send.at[side, p], recv_sem=lat_recv.at[side, p],
            device_id={"lat": (lat + 1, lat - 1)[side]}, device_id_type=mesh_id)

    def diag_copy(p, side, turn):
        return pltpu.make_async_remote_copy(
            src_ref=diag_out.at[side, p], dst_ref=diag_in.at[side, turn, p],
            send_sem=diag_send.at[side, turn, p], recv_sem=diag_recv.at[side, turn, p],
            device_id={"lon": (east, west)[turn], "lat": (lat + 1, lat - 1)[side]},
            device_id_type=mesh_id)

    towards = (below, above)
    comes = (above, below)

    def begin(t, _):
        orbit_copy(STEPS - 1 - t).start()
        return 0

    lax.fori_loop(0, STEPS, begin, 0)

    for side in range(2):
        @pl.when(jnp.logical_not(comes[side]))
        def _():
            lat_in[side] = jnp.zeros(lat_in.shape[1:], F32)
            diag_in[side] = jnp.zeros(diag_in.shape[1:], F32)

    part = (8, CLON, CLAT)
    lane = lax.broadcasted_iota(jnp.int32, part, 2)
    sub = lax.broadcasted_iota(jnp.int32, part, 1)
    level = lax.broadcasted_iota(jnp.int32, part, 0)
    chunks = range(0, levels, 8)
    flat = (CLON, CLAT)
    flat_lane = lax.broadcasted_iota(jnp.int32, flat, 1)
    flat_sub = lax.broadcasted_iota(jnp.int32, flat, 0)
    even = (flat_lane & 1) == 0

    def collect(total, values, first):
        for i in range(8):
            l = first + i
            pair = (flat_lane >= l) & (flat_lane <= l + 1)
            total[l % 2] = jnp.where(pair, pltpu.roll(values[i], l + 1, 1), total[l % 2])

    def gather():
        return [jnp.zeros(flat, F32), jnp.zeros(flat, F32)]

    def rows_of(total):
        return (jnp.where(even, total[0], total[1]),
                pltpu.roll(jnp.where(even, total[1], total[0]), CLAT - 1, 1))

    none = jnp.zeros((1, CLON, CLAT), F32)
    packs = [gather(), gather(), gather()]
    for a in chunks:
        here = slice(a, a + 8)
        h = [horizontal_ref[d, here] for d in range(4)]
        v = (jnp.concatenate([vertical_ref[a:levels - 1], none], axis=0) if a + 8 == levels
             else vertical_ref[here])
        mingled = jnp.where(sub == last, h[0], h[1])
        for i, values in enumerate((v, jnp.where(lane == 0, h[3], h[2]), mingled)):
            collect(packs[i], values, a)
        diagonal_ref[here] = 1.0 - h[0] - h[1] - h[2] - h[3]
        weight_ref[0, here] = jnp.where(sub == 0, 0.0, pltpu.roll(h[0], 1, 1))
        weight_ref[1, here] = jnp.where(sub == last, 0.0, pltpu.roll(h[1], last, 1))
        weight_ref[2, here] = jnp.where(lane == 0, 0.0, pltpu.roll(h[2], 1, 2))
        weight_ref[3, here] = jnp.where(lane == CLAT - 1, 0.0, pltpu.roll(h[3], CLAT - 1, 2))
    packs = [rows_of(total) for total in packs]
    for side in range(2):
        edge = (last, 0)[side]
        lon_out[side, pairs, 0, 0:levels - 1] = vertical_ref[:, edge, :]
        lon_out[side, pairs, 0, levels - 1:] = jnp.zeros((1, CLAT), F32)
        lon_out[side, pairs, 1] = horizontal_ref[side, :, edge, :]
        lat_out[side, pairs, 0] = packs[0][side]
        lat_out[side, pairs, 1] = packs[1][side]
        pack_ref[side, 0] = packs[1][side]
        pack_ref[side, 1] = packs[2][side]
        lon_copy(pairs, side).start()

        @pl.when(towards[side])
        def _():
            lat_copy(pairs, side).start()

    def force(j, target_ref):
        bins = bins_ref[j] + other_ref[j]
        for a in chunks:
            forcing = []
            for l in range(a, a + 8):
                parts = [bins[k:k + 1] * float(weights[l, k]) for k in np.nonzero(weights[l])[0]]
                forcing.append(functools.reduce(lambda x, y: x + y, parts))
            target_ref[a:a + 8] = jnp.concatenate(forcing, axis=0)

    orbit_copy(STEPS - 1).wait_recv()
    force(STEPS - 1, forced_ref)
    orbit_copy(STEPS - 2).wait_recv()
    force(STEPS - 2, second_ref)
    flux_ref[...] = jnp.zeros_like(flux_ref)
    halo_ref[...] = jnp.zeros_like(halo_ref)

    def mix(packed):
        for a in chunks:
            low, high = max(a - 1, 0), min(a + 9, levels)
            forced = forced_ref[low:high]
            up = vertical_ref[low:high - 1] * (forced[1:] - forced[:-1])
            if a == 0:
                up = jnp.concatenate([none, up], axis=0)
            if a + 8 == levels:
                up = jnp.concatenate([up, none], axis=0)
            mixed = forced_ref[a:a + 8] + up[1:] - up[:-1]
            mixed_ref[a:a + 8] = mixed
            if packed is not None:
                collect(packed, mixed, a)

    def stencil(a):
        here = slice(a, a + 8)
        mixed = mixed_ref[here]
        return (diagonal_ref[here] * mixed
                + weight_ref[0, here] * pltpu.roll(mixed, 1, 1)
                + weight_ref[1, here] * pltpu.roll(mixed, last, 1)
                + weight_ref[2, here] * pltpu.roll(mixed, 1, 2)
                + weight_ref[3, here] * pltpu.roll(mixed, CLAT - 1, 2))

    outer = (lane == 0) | (lane == CLAT - 1)

    def weave(rows):
        south = pltpu.roll(rows[1], CLAT - 1, 1)
        return jnp.where(even, rows[0], south), jnp.where(even, south, rows[0])

    def near(woven, a):
        both = jnp.stack([pltpu.roll(woven[l % 2], -l % CLAT, 1) for l in range(a, a + 8)])
        return jnp.where(outer, both, 0.0)

    wide = (levels, CLAT)
    wide_lane = lax.broadcasted_iota(jnp.int32, wide, 1)
    wide_level = lax.broadcasted_iota(jnp.int32, wide, 0)
    blank = jnp.zeros((1, CLAT), F32)

    def upright(row):
        return jnp.sum(jnp.where(wide_lane == wide_level, jnp.broadcast_to(row, wide), 0.0),
                       axis=1, keepdims=True)

    def advance(p, _):
        packed = gather()
        mix(packed)
        packed = rows_of(packed)
        shed = []
        for side in range(2):
            out = pack_ref[side, 0] * packed[side]
            shed.append(out)
            lat_out[side, p, 0] = out
            diag_out[side, p, 0] = out
            diag_out[side, p, 1] = pack_ref[side, 1] * packed[side]

            @pl.when(towards[side])
            def _():
                diag_copy(p, side, 0).start()
                diag_copy(p, side, 1).start()

        for side in range(2):
            edge, inner = ((last, last - 1), (0, 1))[side]
            mixed = mixed_ref[:, edge, :]
            lon_out[side, p, 0] = horizontal_ref[side, :, edge, :] * mixed
            lon_out[side, p, 1] = (
                diagonal_ref[:, edge, :] * mixed
                + weight_ref[side, :, edge, :] * mixed_ref[:, inner, :]
                + weight_ref[2, :, edge, :] * pltpu.roll(mixed, 1, 1)
                + weight_ref[3, :, edge, :] * pltpu.roll(mixed, CLAT - 1, 1)
                + second_ref[:, edge, :])

        @pl.when(lon == 0)
        def _():
            lon_copy(p, 1).start()
            lon_copy(p, 0).start()

        @pl.when(lon > 0)
        def _():
            lon_copy(p, 0).start()
            lon_copy(p, 1).start()

        partial = gather()
        for a in chunks:
            here = slice(a, a + 8)
            local = stencil(a)
            if a == 0:
                flux_ref[...] += local[0]
            local = local + second_ref[here]
            forced_ref[here] = local
            collect(partial, local, a)
        partial = rows_of(partial)
        for side in range(2):
            lat_out[side, p, 1] = partial[side]

            @pl.when(towards[side])
            def _():
                lat_copy(p, side).start()

        @pl.when(p < pairs - 1)
        def _():
            j = jnp.maximum(STEPS - 3 - 2 * p, 1)
            orbit_copy(j).wait_recv()
            force(j, first_ref)
            orbit_copy(j - 1).wait_recv()
            force(j - 1, second_ref)

        @pl.when(p == 0)
        def _():
            for side in range(2):
                lon_copy(pairs, side).wait_recv()

                @pl.when(comes[side])
                def _():
                    lat_copy(pairs, side).wait_recv()

        for side in range(2):
            @pl.when(comes[side])
            def _():
                lat_copy(p, side).wait_recv()
                diag_copy(p, side, 0).wait_recv()
                diag_copy(p, side, 1).wait_recv()

        for side in range(2):
            lon_copy(p, side).wait_recv()
            edge = (0, last)[side]
            halo_ref[0, :, edge, :] = lon_in[side, p, 0]

            far = (last, 0)[side]
            corner = [upright(diag_in[i, side, p, 0, far:far + 1, :]) for i in range(2)]
            beside = (lon_in[side, p, 1] + lon_out[1 - side, p, 0]
                      + jnp.where(wide_lane == 0, corner[0], 0.0)
                      + jnp.where(wide_lane == CLAT - 1, corner[1], 0.0))
            up = lon_in[side, pairs, 0, 0:levels - 1] * (beside[1:] - beside[:-1])
            mixed = (beside + jnp.concatenate([up, blank], axis=0)
                     - jnp.concatenate([blank, up], axis=0))
            halo_ref[1, :, edge, :] = lon_in[side, pairs, 1] * mixed

        rows, later = [], []
        for side in range(2):
            rows.append(lat_in[side, p, 0])
            beside = (lat_in[side, p, 1] + shed[1 - side]
                      + jnp.where(flat_sub == 0, pltpu.roll(diag_in[side, 0, p, 1], 1, 0), 0.0)
                      + jnp.where(flat_sub == last, pltpu.roll(diag_in[side, 1, p, 1], last, 0), 0.0))
            up = lat_in[side, pairs, 0] * (pltpu.roll(beside, CLAT - 1, 1) - beside)
            mixed = beside + up - pltpu.roll(up, 1, 1)
            later.append(lat_in[side, pairs, 1] * mixed)

        rows, later = weave(rows), weave(later)
        for a in chunks:
            here = slice(a, a + 8)
            more = halo_ref[0, here] + near(rows, a)
            if a == 0:
                flux_ref[...] += more[0]
            forced_ref[here] += more
        mix(None)
        for a in chunks:
            here = slice(a, a + 8)
            result = stencil(a) + (halo_ref[1, here] + near(later, a))
            if a == 0:
                flux_ref[...] += result[0]
            adjoint_ref[here] = result
            forced_ref[here] = result + first_ref[here]
        return 0

    first_ref[...] = jnp.zeros_like(first_ref)
    lax.fori_loop(0, pairs, advance, 0)

    def finish(p, _):
        for side in range(2):
            lon_copy(p, side).wait_send()

            @pl.when(towards[side])
            def _():
                lat_copy(p, side).wait_send()

            @pl.when(towards[side] & (p < pairs))
            def _():
                diag_copy(p, side, 0).wait_send()
                diag_copy(p, side, 1).wait_send()
        return 0

    lax.fori_loop(0, pairs + 1, finish, 0)

    def done(t, _):
        orbit_copy(t).wait_send()
        return 0

    lax.fori_loop(0, STEPS, done, 0)


def transport(bins, horizontal, vertical):
    levels = horizontal.shape[1]
    kernel_levels = bins.shape[1]
    orbits, lons, lats = (lax.axis_size(name) for name in ("orbit", "lon", "lat"))
    vmem = pl.BlockSpec(memory_space=pltpu.VMEM)
    block = (levels, CLON, CLAT)
    turns = STEPS // 2 + 1
    flat = (CLON, CLAT)
    return pl.pallas_call(
        functools.partial(steps_kernel, orbits, lons, lats, level_weights(levels, kernel_levels)),
        out_shape=(jax.ShapeDtypeStruct(block, F32), jax.ShapeDtypeStruct((CLON, CLAT), F32)),
        in_specs=[vmem] * 3,
        out_specs=(vmem, vmem),
        scratch_shapes=[
            pltpu.VMEM(bins.shape, F32),
            pltpu.VMEM(block, F32),
            pltpu.VMEM(block, F32),
            pltpu.VMEM(block, F32),
            pltpu.VMEM((4,) + block, F32),
            pltpu.VMEM(block, F32),
            pltpu.VMEM(block, F32),
            pltpu.VMEM((2,) + block, F32),
            pltpu.VMEM((2, 2) + flat, F32),
            pltpu.VMEM((2, turns, 2, levels, CLAT), F32),
            pltpu.VMEM((2, turns, 2, levels, CLAT), F32),
            pltpu.VMEM((2, turns, 2) + flat, F32),
            pltpu.VMEM((2, turns, 2) + flat, F32),
            pltpu.VMEM((2, turns, 2) + flat, F32),
            pltpu.VMEM((2, 2, turns, 2) + flat, F32),
            pltpu.SemaphoreType.DMA((STEPS,)),
            pltpu.SemaphoreType.DMA((STEPS,)),
            pltpu.SemaphoreType.DMA((2, turns)),
            pltpu.SemaphoreType.DMA((2, turns)),
            pltpu.SemaphoreType.DMA((2, turns)),
            pltpu.SemaphoreType.DMA((2, turns)),
            pltpu.SemaphoreType.DMA((2, 2, turns)),
            pltpu.SemaphoreType.DMA((2, 2, turns)),
        ],
        compiler_params=pltpu.CompilerParams(
            collective_id=0, has_side_effects=True, vmem_limit_bytes=VMEM_LIMIT),
    )(bins, horizontal, vertical)


def per_device(kernel, residual, owner_block, column, time_step, horizontal, vertical):
    owners = lax.axis_size("lon") * lax.axis_size("lat")
    capacity = 4 * kernel.shape[1] // owners
    slots = pack(kernel, residual, owner_block, column, time_step, owners, capacity)
    return transport(bin_soundings(slots, kernel.shape[0]), horizontal, vertical)


def solution(mesh):
    placed = (
        P(None, ("orbit", "lon", "lat")),
        P(("orbit", "lon", "lat")),
        P(("orbit", "lon", "lat"), None),
        P(("orbit", "lon", "lat")),
        P(("orbit", "lon", "lat")),
        P(None, None, "lon", "lat"),
        P(None, "lon", "lat"),
    )
    return jax.shard_map(
        per_device,
        mesh=mesh,
        in_specs=placed,
        out_specs=(P(None, "lon", "lat"), P("lon", "lat")),
        check_vma=False,
    )
```

```python
import functools

import jax
import jax.numpy as jnp
import numpy as np
from jax import lax
from jax.experimental import pallas as pl
from jax.experimental.pallas import tpu as pltpu
from jax.sharding import PartitionSpec as P

STEPS = 8
CLON = 8
CLAT = 128
CELLS = CLON * CLAT
ROWS = 24
CHUNK = 256
F32 = jnp.float32
BF16 = jnp.bfloat16
VMEM_LIMIT = 48 * 1024 * 1024
NT = (((1,), (1,)), ((), ()))


def level_weights(levels, kernel_levels):
    one = np.float32
    heights = np.arange(levels, dtype=np.float32)
    centre = np.clip((heights + one(0.5)) * one(kernel_levels) / one(levels) - one(0.5),
                     one(0), one(kernel_levels - 1))
    knots = np.arange(kernel_levels, dtype=np.float32)
    return np.maximum(one(0), one(1) - np.abs(centre[:, None] - knots[None, :]))


def split(values):
    high = values.astype(BF16)
    return high, (values - high.astype(F32)).astype(BF16)


def whole_kernel(orbits, lons, lats, weights, kernel_hbm, residual_hbm, owner_hbm, column_hbm, time_hbm,
                 horizontal_hbm, vertical_hbm, adjoint_ref, flux_ref,
                 kernel_ref, residual_ref, owner_ref, column_ref, time_ref, horizontal_ref, vertical_ref,
                 own_ref, data_ref, place_ref, left_ref, sorted_ref,
                 slots_ref, got_ref, total_ref, taken_ref, chosen_ref,
                 bins_ref, other_ref, forced_ref, mixed_ref, diagonal_ref, weight_ref,
                 first_ref, second_ref, halo_ref, pack_ref, lon_out, lon_in, lat_out, lat_in,
                 diag_out, diag_in, load_sem, slot_send, slot_recv, orbit_send, orbit_recv,
                 lon_send, lon_recv, lat_send, lat_recv, diag_send, diag_recv):
    klevels, count = kernel_hbm.shape
    owners, _, slot_rows, _ = slots_ref.shape
    chunks = count // CHUNK
    loads = [pltpu.make_async_copy(source, target, load_sem.at[i]) for i, (source, target) in enumerate(
        ((owner_hbm, owner_ref), (column_hbm, column_ref), (time_hbm, time_ref),
         (residual_hbm, residual_ref), (kernel_hbm, kernel_ref),
         (vertical_hbm, vertical_ref), (horizontal_hbm, horizontal_ref)))]
    for load in loads:
        load.start()
    heights = sorted_ref.shape[1]
    filled = count // CLAT
    sorted_ref[:, filled:, :] = jnp.zeros((ROWS, heights - filled, CLAT), F32)
    earlier = (lax.broadcasted_iota(jnp.int32, (CHUNK, CHUNK), 0)
               < lax.broadcasted_iota(jnp.int32, (CHUNK, CHUNK), 1)).astype(F32).astype(BF16)
    names = lax.broadcasted_iota(jnp.int32, (owners, CHUNK), 0)
    ones = jnp.ones((CHUNK, CLAT), F32).astype(BF16)
    before = (lax.broadcasted_iota(jnp.int32, (owners, owners), 1)
              < lax.broadcasted_iota(jnp.int32, (owners, owners), 0)).astype(F32)

    levels = adjoint_ref.shape[0]
    lon, lat, orbit = lax.axis_index("lon"), lax.axis_index("lat"), lax.axis_index("orbit")
    east, west = lax.rem(lon + 1, lons), lax.rem(lon + lons - 1, lons)
    partner = 1 - orbit
    mesh_id = pl.DeviceIdType.MESH
    pairs = STEPS // 2
    last = CLON - 1
    below, above = lat < lats - 1, lat > 0
    def peer(d):
        return lax.rem(lon + d // lats, lons), lax.rem(lat + lax.rem(d, lats), lats)

    def slot_copy(d):
        to_lon, to_lat = peer(d)
        return pltpu.make_async_remote_copy(
            src_ref=slots_ref.at[to_lon * lats + to_lat], dst_ref=got_ref.at[d],
            send_sem=slot_send.at[d], recv_sem=slot_recv.at[d],
            device_id={"lon": to_lon, "lat": to_lat}, device_id_type=mesh_id)

    barrier = pltpu.get_barrier_semaphore()
    pl.semaphore_signal(barrier, inc=1, device_id={"orbit": partner}, device_id_type=mesh_id)

    def greet(d, _):
        to_lon, to_lat = peer(d)
        pl.semaphore_signal(barrier, inc=1, device_id={"lon": to_lon, "lat": to_lat},
                            device_id_type=mesh_id)
        return 0

    lax.fori_loop(1, owners, greet, 0)

    def orbit_copy(j):
        return pltpu.make_async_remote_copy(
            src_ref=bins_ref.at[j], dst_ref=other_ref.at[j],
            send_sem=orbit_send.at[j], recv_sem=orbit_recv.at[j],
            device_id={"orbit": partner}, device_id_type=mesh_id)

    def lon_copy(p, side):
        return pltpu.make_async_remote_copy(
            src_ref=lon_out.at[side, p], dst_ref=lon_in.at[side, p],
            send_sem=lon_send.at[side, p], recv_sem=lon_recv.at[side, p],
            device_id={"lon": (east, west)[side]}, device_id_type=mesh_id)

    def lat_copy(p, side):
        return pltpu.make_async_remote_copy(
            src_ref=lat_out.at[side, p], dst_ref=lat_in.at[side, p],
            send_sem=lat_send.at[side, p], recv_sem=lat_recv.at[side, p],
            device_id={"lat": (lat + 1, lat - 1)[side]}, device_id_type=mesh_id)

    def diag_copy(p, side, turn):
        return pltpu.make_async_remote_copy(
            src_ref=diag_out.at[side, p], dst_ref=diag_in.at[side, turn, p],
            send_sem=diag_send.at[side, turn, p], recv_sem=diag_recv.at[side, turn, p],
            device_id={"lon": (east, west)[turn], "lat": (lat + 1, lat - 1)[side]},
            device_id_type=mesh_id)

    towards = (below, above)
    comes = (above, below)

    loads[0].wait()
    for c in range(chunks):
        own_ref[c * owners:(c + 1) * owners] = (
            owner_ref[:, c * CHUNK:(c + 1) * CHUNK] == names).astype(F32).astype(BF16)
    inside = jnp.dot(own_ref[...], earlier, preferred_element_type=F32)
    counts = jnp.dot(own_ref[...], ones, preferred_element_type=F32)
    parts = [counts[c * owners:(c + 1) * owners] for c in range(chunks)]
    totals = functools.reduce(lambda x, y: x + y, parts)
    starts = jnp.dot(before, totals, precision=lax.Precision.HIGHEST, preferred_element_type=F32)
    carry = starts
    for c in range(chunks):
        own = own_ref[c * owners:(c + 1) * owners].astype(F32)
        wide = jnp.concatenate([carry] * (CHUNK // CLAT), axis=1)
        place_ref[:, c * CHUNK:(c + 1) * CHUNK] = jnp.sum(
            own * (inside[c * owners:(c + 1) * owners] + wide), axis=0,
            keepdims=True).astype(jnp.int32)
        carry = carry + parts[c]


    pl.semaphore_wait(barrier, owners)
    loads[5].wait()
    loads[6].wait()
    for side in range(2):
        edge = (last, 0)[side]
        lon_out[side, pairs, 0, 0:levels - 1] = vertical_ref[:, edge, :]
        lon_out[side, pairs, 0, levels - 1:] = jnp.zeros((1, CLAT), F32)
        lon_out[side, pairs, 1] = horizontal_ref[side, :, edge, :]
        lon_copy(pairs, side).start()

    for load in loads[1:5]:
        load.wait()
    high, low = split(kernel_ref[...] * residual_ref[...])
    seg_high = (time_ref[...] * CLON + column_ref[...] // CLAT).astype(F32)
    seg_low = (column_ref[...] % CLAT).astype(F32)
    spare = jnp.zeros((ROWS - klevels - 1, count), F32)
    data_ref[...] = jnp.concatenate(
        [high.astype(F32), seg_high * float(CLAT), spare, low.astype(F32), seg_low, spare],
        axis=0).astype(BF16)

    groups = count // CHUNK
    span = min(count, 4 * CHUNK)
    inner = lax.broadcasted_iota(jnp.int32, (CHUNK, span), 0).astype(F32).astype(BF16)
    none = jnp.zeros((2 * ROWS, span), BF16)
    product = None
    for c in range(count // span):
        here = slice(c * span, (c + 1) * span)
        place = place_ref[:, here]
        outer = jnp.broadcast_to((place // CHUNK).astype(F32), (2 * ROWS, span)).astype(BF16)
        offset = jnp.broadcast_to((place % CHUNK).astype(F32), (CHUNK, span)).astype(BF16)
        data = data_ref[:, here]
        for g in range(groups):
            left_ref[g * 2 * ROWS:(g + 1) * 2 * ROWS] = jnp.where(
                outer == jnp.asarray(g, BF16), data, none)
        chosen = jnp.where(offset == inner, jnp.ones((), BF16), jnp.zeros((), BF16))
        got = lax.dot_general(left_ref[...], chosen, NT, preferred_element_type=F32)
        product = got if product is None else product + got
    for g in range(groups):
        both = product[2 * ROWS * g:2 * ROWS * g + ROWS] + product[2 * ROWS * g + ROWS:2 * ROWS * (g + 1)]
        for p in range(CHUNK // CLAT):
            sorted_ref[:, g * (CHUNK // CLAT) + p, :] = both[:, p * CLAT:(p + 1) * CLAT]

    shape = (klevels + 1, slot_rows, CLAT)
    slot_lane = lax.broadcasted_iota(jnp.int32, shape, 2)
    slot = (lax.broadcasted_iota(jnp.int32, (1, slot_rows, CLAT), 1) * CLAT
            + lax.broadcasted_iota(jnp.int32, (1, slot_rows, CLAT), 2))
    first = [jnp.clip(jnp.max(starts[o:o + 1]).astype(jnp.int32), 0, count)
             for o in range(owners)] + [count]
    for o in range(owners):
        row, shift = first[o] // CLAT, lax.rem(first[o], CLAT)
        back = lax.rem(CLAT - shift, CLAT)
        one = pltpu.roll(sorted_ref[0:klevels + 1, pl.ds(row, slot_rows), :], back, 2)
        two = pltpu.roll(sorted_ref[0:klevels + 1, pl.ds(row + 1, slot_rows), :], back, 2)
        run = jnp.where(slot_lane < CLAT - shift, one, two)
        slots_ref[o, 0:klevels] = run[0:klevels]
        slots_ref[o, klevels:] = jnp.where(slot < first[o + 1] - first[o], run[klevels:], -1.0)


    even_lon = lax.rem(lon, 2) == 0

    def send_turn(i):
        m = jnp.where(lax.rem(i, 2) == 1, i // 2, owners // 2 + i // 2 - 1)
        ring = m // lats
        right = (lax.rem(ring, 2) == 1) == even_lon
        offset = lons // 2 + (ring + 1) // 2 * jnp.where(right, 1, -1)
        return lax.rem(m, lats) + jnp.where(ring == lons - 1, 1, offset * lats)

    def turn(i):
        ring = i // lats
        offset = jnp.where(even_lon, lax.rem(lons - ring, lons), ring)
        return offset * lats + lax.rem(i, lats)

    def begin(i, _):
        slot_copy(send_turn(i)).start()
        return 0

    lax.fori_loop(1, owners, begin, 0)
    total_ref[...] = jnp.zeros_like(total_ref)
    got_ref[0] = slots_ref[lon * lats + lat]

    for side in range(2):
        @pl.when(jnp.logical_not(comes[side]))
        def _():
            lat_in[side] = jnp.zeros(lat_in.shape[1:], F32)
            diag_in[side] = jnp.zeros(diag_in.shape[1:], F32)

    part = (8, CLON, CLAT)
    lane = lax.broadcasted_iota(jnp.int32, part, 2)
    sub = lax.broadcasted_iota(jnp.int32, part, 1)
    level = lax.broadcasted_iota(jnp.int32, part, 0)
    tiles = range(0, levels, 8)
    flat = (CLON, CLAT)
    flat_lane = lax.broadcasted_iota(jnp.int32, flat, 1)
    flat_sub = lax.broadcasted_iota(jnp.int32, flat, 0)
    even = (flat_lane & 1) == 0

    def collect(total, values, first):
        for i in range(8):
            l = first + i
            pair = (flat_lane >= l) & (flat_lane <= l + 1)
            total[l % 2] = jnp.where(pair, pltpu.roll(values[i], l + 1, 1), total[l % 2])

    def gather():
        return [jnp.zeros(flat, F32), jnp.zeros(flat, F32)]

    def rows_of(total):
        return (jnp.where(even, total[0], total[1]),
                pltpu.roll(jnp.where(even, total[1], total[0]), CLAT - 1, 1))

    none = jnp.zeros((1, CLON, CLAT), F32)
    packs = [gather(), gather(), gather()]
    for a in tiles:
        here = slice(a, a + 8)
        h = [horizontal_ref[d, here] for d in range(4)]
        v = (jnp.concatenate([vertical_ref[a:levels - 1], none], axis=0) if a + 8 == levels
             else vertical_ref[here])
        mingled = jnp.where(sub == last, h[0], h[1])
        for i, values in enumerate((v, jnp.where(lane == 0, h[3], h[2]), mingled)):
            collect(packs[i], values, a)
        diagonal_ref[here] = 1.0 - h[0] - h[1] - h[2] - h[3]
        weight_ref[0, here] = jnp.where(sub == 0, 0.0, pltpu.roll(h[0], 1, 1))
        weight_ref[1, here] = jnp.where(sub == last, 0.0, pltpu.roll(h[1], last, 1))
        weight_ref[2, here] = jnp.where(lane == 0, 0.0, pltpu.roll(h[2], 1, 2))
        weight_ref[3, here] = jnp.where(lane == CLAT - 1, 0.0, pltpu.roll(h[3], CLAT - 1, 2))
    packs = [rows_of(total) for total in packs]
    for side in range(2):
        lat_out[side, pairs, 0] = packs[0][side]
        lat_out[side, pairs, 1] = packs[1][side]
        pack_ref[side, 0] = packs[1][side]
        pack_ref[side, 1] = packs[2][side]

        @pl.when(towards[side])
        def _():
            lat_copy(pairs, side).start()

    def gain(i, _):
        d = turn(i)

        @pl.when(i > 0)
        def _():
            slot_copy(d).wait_recv()

        rows = jnp.concatenate([got_ref[d, :, i, :] for i in range(slot_rows)], axis=1)
        width = rows.shape[1]
        segment = rows[klevels:klevels + 1].astype(jnp.int32)
        values = rows[0:klevels]
        high = values.astype(BF16).astype(F32)
        spare = jnp.zeros((ROWS - klevels, width), F32)
        data = jnp.concatenate([high, spare, values - high, spare], axis=0).astype(BF16)
        step = jnp.broadcast_to((segment >> 10).astype(F32), data.shape).astype(BF16)
        for j in range(STEPS):
            taken_ref[j * 2 * ROWS:(j + 1) * 2 * ROWS] = jnp.where(
                step == jnp.asarray(j, BF16), data, jnp.zeros(data.shape, BF16))
        cell = lax.broadcasted_iota(jnp.int32, (CLAT, width), 0).astype(F32).astype(BF16)
        for i in range(CLON):
            key = jnp.where(((segment >> 7) & (CLON - 1)) == i, segment & (CLAT - 1), -1).astype(F32)
            key = jnp.broadcast_to(key, (CLAT, width)).astype(BF16)
            chosen_ref[i * CLAT:(i + 1) * CLAT] = jnp.where(
                key == cell, jnp.ones((), BF16), jnp.zeros((), BF16))
        total_ref[...] += lax.dot_general(
            taken_ref[...], chosen_ref[...], NT, preferred_element_type=F32)
        return 0

    lax.fori_loop(0, owners, gain, 0)
    for j in range(STEPS - 1, -1, -1):
        top = j * 2 * ROWS
        cells = total_ref[top:top + klevels] + total_ref[top + ROWS:top + ROWS + klevels]
        for i in range(CLON):
            bins_ref[j, :, i, :] = cells[:, i * CLAT:(i + 1) * CLAT]
        orbit_copy(j).start()

    def force(j, target_ref):
        bins = bins_ref[j] + other_ref[j]
        for a in tiles:
            forcing = []
            for l in range(a, a + 8):
                parts = [bins[k:k + 1] * float(weights[l, k]) for k in np.nonzero(weights[l])[0]]
                forcing.append(functools.reduce(lambda x, y: x + y, parts))
            target_ref[a:a + 8] = jnp.concatenate(forcing, axis=0)

    orbit_copy(STEPS - 1).wait_recv()
    force(STEPS - 1, forced_ref)
    orbit_copy(STEPS - 2).wait_recv()
    force(STEPS - 2, second_ref)
    flux_ref[...] = jnp.zeros_like(flux_ref)
    halo_ref[...] = jnp.zeros_like(halo_ref)

    def mix(packed):
        for a in tiles:
            low, high = max(a - 1, 0), min(a + 9, levels)
            forced = forced_ref[low:high]
            up = vertical_ref[low:high - 1] * (forced[1:] - forced[:-1])
            if a == 0:
                up = jnp.concatenate([none, up], axis=0)
            if a + 8 == levels:
                up = jnp.concatenate([up, none], axis=0)
            mixed = forced_ref[a:a + 8] + up[1:] - up[:-1]
            mixed_ref[a:a + 8] = mixed
            if packed is not None:
                collect(packed, mixed, a)

    def stencil(a):
        here = slice(a, a + 8)
        mixed = mixed_ref[here]
        return (diagonal_ref[here] * mixed
                + weight_ref[0, here] * pltpu.roll(mixed, 1, 1)
                + weight_ref[1, here] * pltpu.roll(mixed, last, 1)
                + weight_ref[2, here] * pltpu.roll(mixed, 1, 2)
                + weight_ref[3, here] * pltpu.roll(mixed, CLAT - 1, 2))

    outer = (lane == 0) | (lane == CLAT - 1)

    def weave(rows):
        south = pltpu.roll(rows[1], CLAT - 1, 1)
        return jnp.where(even, rows[0], south), jnp.where(even, south, rows[0])

    def near(woven, a):
        both = jnp.stack([pltpu.roll(woven[l % 2], -l % CLAT, 1) for l in range(a, a + 8)])
        return jnp.where(outer, both, 0.0)

    wide = (levels, CLAT)
    wide_lane = lax.broadcasted_iota(jnp.int32, wide, 1)
    wide_level = lax.broadcasted_iota(jnp.int32, wide, 0)
    blank = jnp.zeros((1, CLAT), F32)

    def upright(row):
        return jnp.sum(jnp.where(wide_lane == wide_level, jnp.broadcast_to(row, wide), 0.0),
                       axis=1, keepdims=True)

    def advance(p, _):
        packed = gather()
        mix(packed)
        packed = rows_of(packed)
        shed = []
        for side in range(2):
            out = pack_ref[side, 0] * packed[side]
            shed.append(out)
            lat_out[side, p, 0] = out
            diag_out[side, p, 0] = out
            diag_out[side, p, 1] = pack_ref[side, 1] * packed[side]

            @pl.when(towards[side])
            def _():
                diag_copy(p, side, 0).start()
                diag_copy(p, side, 1).start()

        for side in range(2):
            edge, inner = ((last, last - 1), (0, 1))[side]
            mixed = mixed_ref[:, edge, :]
            lon_out[side, p, 0] = horizontal_ref[side, :, edge, :] * mixed
            lon_out[side, p, 1] = (
                diagonal_ref[:, edge, :] * mixed
                + weight_ref[side, :, edge, :] * mixed_ref[:, inner, :]
                + weight_ref[2, :, edge, :] * pltpu.roll(mixed, 1, 1)
                + weight_ref[3, :, edge, :] * pltpu.roll(mixed, CLAT - 1, 1)
                + second_ref[:, edge, :])

        @pl.when(lon == 0)
        def _():
            lon_copy(p, 1).start()
            lon_copy(p, 0).start()

        @pl.when(lon > 0)
        def _():
            lon_copy(p, 0).start()
            lon_copy(p, 1).start()

        partial = gather()
        for a in tiles:
            here = slice(a, a + 8)
            local = stencil(a)
            if a == 0:
                flux_ref[...] += local[0]
            local = local + second_ref[here]
            forced_ref[here] = local
            collect(partial, local, a)
        partial = rows_of(partial)
        for side in range(2):
            lat_out[side, p, 1] = partial[side]

            @pl.when(towards[side])
            def _():
                lat_copy(p, side).start()

        @pl.when(p < pairs - 1)
        def _():
            j = jnp.maximum(STEPS - 3 - 2 * p, 1)
            orbit_copy(j).wait_recv()
            force(j, first_ref)
            orbit_copy(j - 1).wait_recv()
            force(j - 1, second_ref)

        @pl.when(p == 0)
        def _():
            for side in range(2):
                lon_copy(pairs, side).wait_recv()

                @pl.when(comes[side])
                def _():
                    lat_copy(pairs, side).wait_recv()

        for side in range(2):
            @pl.when(comes[side])
            def _():
                lat_copy(p, side).wait_recv()
                diag_copy(p, side, 0).wait_recv()
                diag_copy(p, side, 1).wait_recv()

        for side in range(2):
            lon_copy(p, side).wait_recv()
            edge = (0, last)[side]
            halo_ref[0, :, edge, :] = lon_in[side, p, 0]

            far = (last, 0)[side]
            corner = [upright(diag_in[i, side, p, 0, far:far + 1, :]) for i in range(2)]
            beside = (lon_in[side, p, 1] + lon_out[1 - side, p, 0]
                      + jnp.where(wide_lane == 0, corner[0], 0.0)
                      + jnp.where(wide_lane == CLAT - 1, corner[1], 0.0))
            up = lon_in[side, pairs, 0, 0:levels - 1] * (beside[1:] - beside[:-1])
            mixed = (beside + jnp.concatenate([up, blank], axis=0)
                     - jnp.concatenate([blank, up], axis=0))
            halo_ref[1, :, edge, :] = lon_in[side, pairs, 1] * mixed

        rows, later = [], []
        for side in range(2):
            rows.append(lat_in[side, p, 0])
            beside = (lat_in[side, p, 1] + shed[1 - side]
                      + jnp.where(flat_sub == 0, pltpu.roll(diag_in[side, 0, p, 1], 1, 0), 0.0)
                      + jnp.where(flat_sub == last, pltpu.roll(diag_in[side, 1, p, 1], last, 0), 0.0))
            up = lat_in[side, pairs, 0] * (pltpu.roll(beside, CLAT - 1, 1) - beside)
            mixed = beside + up - pltpu.roll(up, 1, 1)
            later.append(lat_in[side, pairs, 1] * mixed)

        rows, later = weave(rows), weave(later)
        for a in tiles:
            here = slice(a, a + 8)
            more = halo_ref[0, here] + near(rows, a)
            if a == 0:
                flux_ref[...] += more[0]
            forced_ref[here] += more
        mix(None)
        for a in tiles:
            here = slice(a, a + 8)
            result = stencil(a) + (halo_ref[1, here] + near(later, a))
            if a == 0:
                flux_ref[...] += result[0]
            adjoint_ref[here] = result
            forced_ref[here] = result + first_ref[here]
        return 0

    first_ref[...] = jnp.zeros_like(first_ref)
    lax.fori_loop(0, pairs, advance, 0)

    def finish(p, _):
        for side in range(2):
            lon_copy(p, side).wait_send()

            @pl.when(towards[side])
            def _():
                lat_copy(p, side).wait_send()

            @pl.when(towards[side] & (p < pairs))
            def _():
                diag_copy(p, side, 0).wait_send()
                diag_copy(p, side, 1).wait_send()
        return 0

    lax.fori_loop(0, pairs + 1, finish, 0)

    def done(t, _):
        orbit_copy(t).wait_send()
        return 0

    lax.fori_loop(0, STEPS, done, 0)

    def parted(d, _):
        slot_copy(d).wait_send()
        return 0

    lax.fori_loop(1, owners, parted, 0)


def per_device(kernel, residual, owner_block, column, time_step, horizontal, vertical):
    orbits, lons, lats = (lax.axis_size(name) for name in ("orbit", "lon", "lat"))
    owners = lons * lats
    klevels, count = kernel.shape
    levels = horizontal.shape[1]
    slot_rows = 4 * count // owners // CLAT
    heights = -(-(count // CLAT + slot_rows + 1) // 8) * 8
    chunks = count // CHUNK
    block, flat = (levels, CLON, CLAT), (CLON, CLAT)
    turns = STEPS // 2 + 1
    slots = (owners, klevels + 1, slot_rows, CLAT)
    bins = (STEPS, klevels, CLON, CLAT)
    width = slot_rows * CLAT
    dma, row = pltpu.SemaphoreType.DMA, pltpu.VMEM((1, count), jnp.int32)
    inputs = (kernel, residual.reshape(1, count), owner_block.reshape(1, count),
              column.reshape(1, count), time_step.reshape(1, count), horizontal, vertical)
    vmem = pl.BlockSpec(memory_space=pltpu.VMEM)
    return pl.pallas_call(
        functools.partial(whole_kernel, orbits, lons, lats, level_weights(levels, klevels)),
        out_shape=(jax.ShapeDtypeStruct(block, F32), jax.ShapeDtypeStruct(flat, F32)),
        in_specs=[pl.BlockSpec(memory_space=pltpu.HBM)] * 7,
        out_specs=(vmem, vmem),
        scratch_shapes=[
            pltpu.VMEM(kernel.shape, F32), pltpu.VMEM((1, count), F32), row, row, row,
            pltpu.VMEM(horizontal.shape, F32), pltpu.VMEM(vertical.shape, F32),
            pltpu.VMEM((chunks * owners, CHUNK), BF16),
            pltpu.VMEM((2 * ROWS, count), BF16),
            row,
            pltpu.VMEM((2 * ROWS * chunks, min(count, 4 * CHUNK)), BF16),
            pltpu.VMEM((ROWS, heights, CLAT), F32),
            pltpu.VMEM(slots, F32), pltpu.VMEM(slots, F32),
            pltpu.VMEM((2 * STEPS * ROWS, CELLS), F32),
            pltpu.VMEM((2 * STEPS * ROWS, width), BF16),
            pltpu.VMEM((CELLS, width), BF16),
            pltpu.VMEM(bins, F32), pltpu.VMEM(bins, F32),
            pltpu.VMEM(block, F32), pltpu.VMEM(block, F32), pltpu.VMEM(block, F32),
            pltpu.VMEM((4,) + block, F32),
            pltpu.VMEM(block, F32), pltpu.VMEM(block, F32), pltpu.VMEM((2,) + block, F32),
            pltpu.VMEM((2, 2) + flat, F32),
            pltpu.VMEM((2, turns, 2, levels, CLAT), F32),
            pltpu.VMEM((2, turns, 2, levels, CLAT), F32),
            pltpu.VMEM((2, turns, 2) + flat, F32),
            pltpu.VMEM((2, turns, 2) + flat, F32),
            pltpu.VMEM((2, turns, 2) + flat, F32),
            pltpu.VMEM((2, 2, turns, 2) + flat, F32),
            dma((7,)), dma((owners,)), dma((owners,)), dma((STEPS,)), dma((STEPS,)),
            dma((2, turns)), dma((2, turns)), dma((2, turns)), dma((2, turns)),
            dma((2, 2, turns)), dma((2, 2, turns)),
        ],
        compiler_params=pltpu.CompilerParams(
            collective_id=0, has_side_effects=True, vmem_limit_bytes=VMEM_LIMIT),
    )(*(pltpu.with_memory_space_constraint(x, pltpu.HBM) for x in inputs))


def solution(mesh):
    placed = (
        P(None, ("orbit", "lon", "lat")),
        P(("orbit", "lon", "lat")),
        P(("orbit", "lon", "lat"), None),
        P(("orbit", "lon", "lat")),
        P(("orbit", "lon", "lat")),
        P(None, None, "lon", "lat"),
        P(None, "lon", "lat"),
    )
    return jax.shard_map(
        per_device,
        mesh=mesh,
        in_specs=placed,
        out_specs=(P(None, "lon", "lat"), P("lon", "lat")),
        check_vma=False,
    )
```

```python
import functools

import jax
import jax.numpy as jnp
import numpy as np
from jax import lax
from jax.experimental import pallas as pl
from jax.experimental.pallas import tpu as pltpu
from jax.sharding import PartitionSpec as P

STEPS = 8
CLON = 8
CLAT = 128
CELLS = CLON * CLAT
ROWS = 24
CHUNK = 256
RELAY_LONS = 4
F32 = jnp.float32
BF16 = jnp.bfloat16
VMEM_LIMIT = 48 * 1024 * 1024
NT = (((1,), (1,)), ((), ()))


def level_weights(levels, kernel_levels):
    one = np.float32
    heights = np.arange(levels, dtype=np.float32)
    centre = np.clip((heights + one(0.5)) * one(kernel_levels) / one(levels) - one(0.5),
                     one(0), one(kernel_levels - 1))
    knots = np.arange(kernel_levels, dtype=np.float32)
    return np.maximum(one(0), one(1) - np.abs(centre[:, None] - knots[None, :]))


def split(values):
    high = values.astype(BF16)
    return high, (values - high.astype(F32)).astype(BF16)


def whole_kernel(orbits, lons, lats, weights, kernel_hbm, residual_hbm, owner_hbm, column_hbm, time_hbm,
                 horizontal_hbm, vertical_hbm, adjoint_ref, flux_ref,
                 kernel_ref, residual_ref, owner_ref, column_ref, time_ref, horizontal_ref, vertical_ref,
                 own_ref, data_ref, place_ref, left_ref, sorted_ref,
                 slots_ref, got_ref, raw_ref, shared_ref, total_ref, taken_ref, chosen_ref,
                 bins_ref, other_ref, forced_ref, mixed_ref, diagonal_ref, weight_ref,
                 first_ref, second_ref, halo_ref, pack_ref, lon_out, lon_in, lat_out, lat_in,
                 diag_out, diag_in, load_sem, slot_send, slot_recv, raw_send, raw_recv, shared_send, orbit_send, orbit_recv,
                 lon_send, lon_recv, lat_send, lat_recv, diag_send, diag_recv):
    klevels, count = kernel_hbm.shape
    owners, _, slot_rows, _ = slots_ref.shape
    chunks = count // CHUNK
    loads = [pltpu.make_async_copy(source, target, load_sem.at[i]) for i, (source, target) in enumerate(
        ((owner_hbm, owner_ref), (column_hbm, column_ref), (time_hbm, time_ref),
         (residual_hbm, residual_ref), (kernel_hbm, kernel_ref),
         (vertical_hbm, vertical_ref), (horizontal_hbm, horizontal_ref)))]
    for load in loads:
        load.start()
    heights = sorted_ref.shape[1]
    filled = count // CLAT
    sorted_ref[:, filled:, :] = jnp.zeros((ROWS, heights - filled, CLAT), F32)
    earlier = (lax.broadcasted_iota(jnp.int32, (CHUNK, CHUNK), 0)
               < lax.broadcasted_iota(jnp.int32, (CHUNK, CHUNK), 1)).astype(F32).astype(BF16)
    names = lax.broadcasted_iota(jnp.int32, (owners, CHUNK), 0)
    ones = jnp.ones((CHUNK, CLAT), F32).astype(BF16)
    before = (lax.broadcasted_iota(jnp.int32, (owners, owners), 1)
              < lax.broadcasted_iota(jnp.int32, (owners, owners), 0)).astype(F32)

    levels = adjoint_ref.shape[0]
    lon, lat, orbit = lax.axis_index("lon"), lax.axis_index("lat"), lax.axis_index("orbit")
    east, west = lax.rem(lon + 1, lons), lax.rem(lon + lons - 1, lons)
    partner = 1 - orbit
    mesh_id = pl.DeviceIdType.MESH
    pairs = STEPS // 2
    last = CLON - 1
    below, above = lat < lats - 1, lat > 0
    def peer(d):
        return lax.rem(lon + d // lats, lons), lax.rem(lat + lax.rem(d, lats), lats)

    def slot_copy(d):
        to_lon, to_lat = peer(d)
        return pltpu.make_async_remote_copy(
            src_ref=slots_ref.at[to_lon * lats + to_lat], dst_ref=got_ref.at[d],
            send_sem=slot_send.at[d], recv_sem=slot_recv.at[d],
            device_id={"lon": to_lon, "lat": to_lat}, device_id_type=mesh_id)

    relayed = lons == RELAY_LONS
    central = (lon == 1) | (lon == 2) if relayed else None
    planes = klevels + 2
    via = jnp.where(lon == 1, 3, jnp.where(lon == 2, 1, 2))

    def direct(d):
        offset = d // lats
        return jnp.logical_not(((lon == 1) & (offset >= 1) & (offset <= 2)) | ((lon == 2) & (offset >= 2)))

    def raw_copy(source, turn):
        return pltpu.make_async_remote_copy(
            src_ref=source.at[0:planes, 0:filled], dst_ref=raw_ref.at[0:planes, 0:filled],
            send_sem=raw_send.at[turn], recv_sem=raw_recv.at[0],
            device_id={"lon": (3 - lon, (lon - 1) * 3)[turn]}, device_id_type=mesh_id)

    def shared_copy(t):
        return pltpu.make_async_remote_copy(
            src_ref=shared_ref.at[t], dst_ref=got_ref.at[via * lats + t],
            send_sem=shared_send.at[t], recv_sem=slot_recv.at[via * lats + t],
            device_id={"lat": lax.rem(lat + t, lats)}, device_id_type=mesh_id)

    barrier = pltpu.get_barrier_semaphore()
    pl.semaphore_signal(barrier, inc=1, device_id={"orbit": partner}, device_id_type=mesh_id)

    def greet(d, _):
        to_lon, to_lat = peer(d)
        pl.semaphore_signal(barrier, inc=1, device_id={"lon": to_lon, "lat": to_lat},
                            device_id_type=mesh_id)
        return 0

    lax.fori_loop(1, owners, greet, 0)

    def orbit_copy(j):
        return pltpu.make_async_remote_copy(
            src_ref=bins_ref.at[j], dst_ref=other_ref.at[j],
            send_sem=orbit_send.at[j], recv_sem=orbit_recv.at[j],
            device_id={"orbit": partner}, device_id_type=mesh_id)

    def lon_copy(p, side):
        return pltpu.make_async_remote_copy(
            src_ref=lon_out.at[side, p], dst_ref=lon_in.at[side, p],
            send_sem=lon_send.at[side, p], recv_sem=lon_recv.at[side, p],
            device_id={"lon": (east, west)[side]}, device_id_type=mesh_id)

    def lat_copy(p, side):
        return pltpu.make_async_remote_copy(
            src_ref=lat_out.at[side, p], dst_ref=lat_in.at[side, p],
            send_sem=lat_send.at[side, p], recv_sem=lat_recv.at[side, p],
            device_id={"lat": (lat + 1, lat - 1)[side]}, device_id_type=mesh_id)

    def diag_copy(p, side, turn):
        return pltpu.make_async_remote_copy(
            src_ref=diag_out.at[side, p], dst_ref=diag_in.at[side, turn, p],
            send_sem=diag_send.at[side, turn, p], recv_sem=diag_recv.at[side, turn, p],
            device_id={"lon": (east, west)[turn], "lat": (lat + 1, lat - 1)[side]},
            device_id_type=mesh_id)

    towards = (below, above)
    comes = (above, below)

    loads[0].wait()
    for c in range(chunks):
        own_ref[c * owners:(c + 1) * owners] = (
            owner_ref[:, c * CHUNK:(c + 1) * CHUNK] == names).astype(F32).astype(BF16)
    inside = jnp.dot(own_ref[...], earlier, preferred_element_type=F32)
    counts = jnp.dot(own_ref[...], ones, preferred_element_type=F32)
    parts = [counts[c * owners:(c + 1) * owners] for c in range(chunks)]
    totals = functools.reduce(lambda x, y: x + y, parts)
    starts = jnp.dot(before, totals, precision=lax.Precision.HIGHEST, preferred_element_type=F32)
    carry = starts
    for c in range(chunks):
        own = own_ref[c * owners:(c + 1) * owners].astype(F32)
        wide = jnp.concatenate([carry] * (CHUNK // CLAT), axis=1)
        place_ref[:, c * CHUNK:(c + 1) * CHUNK] = jnp.sum(
            own * (inside[c * owners:(c + 1) * owners] + wide), axis=0,
            keepdims=True).astype(jnp.int32)
        carry = carry + parts[c]


    pl.semaphore_wait(barrier, owners)
    loads[5].wait()
    loads[6].wait()
    for side in range(2):
        edge = (last, 0)[side]
        lon_out[side, pairs, 0, 0:levels - 1] = vertical_ref[:, edge, :]
        lon_out[side, pairs, 0, levels - 1:] = jnp.zeros((1, CLAT), F32)
        lon_out[side, pairs, 1] = horizontal_ref[side, :, edge, :]
        lon_copy(pairs, side).start()

    for load in loads[1:5]:
        load.wait()
    high, low = split(kernel_ref[...] * residual_ref[...])
    seg_high = (time_ref[...] * CLON + column_ref[...] // CLAT).astype(F32)
    seg_low = (column_ref[...] % CLAT).astype(F32)
    spare = jnp.zeros((ROWS - klevels - 1, count), F32)
    data_ref[...] = jnp.concatenate(
        [high.astype(F32), seg_high * float(CLAT), spare, low.astype(F32), seg_low, spare],
        axis=0).astype(BF16)

    groups = count // CHUNK
    span = min(count, 4 * CHUNK)
    inner = lax.broadcasted_iota(jnp.int32, (CHUNK, span), 0).astype(F32).astype(BF16)
    none = jnp.zeros((2 * ROWS, span), BF16)
    product = None
    for c in range(count // span):
        here = slice(c * span, (c + 1) * span)
        place = place_ref[:, here]
        outer = jnp.broadcast_to((place // CHUNK).astype(F32), (2 * ROWS, span)).astype(BF16)
        offset = jnp.broadcast_to((place % CHUNK).astype(F32), (CHUNK, span)).astype(BF16)
        data = data_ref[:, here]
        for g in range(groups):
            left_ref[g * 2 * ROWS:(g + 1) * 2 * ROWS] = jnp.where(
                outer == jnp.asarray(g, BF16), data, none)
        chosen = jnp.where(offset == inner, jnp.ones((), BF16), jnp.zeros((), BF16))
        got = lax.dot_general(left_ref[...], chosen, NT, preferred_element_type=F32)
        product = got if product is None else product + got
    for g in range(groups):
        both = product[2 * ROWS * g:2 * ROWS * g + ROWS] + product[2 * ROWS * g + ROWS:2 * ROWS * (g + 1)]
        for p in range(CHUNK // CLAT):
            sorted_ref[:, g * (CHUNK // CLAT) + p, :] = both[:, p * CLAT:(p + 1) * CLAT]

    shape = (klevels + 1, slot_rows, CLAT)
    slot_lane = lax.broadcasted_iota(jnp.int32, shape, 2)
    slot = (lax.broadcasted_iota(jnp.int32, (1, slot_rows, CLAT), 1) * CLAT
            + lax.broadcasted_iota(jnp.int32, (1, slot_rows, CLAT), 2))
    def scalar(row):
        return jnp.clip(jnp.max(row).astype(jnp.int32), 0, count)

    def hand_out(source, begins, ends_at):
        row, shift = begins // CLAT, lax.rem(begins, CLAT)
        back = lax.rem(CLAT - shift, CLAT)
        one = pltpu.roll(source[0:klevels + 1, pl.ds(row, slot_rows), :], back, 2)
        two = pltpu.roll(source[0:klevels + 1, pl.ds(row + 1, slot_rows), :], back, 2)
        run = jnp.where(slot_lane < CLAT - shift, one, two)
        return run[0:klevels], jnp.where(slot < ends_at - begins, run[klevels:], -1.0)

    if relayed:
        sorted_ref[klevels + 1, 0:owners, :] = starts
        sorted_ref[klevels + 1, owners:owners + 8, :] = jnp.full((8, CLAT), float(count), F32)
        raw_ref[:, filled:, :] = jnp.zeros((ROWS, heights - filled, CLAT), F32)

        @pl.when(central)
        def _():
            raw_copy(sorted_ref, 0).start()

    first = [scalar(starts[o:o + 1]) for o in range(owners)] + [count]
    for o in range(owners):
        slots_ref[o, 0:klevels], slots_ref[o, klevels:] = hand_out(sorted_ref, first[o], first[o + 1])

    even_lon = lax.rem(lon, 2) == 0

    def send_turn(i):
        if relayed:
            early = i <= 2 * (lats - 1)
            m = jnp.where(early, i // 2, i - lats)
            ring = m // lats
            offset = jnp.where(ring == 2, 2, jnp.where((ring == 0) == even_lon, 1, 3))
            return jnp.where(early & (lax.rem(i, 2) == 0), i // 2, offset * lats + lax.rem(m, lats))
        m = jnp.where(lax.rem(i, 2) == 1, i // 2, owners // 2 + i // 2 - 1)
        ring = m // lats
        right = (lax.rem(ring, 2) == 1) == even_lon
        offset = lons // 2 + (ring + 1) // 2 * jnp.where(right, 1, -1)
        return lax.rem(m, lats) + jnp.where(ring == lons - 1, 1, offset * lats)

    def turn(i):
        ring = i // lats
        if relayed:
            offset = jnp.where(ring == 0, 0, jnp.where(ring == 3, 2, jnp.where(
                (ring == 1) == even_lon, 3, 1)))
        else:
            offset = jnp.where(even_lon, lax.rem(lons - ring, lons), ring)
        return offset * lats + lax.rem(i, lats)

    def begin(i, _):
        d = send_turn(i)
        if relayed:
            @pl.when(direct(d))
            def _():
                slot_copy(d).start()
        else:
            slot_copy(d).start()
        return 0

    lax.fori_loop(1, owners, begin, 0)

    def share():
        raw_copy(sorted_ref, 0).wait_recv()

        @pl.when(central)
        def _():
            raw_copy(raw_ref, 1).start()

        for t in range(lats):
            name = lon * lats + lax.rem(lat + t, lats)
            values, segment = hand_out(raw_ref, scalar(raw_ref[klevels + 1, pl.ds(name, 1), :]),
                                       scalar(raw_ref[klevels + 1, pl.ds(name + 1, 1), :]))
            if t == 0:
                got_ref[via * lats, 0:klevels], got_ref[via * lats, klevels:] = values, segment
            else:
                shared_ref[t, 0:klevels], shared_ref[t, klevels:] = values, segment
                shared_copy(t).start()

    total_ref[...] = jnp.zeros_like(total_ref)
    got_ref[0] = slots_ref[lon * lats + lat]

    for side in range(2):
        @pl.when(jnp.logical_not(comes[side]))
        def _():
            lat_in[side] = jnp.zeros(lat_in.shape[1:], F32)
            diag_in[side] = jnp.zeros(diag_in.shape[1:], F32)

    part = (8, CLON, CLAT)
    lane = lax.broadcasted_iota(jnp.int32, part, 2)
    sub = lax.broadcasted_iota(jnp.int32, part, 1)
    level = lax.broadcasted_iota(jnp.int32, part, 0)
    tiles = range(0, levels, 8)
    flat = (CLON, CLAT)
    flat_lane = lax.broadcasted_iota(jnp.int32, flat, 1)
    flat_sub = lax.broadcasted_iota(jnp.int32, flat, 0)
    even = (flat_lane & 1) == 0

    def collect(total, values, first):
        for i in range(8):
            l = first + i
            pair = (flat_lane >= l) & (flat_lane <= l + 1)
            total[l % 2] = jnp.where(pair, pltpu.roll(values[i], l + 1, 1), total[l % 2])

    def gather():
        return [jnp.zeros(flat, F32), jnp.zeros(flat, F32)]

    def rows_of(total):
        return (jnp.where(even, total[0], total[1]),
                pltpu.roll(jnp.where(even, total[1], total[0]), CLAT - 1, 1))

    none = jnp.zeros((1, CLON, CLAT), F32)
    packs = [gather(), gather(), gather()]
    for a in tiles:
        here = slice(a, a + 8)
        h = [horizontal_ref[d, here] for d in range(4)]
        v = (jnp.concatenate([vertical_ref[a:levels - 1], none], axis=0) if a + 8 == levels
             else vertical_ref[here])
        mingled = jnp.where(sub == last, h[0], h[1])
        for i, values in enumerate((v, jnp.where(lane == 0, h[3], h[2]), mingled)):
            collect(packs[i], values, a)
        diagonal_ref[here] = 1.0 - h[0] - h[1] - h[2] - h[3]
        weight_ref[0, here] = jnp.where(sub == 0, 0.0, pltpu.roll(h[0], 1, 1))
        weight_ref[1, here] = jnp.where(sub == last, 0.0, pltpu.roll(h[1], last, 1))
        weight_ref[2, here] = jnp.where(lane == 0, 0.0, pltpu.roll(h[2], 1, 2))
        weight_ref[3, here] = jnp.where(lane == CLAT - 1, 0.0, pltpu.roll(h[3], CLAT - 1, 2))
    packs = [rows_of(total) for total in packs]
    for side in range(2):
        lat_out[side, pairs, 0] = packs[0][side]
        lat_out[side, pairs, 1] = packs[1][side]
        pack_ref[side, 0] = packs[1][side]
        pack_ref[side, 1] = packs[2][side]

        @pl.when(towards[side])
        def _():
            lat_copy(pairs, side).start()

    def gain(i, _):
        d = turn(i)

        if relayed:
            @pl.when(i == jnp.where(central, lats, 2 * lats))
            def _():
                share()

        @pl.when((i > 0) & (d != via * lats) if relayed else i > 0)
        def _():
            slot_copy(d).wait_recv()

        rows = jnp.concatenate([got_ref[d, :, i, :] for i in range(slot_rows)], axis=1)
        width = rows.shape[1]
        segment = rows[klevels:klevels + 1].astype(jnp.int32)
        values = rows[0:klevels]
        high = values.astype(BF16).astype(F32)
        spare = jnp.zeros((ROWS - klevels, width), F32)
        data = jnp.concatenate([high, spare, values - high, spare], axis=0).astype(BF16)
        step = jnp.broadcast_to((segment >> 10).astype(F32), data.shape).astype(BF16)
        for j in range(STEPS):
            taken_ref[j * 2 * ROWS:(j + 1) * 2 * ROWS] = jnp.where(
                step == jnp.asarray(j, BF16), data, jnp.zeros(data.shape, BF16))
        cell = lax.broadcasted_iota(jnp.int32, (CLAT, width), 0).astype(F32).astype(BF16)
        for i in range(CLON):
            key = jnp.where(((segment >> 7) & (CLON - 1)) == i, segment & (CLAT - 1), -1).astype(F32)
            key = jnp.broadcast_to(key, (CLAT, width)).astype(BF16)
            chosen_ref[i * CLAT:(i + 1) * CLAT] = jnp.where(
                key == cell, jnp.ones((), BF16), jnp.zeros((), BF16))
        total_ref[...] += lax.dot_general(
            taken_ref[...], chosen_ref[...], NT, preferred_element_type=F32)
        return 0

    lax.fori_loop(0, owners, gain, 0)
    for j in range(STEPS - 1, -1, -1):
        top = j * 2 * ROWS
        cells = total_ref[top:top + klevels] + total_ref[top + ROWS:top + ROWS + klevels]
        for i in range(CLON):
            bins_ref[j, :, i, :] = cells[:, i * CLAT:(i + 1) * CLAT]
        orbit_copy(j).start()

    def force(j, target_ref):
        bins = bins_ref[j] + other_ref[j]
        for a in tiles:
            forcing = []
            for l in range(a, a + 8):
                parts = [bins[k:k + 1] * float(weights[l, k]) for k in np.nonzero(weights[l])[0]]
                forcing.append(functools.reduce(lambda x, y: x + y, parts))
            target_ref[a:a + 8] = jnp.concatenate(forcing, axis=0)

    orbit_copy(STEPS - 1).wait_recv()
    force(STEPS - 1, forced_ref)
    orbit_copy(STEPS - 2).wait_recv()
    force(STEPS - 2, second_ref)
    flux_ref[...] = jnp.zeros_like(flux_ref)
    halo_ref[...] = jnp.zeros_like(halo_ref)

    def mix(packed):
        for a in tiles:
            low, high = max(a - 1, 0), min(a + 9, levels)
            forced = forced_ref[low:high]
            up = vertical_ref[low:high - 1] * (forced[1:] - forced[:-1])
            if a == 0:
                up = jnp.concatenate([none, up], axis=0)
            if a + 8 == levels:
                up = jnp.concatenate([up, none], axis=0)
            mixed = forced_ref[a:a + 8] + up[1:] - up[:-1]
            mixed_ref[a:a + 8] = mixed
            if packed is not None:
                collect(packed, mixed, a)

    def stencil(a):
        here = slice(a, a + 8)
        mixed = mixed_ref[here]
        return (diagonal_ref[here] * mixed
                + weight_ref[0, here] * pltpu.roll(mixed, 1, 1)
                + weight_ref[1, here] * pltpu.roll(mixed, last, 1)
                + weight_ref[2, here] * pltpu.roll(mixed, 1, 2)
                + weight_ref[3, here] * pltpu.roll(mixed, CLAT - 1, 2))

    outer = (lane == 0) | (lane == CLAT - 1)

    def weave(rows):
        south = pltpu.roll(rows[1], CLAT - 1, 1)
        return jnp.where(even, rows[0], south), jnp.where(even, south, rows[0])

    def near(woven, a):
        both = jnp.stack([pltpu.roll(woven[l % 2], -l % CLAT, 1) for l in range(a, a + 8)])
        return jnp.where(outer, both, 0.0)

    wide = (levels, CLAT)
    wide_lane = lax.broadcasted_iota(jnp.int32, wide, 1)
    wide_level = lax.broadcasted_iota(jnp.int32, wide, 0)
    blank = jnp.zeros((1, CLAT), F32)

    def upright(row):
        return jnp.sum(jnp.where(wide_lane == wide_level, jnp.broadcast_to(row, wide), 0.0),
                       axis=1, keepdims=True)

    def advance(p, _):
        packed = gather()
        mix(packed)
        packed = rows_of(packed)
        shed = []
        for side in range(2):
            out = pack_ref[side, 0] * packed[side]
            shed.append(out)
            lat_out[side, p, 0] = out
            diag_out[side, p, 0] = out
            diag_out[side, p, 1] = pack_ref[side, 1] * packed[side]

            @pl.when(towards[side])
            def _():
                diag_copy(p, side, 0).start()
                diag_copy(p, side, 1).start()

        for side in range(2):
            edge, inner = ((last, last - 1), (0, 1))[side]
            mixed = mixed_ref[:, edge, :]
            lon_out[side, p, 0] = horizontal_ref[side, :, edge, :] * mixed
            lon_out[side, p, 1] = (
                diagonal_ref[:, edge, :] * mixed
                + weight_ref[side, :, edge, :] * mixed_ref[:, inner, :]
                + weight_ref[2, :, edge, :] * pltpu.roll(mixed, 1, 1)
                + weight_ref[3, :, edge, :] * pltpu.roll(mixed, CLAT - 1, 1)
                + second_ref[:, edge, :])

        @pl.when(lon == 0)
        def _():
            lon_copy(p, 1).start()
            lon_copy(p, 0).start()

        @pl.when(lon > 0)
        def _():
            lon_copy(p, 0).start()
            lon_copy(p, 1).start()

        partial = gather()
        for a in tiles:
            here = slice(a, a + 8)
            local = stencil(a)
            if a == 0:
                flux_ref[...] += local[0]
            local = local + second_ref[here]
            forced_ref[here] = local
            collect(partial, local, a)
        partial = rows_of(partial)
        for side in range(2):
            lat_out[side, p, 1] = partial[side]

            @pl.when(towards[side])
            def _():
                lat_copy(p, side).start()

        @pl.when(p < pairs - 1)
        def _():
            j = jnp.maximum(STEPS - 3 - 2 * p, 1)
            orbit_copy(j).wait_recv()
            force(j, first_ref)
            orbit_copy(j - 1).wait_recv()
            force(j - 1, second_ref)

        @pl.when(p == 0)
        def _():
            for side in range(2):
                lon_copy(pairs, side).wait_recv()

                @pl.when(comes[side])
                def _():
                    lat_copy(pairs, side).wait_recv()

        for side in range(2):
            @pl.when(comes[side])
            def _():
                lat_copy(p, side).wait_recv()
                diag_copy(p, side, 0).wait_recv()
                diag_copy(p, side, 1).wait_recv()

        for side in range(2):
            lon_copy(p, side).wait_recv()
            edge = (0, last)[side]
            halo_ref[0, :, edge, :] = lon_in[side, p, 0]

            far = (last, 0)[side]
            corner = [upright(diag_in[i, side, p, 0, far:far + 1, :]) for i in range(2)]
            beside = (lon_in[side, p, 1] + lon_out[1 - side, p, 0]
                      + jnp.where(wide_lane == 0, corner[0], 0.0)
                      + jnp.where(wide_lane == CLAT - 1, corner[1], 0.0))
            up = lon_in[side, pairs, 0, 0:levels - 1] * (beside[1:] - beside[:-1])
            mixed = (beside + jnp.concatenate([up, blank], axis=0)
                     - jnp.concatenate([blank, up], axis=0))
            halo_ref[1, :, edge, :] = lon_in[side, pairs, 1] * mixed

        rows, later = [], []
        for side in range(2):
            rows.append(lat_in[side, p, 0])
            beside = (lat_in[side, p, 1] + shed[1 - side]
                      + jnp.where(flat_sub == 0, pltpu.roll(diag_in[side, 0, p, 1], 1, 0), 0.0)
                      + jnp.where(flat_sub == last, pltpu.roll(diag_in[side, 1, p, 1], last, 0), 0.0))
            up = lat_in[side, pairs, 0] * (pltpu.roll(beside, CLAT - 1, 1) - beside)
            mixed = beside + up - pltpu.roll(up, 1, 1)
            later.append(lat_in[side, pairs, 1] * mixed)

        rows, later = weave(rows), weave(later)
        for a in tiles:
            here = slice(a, a + 8)
            more = halo_ref[0, here] + near(rows, a)
            if a == 0:
                flux_ref[...] += more[0]
            forced_ref[here] += more
        mix(None)
        for a in tiles:
            here = slice(a, a + 8)
            result = stencil(a) + (halo_ref[1, here] + near(later, a))
            if a == 0:
                flux_ref[...] += result[0]
            adjoint_ref[here] = result
            forced_ref[here] = result + first_ref[here]
        return 0

    first_ref[...] = jnp.zeros_like(first_ref)
    lax.fori_loop(0, pairs, advance, 0)

    def finish(p, _):
        for side in range(2):
            lon_copy(p, side).wait_send()

            @pl.when(towards[side])
            def _():
                lat_copy(p, side).wait_send()

            @pl.when(towards[side] & (p < pairs))
            def _():
                diag_copy(p, side, 0).wait_send()
                diag_copy(p, side, 1).wait_send()
        return 0

    lax.fori_loop(0, pairs + 1, finish, 0)

    def done(t, _):
        orbit_copy(t).wait_send()
        return 0

    lax.fori_loop(0, STEPS, done, 0)

    def parted(d, _):
        if relayed:
            @pl.when(direct(d))
            def _():
                slot_copy(d).wait_send()
        else:
            slot_copy(d).wait_send()
        return 0

    lax.fori_loop(1, owners, parted, 0)
    if relayed:
        for t in range(1, lats):
            shared_copy(t).wait_send()

        @pl.when(central)
        def _():
            raw_copy(sorted_ref, 0).wait_send()
            raw_copy(raw_ref, 1).wait_send()


def per_device(kernel, residual, owner_block, column, time_step, horizontal, vertical):
    orbits, lons, lats = (lax.axis_size(name) for name in ("orbit", "lon", "lat"))
    owners = lons * lats
    klevels, count = kernel.shape
    levels = horizontal.shape[1]
    slot_rows = 4 * count // owners // CLAT
    heights = -(-(count // CLAT + slot_rows + 1) // 8) * 8
    chunks = count // CHUNK
    block, flat = (levels, CLON, CLAT), (CLON, CLAT)
    turns = STEPS // 2 + 1
    slots = (owners, klevels + 1, slot_rows, CLAT)
    bins = (STEPS, klevels, CLON, CLAT)
    width = slot_rows * CLAT
    dma, row = pltpu.SemaphoreType.DMA, pltpu.VMEM((1, count), jnp.int32)
    inputs = (kernel, residual.reshape(1, count), owner_block.reshape(1, count),
              column.reshape(1, count), time_step.reshape(1, count), horizontal, vertical)
    vmem = pl.BlockSpec(memory_space=pltpu.VMEM)
    return pl.pallas_call(
        functools.partial(whole_kernel, orbits, lons, lats, level_weights(levels, klevels)),
        out_shape=(jax.ShapeDtypeStruct(block, F32), jax.ShapeDtypeStruct(flat, F32)),
        in_specs=[pl.BlockSpec(memory_space=pltpu.HBM)] * 7,
        out_specs=(vmem, vmem),
        scratch_shapes=[
            pltpu.VMEM(kernel.shape, F32), pltpu.VMEM((1, count), F32), row, row, row,
            pltpu.VMEM(horizontal.shape, F32), pltpu.VMEM(vertical.shape, F32),
            pltpu.VMEM((chunks * owners, CHUNK), BF16),
            pltpu.VMEM((2 * ROWS, count), BF16),
            row,
            pltpu.VMEM((2 * ROWS * chunks, min(count, 4 * CHUNK)), BF16),
            pltpu.VMEM((ROWS, heights, CLAT), F32),
            pltpu.VMEM(slots, F32), pltpu.VMEM(slots, F32),
            pltpu.VMEM((ROWS, heights, CLAT), F32), pltpu.VMEM((lats,) + slots[1:], F32),
            pltpu.VMEM((2 * STEPS * ROWS, CELLS), F32),
            pltpu.VMEM((2 * STEPS * ROWS, width), BF16),
            pltpu.VMEM((CELLS, width), BF16),
            pltpu.VMEM(bins, F32), pltpu.VMEM(bins, F32),
            pltpu.VMEM(block, F32), pltpu.VMEM(block, F32), pltpu.VMEM(block, F32),
            pltpu.VMEM((4,) + block, F32),
            pltpu.VMEM(block, F32), pltpu.VMEM(block, F32), pltpu.VMEM((2,) + block, F32),
            pltpu.VMEM((2, 2) + flat, F32),
            pltpu.VMEM((2, turns, 2, levels, CLAT), F32),
            pltpu.VMEM((2, turns, 2, levels, CLAT), F32),
            pltpu.VMEM((2, turns, 2) + flat, F32),
            pltpu.VMEM((2, turns, 2) + flat, F32),
            pltpu.VMEM((2, turns, 2) + flat, F32),
            pltpu.VMEM((2, 2, turns, 2) + flat, F32),
            dma((7,)), dma((owners,)), dma((owners,)), dma((2,)), dma((1,)), dma((lats,)), dma((STEPS,)), dma((STEPS,)),
            dma((2, turns)), dma((2, turns)), dma((2, turns)), dma((2, turns)),
            dma((2, 2, turns)), dma((2, 2, turns)),
        ],
        compiler_params=pltpu.CompilerParams(
            collective_id=0, has_side_effects=True, vmem_limit_bytes=VMEM_LIMIT),
    )(*(pltpu.with_memory_space_constraint(x, pltpu.HBM) for x in inputs))


def solution(mesh):
    placed = (
        P(None, ("orbit", "lon", "lat")),
        P(("orbit", "lon", "lat")),
        P(("orbit", "lon", "lat"), None),
        P(("orbit", "lon", "lat")),
        P(("orbit", "lon", "lat")),
        P(None, None, "lon", "lat"),
        P(None, "lon", "lat"),
    )
    return jax.shard_map(
        per_device,
        mesh=mesh,
        in_specs=placed,
        out_specs=(P(None, "lon", "lat"), P("lon", "lat")),
        check_vma=False,
    )
```

```python
import functools

import jax
import jax.numpy as jnp
import numpy as np
from jax import lax
from jax.experimental import pallas as pl
from jax.experimental.pallas import tpu as pltpu
from jax.sharding import PartitionSpec as P

STEPS = 8
CLON = 8
CLAT = 128
CELLS = CLON * CLAT
ROWS = 24
CHUNK = 256
F32 = jnp.float32
BF16 = jnp.bfloat16
VMEM_LIMIT = 48 * 1024 * 1024
NT = (((1,), (1,)), ((), ()))


def level_weights(levels, kernel_levels):
    one = np.float32
    heights = np.arange(levels, dtype=np.float32)
    centre = np.clip((heights + one(0.5)) * one(kernel_levels) / one(levels) - one(0.5),
                     one(0), one(kernel_levels - 1))
    knots = np.arange(kernel_levels, dtype=np.float32)
    return np.maximum(one(0), one(1) - np.abs(centre[:, None] - knots[None, :]))


def split(values):
    high = values.astype(BF16)
    return high, (values - high.astype(F32)).astype(BF16)


def whole_kernel(orbits, lons, lats, weights, kernel_hbm, residual_hbm, owner_hbm, column_hbm, time_hbm,
                 horizontal_hbm, vertical_hbm, adjoint_ref, flux_ref,
                 kernel_ref, residual_ref, owner_ref, column_ref, time_ref, horizontal_ref, vertical_ref,
                 own_ref, data_ref, place_ref, left_ref, sorted_ref,
                 slots_ref, got_ref, total_ref, taken_ref, chosen_ref,
                 bins_ref, other_ref, forced_ref, mixed_ref, diagonal_ref, weight_ref,
                 first_ref, second_ref, halo_ref, pack_ref, corner_ref, lon_out, lon_in, lat_out, lat_in,
                 diag_out, diag_in, load_sem, slot_send, slot_recv, orbit_send, orbit_recv,
                 lon_send, lon_recv, lat_send, lat_recv, diag_send, diag_recv):
    klevels, count = kernel_hbm.shape
    owners, _, slot_rows, _ = slots_ref.shape
    chunks = count // CHUNK
    loads = [pltpu.make_async_copy(source, target, load_sem.at[i]) for i, (source, target) in enumerate(
        ((owner_hbm, owner_ref), (column_hbm, column_ref), (time_hbm, time_ref),
         (residual_hbm, residual_ref), (kernel_hbm, kernel_ref),
         (vertical_hbm, vertical_ref), (horizontal_hbm, horizontal_ref)))]
    for load in loads:
        load.start()
    heights = sorted_ref.shape[1]
    filled = count // CLAT
    sorted_ref[:, filled:, :] = jnp.zeros((ROWS, heights - filled, CLAT), F32)
    earlier = (lax.broadcasted_iota(jnp.int32, (CHUNK, CHUNK), 0)
               < lax.broadcasted_iota(jnp.int32, (CHUNK, CHUNK), 1)).astype(F32).astype(BF16)
    names = lax.broadcasted_iota(jnp.int32, (owners, CHUNK), 0)
    ones = jnp.ones((CHUNK, CLAT), F32).astype(BF16)
    before = (lax.broadcasted_iota(jnp.int32, (owners, owners), 1)
              < lax.broadcasted_iota(jnp.int32, (owners, owners), 0)).astype(F32)

    levels = adjoint_ref.shape[0]
    lon, lat, orbit = lax.axis_index("lon"), lax.axis_index("lat"), lax.axis_index("orbit")
    east, west = lax.rem(lon + 1, lons), lax.rem(lon + lons - 1, lons)
    partner = 1 - orbit
    mesh_id = pl.DeviceIdType.MESH
    pairs = STEPS // 2
    last = CLON - 1
    below, above = lat < lats - 1, lat > 0
    def peer(d):
        return lax.rem(lon + d // lats, lons), lax.rem(lat + lax.rem(d, lats), lats)

    def slot_copy(d):
        to_lon, to_lat = peer(d)
        return pltpu.make_async_remote_copy(
            src_ref=slots_ref.at[to_lon * lats + to_lat], dst_ref=got_ref.at[d],
            send_sem=slot_send.at[d], recv_sem=slot_recv.at[d],
            device_id={"lon": to_lon, "lat": to_lat}, device_id_type=mesh_id)

    barrier = pltpu.get_barrier_semaphore()
    pl.semaphore_signal(barrier, inc=1, device_id={"orbit": partner}, device_id_type=mesh_id)

    def greet(d, _):
        to_lon, to_lat = peer(d)
        pl.semaphore_signal(barrier, inc=1, device_id={"lon": to_lon, "lat": to_lat},
                            device_id_type=mesh_id)
        return 0

    lax.fori_loop(1, owners, greet, 0)

    def orbit_copy(j):
        return pltpu.make_async_remote_copy(
            src_ref=bins_ref.at[j], dst_ref=other_ref.at[j],
            send_sem=orbit_send.at[j], recv_sem=orbit_recv.at[j],
            device_id={"orbit": partner}, device_id_type=mesh_id)

    def lon_copy(p, side):
        return pltpu.make_async_remote_copy(
            src_ref=lon_out.at[side, p], dst_ref=lon_in.at[side, p],
            send_sem=lon_send.at[side, p], recv_sem=lon_recv.at[side, p],
            device_id={"lon": (east, west)[side]}, device_id_type=mesh_id)

    def lat_copy(p, side):
        return pltpu.make_async_remote_copy(
            src_ref=lat_out.at[side, p], dst_ref=lat_in.at[side, p],
            send_sem=lat_send.at[side, p], recv_sem=lat_recv.at[side, p],
            device_id={"lat": (lat + 1, lat - 1)[side]}, device_id_type=mesh_id)

    def diag_copy(p, side, turn):
        return pltpu.make_async_remote_copy(
            src_ref=diag_out.at[side, turn, p], dst_ref=diag_in.at[side, turn, p],
            send_sem=diag_send.at[side, turn, p], recv_sem=diag_recv.at[side, turn, p],
            device_id={"lon": (east, west)[turn], "lat": (lat + 1, lat - 1)[side]},
            device_id_type=mesh_id)

    towards = (below, above)
    comes = (above, below)

    loads[0].wait()
    for c in range(chunks):
        own_ref[c * owners:(c + 1) * owners] = (
            owner_ref[:, c * CHUNK:(c + 1) * CHUNK] == names).astype(F32).astype(BF16)
    inside = jnp.dot(own_ref[...], earlier, preferred_element_type=F32)
    counts = jnp.dot(own_ref[...], ones, preferred_element_type=F32)
    parts = [counts[c * owners:(c + 1) * owners] for c in range(chunks)]
    totals = functools.reduce(lambda x, y: x + y, parts)
    starts = jnp.dot(before, totals, precision=lax.Precision.HIGHEST, preferred_element_type=F32)
    carry = starts
    for c in range(chunks):
        own = own_ref[c * owners:(c + 1) * owners].astype(F32)
        wide = jnp.concatenate([carry] * (CHUNK // CLAT), axis=1)
        place_ref[:, c * CHUNK:(c + 1) * CHUNK] = jnp.sum(
            own * (inside[c * owners:(c + 1) * owners] + wide), axis=0,
            keepdims=True).astype(jnp.int32)
        carry = carry + parts[c]


    pl.semaphore_wait(barrier, owners)
    loads[5].wait()
    loads[6].wait()
    for side in range(2):
        edge = (last, 0)[side]
        lon_out[side, pairs, 0, 0:levels - 1] = vertical_ref[:, edge, :]
        lon_out[side, pairs, 0, levels - 1:] = jnp.zeros((1, CLAT), F32)
        lon_out[side, pairs, 1] = horizontal_ref[side, :, edge, :]
        lon_copy(pairs, side).start()

    for load in loads[1:5]:
        load.wait()
    high, low = split(kernel_ref[...] * residual_ref[...])
    seg_high = (time_ref[...] * CLON + column_ref[...] // CLAT).astype(F32)
    seg_low = (column_ref[...] % CLAT).astype(F32)
    spare = jnp.zeros((ROWS - klevels - 1, count), F32)
    data_ref[...] = jnp.concatenate(
        [high.astype(F32), seg_high * float(CLAT), spare, low.astype(F32), seg_low, spare],
        axis=0).astype(BF16)

    groups = count // CHUNK
    span = min(count, 4 * CHUNK)
    inner = lax.broadcasted_iota(jnp.int32, (CHUNK, span), 0).astype(F32).astype(BF16)
    none = jnp.zeros((2 * ROWS, span), BF16)
    product = None
    for c in range(count // span):
        here = slice(c * span, (c + 1) * span)
        place = place_ref[:, here]
        outer = jnp.broadcast_to((place // CHUNK).astype(F32), (2 * ROWS, span)).astype(BF16)
        offset = jnp.broadcast_to((place % CHUNK).astype(F32), (CHUNK, span)).astype(BF16)
        data = data_ref[:, here]
        for g in range(groups):
            left_ref[g * 2 * ROWS:(g + 1) * 2 * ROWS] = jnp.where(
                outer == jnp.asarray(g, BF16), data, none)
        chosen = jnp.where(offset == inner, jnp.ones((), BF16), jnp.zeros((), BF16))
        got = lax.dot_general(left_ref[...], chosen, NT, preferred_element_type=F32)
        product = got if product is None else product + got
    for g in range(groups):
        both = product[2 * ROWS * g:2 * ROWS * g + ROWS] + product[2 * ROWS * g + ROWS:2 * ROWS * (g + 1)]
        for p in range(CHUNK // CLAT):
            sorted_ref[:, g * (CHUNK // CLAT) + p, :] = both[:, p * CLAT:(p + 1) * CLAT]

    shape = (klevels + 1, slot_rows, CLAT)
    slot_lane = lax.broadcasted_iota(jnp.int32, shape, 2)
    slot = (lax.broadcasted_iota(jnp.int32, (1, slot_rows, CLAT), 1) * CLAT
            + lax.broadcasted_iota(jnp.int32, (1, slot_rows, CLAT), 2))
    first = [jnp.clip(jnp.max(starts[o:o + 1]).astype(jnp.int32), 0, count)
             for o in range(owners)] + [count]
    for o in range(owners):
        row, shift = first[o] // CLAT, lax.rem(first[o], CLAT)
        back = lax.rem(CLAT - shift, CLAT)
        one = pltpu.roll(sorted_ref[0:klevels + 1, pl.ds(row, slot_rows), :], back, 2)
        two = pltpu.roll(sorted_ref[0:klevels + 1, pl.ds(row + 1, slot_rows), :], back, 2)
        run = jnp.where(slot_lane < CLAT - shift, one, two)
        slots_ref[o, 0:klevels] = run[0:klevels]
        slots_ref[o, klevels:] = jnp.where(slot < first[o + 1] - first[o], run[klevels:], -1.0)


    even_lon = lax.rem(lon, 2) == 0

    def send_turn(i):
        m = jnp.where(lax.rem(i, 2) == 1, i // 2, owners // 2 + i // 2 - 1)
        ring = m // lats
        right = (lax.rem(ring, 2) == 1) == even_lon
        offset = lons // 2 + (ring + 1) // 2 * jnp.where(right, 1, -1)
        return lax.rem(m, lats) + jnp.where(ring == lons - 1, 1, offset * lats)

    def turn(i):
        ring = i // lats
        offset = jnp.where(even_lon, lax.rem(lons - ring, lons), ring)
        return offset * lats + lax.rem(i, lats)

    def begin(i, _):
        slot_copy(send_turn(i)).start()
        return 0

    lax.fori_loop(1, owners, begin, 0)
    total_ref[...] = jnp.zeros_like(total_ref)
    got_ref[0] = slots_ref[lon * lats + lat]

    for side in range(2):
        @pl.when(jnp.logical_not(comes[side]))
        def _():
            lat_in[side] = jnp.zeros(lat_in.shape[1:], F32)
            diag_in[side] = jnp.zeros(diag_in.shape[1:], F32)

    part = (8, CLON, CLAT)
    lane = lax.broadcasted_iota(jnp.int32, part, 2)
    sub = lax.broadcasted_iota(jnp.int32, part, 1)
    level = lax.broadcasted_iota(jnp.int32, part, 0)
    tiles = range(0, levels, 8)
    flat = (CLON, CLAT)
    flat_lane = lax.broadcasted_iota(jnp.int32, flat, 1)
    flat_sub = lax.broadcasted_iota(jnp.int32, flat, 0)
    even = (flat_lane & 1) == 0

    def collect(total, values, first):
        for i in range(8):
            l = first + i
            pair = (flat_lane >= l) & (flat_lane <= l + 1)
            total[l % 2] = jnp.where(pair, pltpu.roll(values[i], l + 1, 1), total[l % 2])

    def gather():
        return [jnp.zeros(flat, F32), jnp.zeros(flat, F32)]

    def rows_of(total):
        return (jnp.where(even, total[0], total[1]),
                pltpu.roll(jnp.where(even, total[1], total[0]), CLAT - 1, 1))

    none = jnp.zeros((1, CLON, CLAT), F32)
    packs = [gather(), gather(), gather()]
    for a in tiles:
        here = slice(a, a + 8)
        h = [horizontal_ref[d, here] for d in range(4)]
        v = (jnp.concatenate([vertical_ref[a:levels - 1], none], axis=0) if a + 8 == levels
             else vertical_ref[here])
        mingled = jnp.where(sub == last, h[0], h[1])
        for i, values in enumerate((v, jnp.where(lane == 0, h[3], h[2]), mingled)):
            collect(packs[i], values, a)
        diagonal_ref[here] = 1.0 - h[0] - h[1] - h[2] - h[3]
        weight_ref[0, here] = jnp.where(sub == 0, 0.0, pltpu.roll(h[0], 1, 1))
        weight_ref[1, here] = jnp.where(sub == last, 0.0, pltpu.roll(h[1], last, 1))
        weight_ref[2, here] = jnp.where(lane == 0, 0.0, pltpu.roll(h[2], 1, 2))
        weight_ref[3, here] = jnp.where(lane == CLAT - 1, 0.0, pltpu.roll(h[3], CLAT - 1, 2))
    packs = [rows_of(total) for total in packs]
    for side in range(2):
        lat_out[side, pairs, 0] = packs[0][side]
        lat_out[side, pairs, 1] = packs[1][side]
        pack_ref[side, 0] = packs[1][side]
        pack_ref[side, 1] = packs[2][side]

        @pl.when(towards[side])
        def _():
            lat_copy(pairs, side).start()

    def take(i):
        d = turn(i)

        @pl.when(i > 0)
        def _():
            slot_copy(d).wait_recv()

        rows = jnp.concatenate([got_ref[d, :, i, :] for i in range(slot_rows)], axis=1)
        width = rows.shape[1]
        segment = rows[klevels:klevels + 1].astype(jnp.int32)
        values = rows[0:klevels]
        high = values.astype(BF16).astype(F32)
        spare = jnp.zeros((ROWS - klevels, width), F32)
        data = jnp.concatenate([high, spare, values - high, spare], axis=0).astype(BF16)
        step = jnp.broadcast_to((segment >> 10).astype(F32), data.shape).astype(BF16)
        for j in range(STEPS):
            taken_ref[j * 2 * ROWS:(j + 1) * 2 * ROWS] = jnp.where(
                step == jnp.asarray(j, BF16), data, jnp.zeros(data.shape, BF16))
        cell = lax.broadcasted_iota(jnp.int32, (CLAT, width), 0).astype(F32).astype(BF16)
        for i in range(CLON):
            key = jnp.where(((segment >> 7) & (CLON - 1)) == i, segment & (CLAT - 1), -1).astype(F32)
            key = jnp.broadcast_to(key, (CLAT, width)).astype(BF16)
            chosen_ref[i * CLAT:(i + 1) * CLAT] = jnp.where(
                key == cell, jnp.ones((), BF16), jnp.zeros((), BF16))

    def gain(i, _):
        take(i)
        total_ref[...] += lax.dot_general(
            taken_ref[...], chosen_ref[...], NT, preferred_element_type=F32)
        return 0

    lax.fori_loop(0, owners - 1, gain, 0)
    take(owners - 1)
    for j in range(STEPS - 1, -1, -1):
        top = j * 2 * ROWS
        if j >= STEPS - 2 or j == STEPS - 3:
            low = top if j >= STEPS - 2 else 0
            total_ref[low:top + 2 * ROWS] += lax.dot_general(
                taken_ref[low:top + 2 * ROWS], chosen_ref[...], NT, preferred_element_type=F32)
        cells = total_ref[top:top + klevels] + total_ref[top + ROWS:top + ROWS + klevels]
        for i in range(CLON):
            bins_ref[j, :, i, :] = cells[:, i * CLAT:(i + 1) * CLAT]
        orbit_copy(j).start()

    def force(j, target_ref):
        bins = bins_ref[j] + other_ref[j]
        for a in tiles:
            forcing = []
            for l in range(a, a + 8):
                parts = [bins[k:k + 1] * float(weights[l, k]) for k in np.nonzero(weights[l])[0]]
                forcing.append(functools.reduce(lambda x, y: x + y, parts))
            target_ref[a:a + 8] = jnp.concatenate(forcing, axis=0)

    orbit_copy(STEPS - 1).wait_recv()
    force(STEPS - 1, forced_ref)
    orbit_copy(STEPS - 2).wait_recv()
    force(STEPS - 2, second_ref)
    flux_ref[...] = jnp.zeros_like(flux_ref)
    halo_ref[...] = jnp.zeros_like(halo_ref)

    def mix(packed):
        for a in tiles:
            low, high = max(a - 1, 0), min(a + 9, levels)
            forced = forced_ref[low:high]
            up = vertical_ref[low:high - 1] * (forced[1:] - forced[:-1])
            if a == 0:
                up = jnp.concatenate([none, up], axis=0)
            if a + 8 == levels:
                up = jnp.concatenate([up, none], axis=0)
            mixed = forced_ref[a:a + 8] + up[1:] - up[:-1]
            mixed_ref[a:a + 8] = mixed
            if packed is not None:
                collect(packed, mixed, a)

    def stencil(a):
        here = slice(a, a + 8)
        mixed = mixed_ref[here]
        return (diagonal_ref[here] * mixed
                + weight_ref[0, here] * pltpu.roll(mixed, 1, 1)
                + weight_ref[1, here] * pltpu.roll(mixed, last, 1)
                + weight_ref[2, here] * pltpu.roll(mixed, 1, 2)
                + weight_ref[3, here] * pltpu.roll(mixed, CLAT - 1, 2))

    outer = (lane == 0) | (lane == CLAT - 1)

    def weave(rows):
        south = pltpu.roll(rows[1], CLAT - 1, 1)
        return jnp.where(even, rows[0], south), jnp.where(even, south, rows[0])

    def near(woven, a):
        both = jnp.stack([pltpu.roll(woven[l % 2], -l % CLAT, 1) for l in range(a, a + 8)])
        return jnp.where(outer, both, 0.0)

    wide = (levels, CLAT)
    wide_lane = lax.broadcasted_iota(jnp.int32, wide, 1)
    wide_level = lax.broadcasted_iota(jnp.int32, wide, 0)
    blank = jnp.zeros((1, CLAT), F32)

    def level_row(column):
        return jnp.sum(jnp.where(wide_lane == wide_level, jnp.broadcast_to(column, wide), 0.0),
                       axis=0, keepdims=True)

    def corners(first, second):
        return jnp.where(flat_sub == 0, first, jnp.where(flat_sub == last, second, 0.0))

    def mix_rows(rows, weight):
        up = weight * (pltpu.roll(rows, CLAT - 1, 1) - rows)
        return rows + up - pltpu.roll(up, 1, 1)

    def advance(p, _):
        packed = gather()
        mix(packed)
        packed = rows_of(packed)
        shed = []
        for side in range(2):
            out = pack_ref[side, 0] * packed[side]
            shed.append(out)
            lat_out[side, p, 0] = out
            mingled = pack_ref[side, 1] * packed[side]
            for turn_to in range(2):
                far = (last, 0)[turn_to]
                diag_out[side, turn_to, p, 0:1] = out[far:far + 1]
                diag_out[side, turn_to, p, 1:2] = mingled[far:far + 1]

            @pl.when(towards[side])
            def _():
                diag_copy(p, side, 0).start()
                diag_copy(p, side, 1).start()

        for side in range(2):
            edge, inner = ((last, last - 1), (0, 1))[side]
            mixed = mixed_ref[:, edge, :]
            lon_out[side, p, 0] = horizontal_ref[side, :, edge, :] * mixed
            lon_out[side, p, 1] = (
                diagonal_ref[:, edge, :] * mixed
                + weight_ref[side, :, edge, :] * mixed_ref[:, inner, :]
                + weight_ref[2, :, edge, :] * pltpu.roll(mixed, 1, 1)
                + weight_ref[3, :, edge, :] * pltpu.roll(mixed, CLAT - 1, 1)
                + second_ref[:, edge, :])

        @pl.when(lon == 0)
        def _():
            lon_copy(p, 1).start()
            lon_copy(p, 0).start()

        @pl.when(lon > 0)
        def _():
            lon_copy(p, 0).start()
            lon_copy(p, 1).start()

        partial = gather()
        for a in tiles:
            here = slice(a, a + 8)
            local = stencil(a)
            if a == 0:
                flux_ref[...] += local[0]
            local = local + second_ref[here]
            forced_ref[here] = local
            collect(partial, local, a)
        partial = rows_of(partial)
        for side in range(2):
            lat_out[side, p, 1] = partial[side]

            @pl.when(towards[side])
            def _():
                lat_copy(p, side).start()

        @pl.when(p < pairs - 1)
        def _():
            j = jnp.maximum(STEPS - 3 - 2 * p, 1)
            orbit_copy(j).wait_recv()
            force(j, first_ref)
            orbit_copy(j - 1).wait_recv()
            force(j - 1, second_ref)

        @pl.when(p == 0)
        def _():
            for side in range(2):
                lon_copy(pairs, side).wait_recv()

                @pl.when(comes[side])
                def _():
                    lat_copy(pairs, side).wait_recv()
            for side in range(2):
                end = (0, CLAT - 1)[side]
                for which in range(2):
                    corner_ref[side, which] = corners(*(
                        level_row(lon_in[turn, pairs, which, :, end:end + 1]) for turn in range(2)))

        for side in range(2):
            @pl.when(comes[side])
            def _():
                lat_copy(p, side).wait_recv()

        for side in range(2):
            lon_copy(p, side).wait_recv()
            edge = (0, last)[side]
            halo_ref[0, :, edge, :] = lon_in[side, p, 0]

            beside = lon_in[side, p, 1] + lon_out[1 - side, p, 0]
            up = lon_in[side, pairs, 0, 0:levels - 1] * (beside[1:] - beside[:-1])
            mixed = (beside + jnp.concatenate([up, blank], axis=0)
                     - jnp.concatenate([blank, up], axis=0))
            halo_ref[1, :, edge, :] = lon_in[side, pairs, 1] * mixed

        rows = weave([lat_in[side, p, 0] for side in range(2)])
        for a in tiles:
            here = slice(a, a + 8)
            more = halo_ref[0, here] + near(rows, a)
            if a == 0:
                flux_ref[...] += more[0]
            forced_ref[here] += more
        mix(None)
        for side in range(2):
            @pl.when(comes[side])
            def _():
                diag_copy(p, side, 0).wait_recv()
                diag_copy(p, side, 1).wait_recv()

        later = []
        for side in range(2):
            turned = [corners(diag_in[side, 0, p, which:which + 1],
                              diag_in[side, 1, p, which:which + 1]) for which in range(2)]
            beside = lat_in[side, p, 1] + shed[1 - side] + turned[1]
            later.append(lat_in[side, pairs, 1] * mix_rows(beside, lat_in[side, pairs, 0])
                         + corner_ref[side, 1] * mix_rows(turned[0], corner_ref[side, 0]))
        later = weave(later)
        for a in tiles:
            here = slice(a, a + 8)
            result = stencil(a) + (halo_ref[1, here] + near(later, a))
            if a == 0:
                flux_ref[...] += result[0]
            adjoint_ref[here] = result
            forced_ref[here] = result + first_ref[here]
        return 0

    first_ref[...] = jnp.zeros_like(first_ref)
    lax.fori_loop(0, pairs, advance, 0)

    def finish(p, _):
        for side in range(2):
            lon_copy(p, side).wait_send()

            @pl.when(towards[side])
            def _():
                lat_copy(p, side).wait_send()

            @pl.when(towards[side] & (p < pairs))
            def _():
                diag_copy(p, side, 0).wait_send()
                diag_copy(p, side, 1).wait_send()
        return 0

    lax.fori_loop(0, pairs + 1, finish, 0)

    def done(t, _):
        orbit_copy(t).wait_send()
        return 0

    lax.fori_loop(0, STEPS, done, 0)

    def parted(d, _):
        slot_copy(d).wait_send()
        return 0

    lax.fori_loop(1, owners, parted, 0)


def per_device(kernel, residual, owner_block, column, time_step, horizontal, vertical):
    orbits, lons, lats = (lax.axis_size(name) for name in ("orbit", "lon", "lat"))
    owners = lons * lats
    klevels, count = kernel.shape
    levels = horizontal.shape[1]
    slot_rows = 4 * count // owners // CLAT
    heights = -(-(count // CLAT + slot_rows + 1) // 8) * 8
    chunks = count // CHUNK
    block, flat = (levels, CLON, CLAT), (CLON, CLAT)
    turns = STEPS // 2 + 1
    slots = (owners, klevels + 1, slot_rows, CLAT)
    bins = (STEPS, klevels, CLON, CLAT)
    width = slot_rows * CLAT
    dma, row = pltpu.SemaphoreType.DMA, pltpu.VMEM((1, count), jnp.int32)
    inputs = (kernel, residual.reshape(1, count), owner_block.reshape(1, count),
              column.reshape(1, count), time_step.reshape(1, count), horizontal, vertical)
    vmem = pl.BlockSpec(memory_space=pltpu.VMEM)
    return pl.pallas_call(
        functools.partial(whole_kernel, orbits, lons, lats, level_weights(levels, klevels)),
        out_shape=(jax.ShapeDtypeStruct(block, F32), jax.ShapeDtypeStruct(flat, F32)),
        in_specs=[pl.BlockSpec(memory_space=pltpu.HBM)] * 7,
        out_specs=(vmem, vmem),
        scratch_shapes=[
            pltpu.VMEM(kernel.shape, F32), pltpu.VMEM((1, count), F32), row, row, row,
            pltpu.VMEM(horizontal.shape, F32), pltpu.VMEM(vertical.shape, F32),
            pltpu.VMEM((chunks * owners, CHUNK), BF16),
            pltpu.VMEM((2 * ROWS, count), BF16),
            row,
            pltpu.VMEM((2 * ROWS * chunks, min(count, 4 * CHUNK)), BF16),
            pltpu.VMEM((ROWS, heights, CLAT), F32),
            pltpu.VMEM(slots, F32), pltpu.VMEM(slots, F32),
            pltpu.VMEM((2 * STEPS * ROWS, CELLS), F32),
            pltpu.VMEM((2 * STEPS * ROWS, width), BF16),
            pltpu.VMEM((CELLS, width), BF16),
            pltpu.VMEM(bins, F32), pltpu.VMEM(bins, F32),
            pltpu.VMEM(block, F32), pltpu.VMEM(block, F32), pltpu.VMEM(block, F32),
            pltpu.VMEM((4,) + block, F32),
            pltpu.VMEM(block, F32), pltpu.VMEM(block, F32), pltpu.VMEM((2,) + block, F32),
            pltpu.VMEM((2, 2) + flat, F32),
            pltpu.VMEM((2, 2) + flat, F32),
            pltpu.VMEM((2, turns, 2, levels, CLAT), F32),
            pltpu.VMEM((2, turns, 2, levels, CLAT), F32),
            pltpu.VMEM((2, turns, 2) + flat, F32),
            pltpu.VMEM((2, turns, 2) + flat, F32),
            pltpu.VMEM((2, 2, turns, 2, CLAT), F32),
            pltpu.VMEM((2, 2, turns, 2, CLAT), F32),
            dma((7,)), dma((owners,)), dma((owners,)), dma((STEPS,)), dma((STEPS,)),
            dma((2, turns)), dma((2, turns)), dma((2, turns)), dma((2, turns)),
            dma((2, 2, turns)), dma((2, 2, turns)),
        ],
        compiler_params=pltpu.CompilerParams(
            collective_id=0, has_side_effects=True, vmem_limit_bytes=VMEM_LIMIT),
    )(*(pltpu.with_memory_space_constraint(x, pltpu.HBM) for x in inputs))


def solution(mesh):
    placed = (
        P(None, ("orbit", "lon", "lat")),
        P(("orbit", "lon", "lat")),
        P(("orbit", "lon", "lat"), None),
        P(("orbit", "lon", "lat")),
        P(("orbit", "lon", "lat")),
        P(None, None, "lon", "lat"),
        P(None, "lon", "lat"),
    )
    return jax.shard_map(
        per_device,
        mesh=mesh,
        in_specs=placed,
        out_specs=(P(None, "lon", "lat"), P("lon", "lat")),
        check_vma=False,
    )
```

```python
import functools

import jax
import jax.numpy as jnp
import numpy as np
from jax import lax
from jax.experimental import pallas as pl
from jax.experimental.pallas import tpu as pltpu
from jax.sharding import PartitionSpec as P

STEPS = 8
CLON = 8
CLAT = 128
CELLS = CLON * CLAT
ROWS = 24
CHUNK = 256
F32 = jnp.float32
BF16 = jnp.bfloat16
VMEM_LIMIT = 48 * 1024 * 1024
NT = (((1,), (1,)), ((), ()))


def level_weights(levels, kernel_levels):
    one = np.float32
    heights = np.arange(levels, dtype=np.float32)
    centre = np.clip((heights + one(0.5)) * one(kernel_levels) / one(levels) - one(0.5),
                     one(0), one(kernel_levels - 1))
    knots = np.arange(kernel_levels, dtype=np.float32)
    return np.maximum(one(0), one(1) - np.abs(centre[:, None] - knots[None, :]))


def split(values):
    high = values.astype(BF16)
    return high, (values - high.astype(F32)).astype(BF16)


def whole_kernel(orbits, lons, lats, weights, kernel_hbm, residual_hbm, owner_hbm, column_hbm, time_hbm,
                 horizontal_hbm, vertical_hbm, adjoint_ref, flux_ref,
                 kernel_ref, residual_ref, owner_ref, column_ref, time_ref, horizontal_ref, vertical_ref,
                 own_ref, data_ref, place_ref, left_ref, sorted_ref,
                 slots_ref, got_ref, total_ref, taken_ref, chosen_ref,
                 bins_ref, other_ref, forced_ref, mixed_ref, diagonal_ref, weight_ref,
                 first_ref, second_ref, halo_ref, pack_ref, corner_ref, lon_out, lon_in, lat_out, lat_in,
                 diag_out, diag_in, load_sem, slot_send, slot_recv, orbit_send, orbit_recv,
                 lon_send, lon_recv, lat_send, lat_recv, diag_send, diag_recv):
    klevels, count = kernel_hbm.shape
    owners, _, slot_rows, _ = slots_ref.shape
    chunks = count // CHUNK
    loads = [pltpu.make_async_copy(source, target, load_sem.at[i]) for i, (source, target) in enumerate(
        ((owner_hbm, owner_ref), (column_hbm, column_ref), (time_hbm, time_ref),
         (residual_hbm, residual_ref), (kernel_hbm, kernel_ref),
         (vertical_hbm, vertical_ref), (horizontal_hbm, horizontal_ref)))]
    for load in loads:
        load.start()
    heights = sorted_ref.shape[1]
    filled = count // CLAT
    sorted_ref[:, filled:, :] = jnp.zeros((ROWS, heights - filled, CLAT), F32)
    earlier = (lax.broadcasted_iota(jnp.int32, (CHUNK, CHUNK), 0)
               < lax.broadcasted_iota(jnp.int32, (CHUNK, CHUNK), 1)).astype(F32).astype(BF16)
    names = lax.broadcasted_iota(jnp.int32, (owners, CHUNK), 0)
    ones = jnp.ones((CHUNK, CLAT), F32).astype(BF16)
    before = (lax.broadcasted_iota(jnp.int32, (owners, owners), 1)
              < lax.broadcasted_iota(jnp.int32, (owners, owners), 0)).astype(F32)

    levels = adjoint_ref.shape[0]
    lon, lat, orbit = lax.axis_index("lon"), lax.axis_index("lat"), lax.axis_index("orbit")
    east, west = lax.rem(lon + 1, lons), lax.rem(lon + lons - 1, lons)
    partner = 1 - orbit
    mesh_id = pl.DeviceIdType.MESH
    pairs = STEPS // 2
    last = CLON - 1
    below, above = lat < lats - 1, lat > 0
    def peer(d):
        return lax.rem(lon + d // lats, lons), lax.rem(lat + lax.rem(d, lats), lats)

    def slot_copy(d):
        to_lon, to_lat = peer(d)
        return pltpu.make_async_remote_copy(
            src_ref=slots_ref.at[to_lon * lats + to_lat], dst_ref=got_ref.at[d],
            send_sem=slot_send.at[d], recv_sem=slot_recv.at[d],
            device_id={"lon": to_lon, "lat": to_lat}, device_id_type=mesh_id)

    barrier = pltpu.get_barrier_semaphore()
    pl.semaphore_signal(barrier, inc=1, device_id={"orbit": partner}, device_id_type=mesh_id)

    def greet(d, _):
        to_lon, to_lat = peer(d)
        pl.semaphore_signal(barrier, inc=1, device_id={"lon": to_lon, "lat": to_lat},
                            device_id_type=mesh_id)
        return 0

    lax.fori_loop(1, owners, greet, 0)

    def orbit_copy(j):
        return pltpu.make_async_remote_copy(
            src_ref=bins_ref.at[j], dst_ref=other_ref.at[j],
            send_sem=orbit_send.at[j], recv_sem=orbit_recv.at[j],
            device_id={"orbit": partner}, device_id_type=mesh_id)

    def lon_copy(p, side, which):
        return pltpu.make_async_remote_copy(
            src_ref=lon_out.at[side, p, which], dst_ref=lon_in.at[side, p, which],
            send_sem=lon_send.at[side, p, which], recv_sem=lon_recv.at[side, p, which],
            device_id={"lon": (east, west)[side]}, device_id_type=mesh_id)

    def lat_copy(p, side):
        return pltpu.make_async_remote_copy(
            src_ref=lat_out.at[side, p], dst_ref=lat_in.at[side, p],
            send_sem=lat_send.at[side, p], recv_sem=lat_recv.at[side, p],
            device_id={"lat": (lat + 1, lat - 1)[side]}, device_id_type=mesh_id)

    def diag_copy(p, side, turn):
        return pltpu.make_async_remote_copy(
            src_ref=diag_out.at[side, turn, p], dst_ref=diag_in.at[side, turn, p],
            send_sem=diag_send.at[side, turn, p], recv_sem=diag_recv.at[side, turn, p],
            device_id={"lon": (east, west)[turn], "lat": (lat + 1, lat - 1)[side]},
            device_id_type=mesh_id)

    towards = (below, above)
    comes = (above, below)

    loads[0].wait()
    for c in range(chunks):
        own_ref[c * owners:(c + 1) * owners] = (
            owner_ref[:, c * CHUNK:(c + 1) * CHUNK] == names).astype(F32).astype(BF16)
    inside = jnp.dot(own_ref[...], earlier, preferred_element_type=F32)
    counts = jnp.dot(own_ref[...], ones, preferred_element_type=F32)
    parts = [counts[c * owners:(c + 1) * owners] for c in range(chunks)]
    totals = functools.reduce(lambda x, y: x + y, parts)
    starts = jnp.dot(before, totals, precision=lax.Precision.HIGHEST, preferred_element_type=F32)
    carry = starts
    for c in range(chunks):
        own = own_ref[c * owners:(c + 1) * owners].astype(F32)
        wide = jnp.concatenate([carry] * (CHUNK // CLAT), axis=1)
        place_ref[:, c * CHUNK:(c + 1) * CHUNK] = jnp.sum(
            own * (inside[c * owners:(c + 1) * owners] + wide), axis=0,
            keepdims=True).astype(jnp.int32)
        carry = carry + parts[c]


    pl.semaphore_wait(barrier, owners)
    loads[5].wait()
    loads[6].wait()
    for side in range(2):
        edge = (last, 0)[side]
        lon_out[side, pairs, 0, 0:levels - 1] = vertical_ref[:, edge, :]
        lon_out[side, pairs, 0, levels - 1:] = jnp.zeros((1, CLAT), F32)
        lon_out[side, pairs, 1] = horizontal_ref[side, :, edge, :]
        lon_copy(pairs, side, 0).start()
        lon_copy(pairs, side, 1).start()

    for load in loads[1:5]:
        load.wait()
    high, low = split(kernel_ref[...] * residual_ref[...])
    seg_high = (time_ref[...] * CLON + column_ref[...] // CLAT).astype(F32)
    seg_low = (column_ref[...] % CLAT).astype(F32)
    spare = jnp.zeros((ROWS - klevels - 1, count), F32)
    data_ref[...] = jnp.concatenate(
        [high.astype(F32), seg_high * float(CLAT), spare, low.astype(F32), seg_low, spare],
        axis=0).astype(BF16)

    groups = count // CHUNK
    span = min(count, 4 * CHUNK)
    inner = lax.broadcasted_iota(jnp.int32, (CHUNK, span), 0).astype(F32).astype(BF16)
    none = jnp.zeros((2 * ROWS, span), BF16)
    product = None
    for c in range(count // span):
        here = slice(c * span, (c + 1) * span)
        place = place_ref[:, here]
        outer = jnp.broadcast_to((place // CHUNK).astype(F32), (2 * ROWS, span)).astype(BF16)
        offset = jnp.broadcast_to((place % CHUNK).astype(F32), (CHUNK, span)).astype(BF16)
        data = data_ref[:, here]
        for g in range(groups):
            left_ref[g * 2 * ROWS:(g + 1) * 2 * ROWS] = jnp.where(
                outer == jnp.asarray(g, BF16), data, none)
        chosen = jnp.where(offset == inner, jnp.ones((), BF16), jnp.zeros((), BF16))
        got = lax.dot_general(left_ref[...], chosen, NT, preferred_element_type=F32)
        product = got if product is None else product + got
    for g in range(groups):
        both = product[2 * ROWS * g:2 * ROWS * g + ROWS] + product[2 * ROWS * g + ROWS:2 * ROWS * (g + 1)]
        for p in range(CHUNK // CLAT):
            sorted_ref[:, g * (CHUNK // CLAT) + p, :] = both[:, p * CLAT:(p + 1) * CLAT]

    shape = (klevels + 1, slot_rows, CLAT)
    slot_lane = lax.broadcasted_iota(jnp.int32, shape, 2)
    slot = (lax.broadcasted_iota(jnp.int32, (1, slot_rows, CLAT), 1) * CLAT
            + lax.broadcasted_iota(jnp.int32, (1, slot_rows, CLAT), 2))
    first = [jnp.clip(jnp.max(starts[o:o + 1]).astype(jnp.int32), 0, count)
             for o in range(owners)] + [count]
    for o in range(owners):
        row, shift = first[o] // CLAT, lax.rem(first[o], CLAT)
        back = lax.rem(CLAT - shift, CLAT)
        one = pltpu.roll(sorted_ref[0:klevels + 1, pl.ds(row, slot_rows), :], back, 2)
        two = pltpu.roll(sorted_ref[0:klevels + 1, pl.ds(row + 1, slot_rows), :], back, 2)
        run = jnp.where(slot_lane < CLAT - shift, one, two)
        slots_ref[o, 0:klevels] = run[0:klevels]
        slots_ref[o, klevels:] = jnp.where(slot < first[o + 1] - first[o], run[klevels:], -1.0)


    even_lon = lax.rem(lon, 2) == 0

    def send_turn(i):
        m = jnp.where(lax.rem(i, 2) == 1, i // 2, owners // 2 + i // 2 - 1)
        ring = m // lats
        right = (lax.rem(ring, 2) == 1) == even_lon
        offset = lons // 2 + (ring + 1) // 2 * jnp.where(right, 1, -1)
        return lax.rem(m, lats) + jnp.where(ring == lons - 1, 1, offset * lats)

    def turn(i):
        ring = i // lats
        offset = jnp.where(even_lon, lax.rem(lons - ring, lons), ring)
        return offset * lats + lax.rem(i, lats)

    def begin(i, _):
        slot_copy(send_turn(i)).start()
        return 0

    lax.fori_loop(1, owners, begin, 0)
    total_ref[...] = jnp.zeros_like(total_ref)
    got_ref[0] = slots_ref[lon * lats + lat]

    for side in range(2):
        @pl.when(jnp.logical_not(comes[side]))
        def _():
            lat_in[side] = jnp.zeros(lat_in.shape[1:], F32)
            diag_in[side] = jnp.zeros(diag_in.shape[1:], F32)

    part = (8, CLON, CLAT)
    lane = lax.broadcasted_iota(jnp.int32, part, 2)
    sub = lax.broadcasted_iota(jnp.int32, part, 1)
    level = lax.broadcasted_iota(jnp.int32, part, 0)
    tiles = range(0, levels, 8)
    flat = (CLON, CLAT)
    flat_lane = lax.broadcasted_iota(jnp.int32, flat, 1)
    flat_sub = lax.broadcasted_iota(jnp.int32, flat, 0)
    even = (flat_lane & 1) == 0

    def collect(total, values, first):
        for i in range(8):
            l = first + i
            pair = (flat_lane >= l) & (flat_lane <= l + 1)
            total[l % 2] = jnp.where(pair, pltpu.roll(values[i], l + 1, 1), total[l % 2])

    def gather():
        return [jnp.zeros(flat, F32), jnp.zeros(flat, F32)]

    def rows_of(total):
        return (jnp.where(even, total[0], total[1]),
                pltpu.roll(jnp.where(even, total[1], total[0]), CLAT - 1, 1))

    none = jnp.zeros((1, CLON, CLAT), F32)
    packs = [gather(), gather(), gather()]
    for a in tiles:
        here = slice(a, a + 8)
        h = [horizontal_ref[d, here] for d in range(4)]
        v = (jnp.concatenate([vertical_ref[a:levels - 1], none], axis=0) if a + 8 == levels
             else vertical_ref[here])
        mingled = jnp.where(sub == last, h[0], h[1])
        for i, values in enumerate((v, jnp.where(lane == 0, h[3], h[2]), mingled)):
            collect(packs[i], values, a)
        diagonal_ref[here] = 1.0 - h[0] - h[1] - h[2] - h[3]
        weight_ref[0, here] = jnp.where(sub == 0, 0.0, pltpu.roll(h[0], 1, 1))
        weight_ref[1, here] = jnp.where(sub == last, 0.0, pltpu.roll(h[1], last, 1))
        weight_ref[2, here] = jnp.where(lane == 0, 0.0, pltpu.roll(h[2], 1, 2))
        weight_ref[3, here] = jnp.where(lane == CLAT - 1, 0.0, pltpu.roll(h[3], CLAT - 1, 2))
    packs = [rows_of(total) for total in packs]
    for side in range(2):
        lat_out[side, pairs, 0] = packs[0][side]
        lat_out[side, pairs, 1] = packs[1][side]
        pack_ref[side, 0] = packs[1][side]
        pack_ref[side, 1] = packs[2][side]

        @pl.when(towards[side])
        def _():
            lat_copy(pairs, side).start()

    def take(i):
        d = turn(i)

        @pl.when(i > 0)
        def _():
            slot_copy(d).wait_recv()

        rows = jnp.concatenate([got_ref[d, :, i, :] for i in range(slot_rows)], axis=1)
        width = rows.shape[1]
        segment = rows[klevels:klevels + 1].astype(jnp.int32)
        values = rows[0:klevels]
        high = values.astype(BF16).astype(F32)
        spare = jnp.zeros((ROWS - klevels, width), F32)
        data = jnp.concatenate([high, spare, values - high, spare], axis=0).astype(BF16)
        step = jnp.broadcast_to((segment >> 10).astype(F32), data.shape).astype(BF16)
        for j in range(STEPS):
            taken_ref[j * 2 * ROWS:(j + 1) * 2 * ROWS] = jnp.where(
                step == jnp.asarray(j, BF16), data, jnp.zeros(data.shape, BF16))
        cell = lax.broadcasted_iota(jnp.int32, (CLAT, width), 0).astype(F32).astype(BF16)
        for i in range(CLON):
            key = jnp.where(((segment >> 7) & (CLON - 1)) == i, segment & (CLAT - 1), -1).astype(F32)
            key = jnp.broadcast_to(key, (CLAT, width)).astype(BF16)
            chosen_ref[i * CLAT:(i + 1) * CLAT] = jnp.where(
                key == cell, jnp.ones((), BF16), jnp.zeros((), BF16))

    def gain(i, _):
        take(i)
        total_ref[...] += lax.dot_general(
            taken_ref[...], chosen_ref[...], NT, preferred_element_type=F32)
        return 0

    lax.fori_loop(0, owners - 1, gain, 0)
    take(owners - 1)
    for j in range(STEPS - 1, -1, -1):
        top = j * 2 * ROWS
        if j >= STEPS - 2 or j == STEPS - 3:
            low = top if j >= STEPS - 2 else 0
            total_ref[low:top + 2 * ROWS] += lax.dot_general(
                taken_ref[low:top + 2 * ROWS], chosen_ref[...], NT, preferred_element_type=F32)
        cells = total_ref[top:top + klevels] + total_ref[top + ROWS:top + ROWS + klevels]
        for i in range(CLON):
            bins_ref[j, :, i, :] = cells[:, i * CLAT:(i + 1) * CLAT]
        orbit_copy(j).start()

    def force(j, target_ref):
        bins = bins_ref[j] + other_ref[j]
        for a in tiles:
            forcing = []
            for l in range(a, a + 8):
                parts = [bins[k:k + 1] * float(weights[l, k]) for k in np.nonzero(weights[l])[0]]
                forcing.append(functools.reduce(lambda x, y: x + y, parts))
            target_ref[a:a + 8] = jnp.concatenate(forcing, axis=0)

    orbit_copy(STEPS - 1).wait_recv()
    force(STEPS - 1, forced_ref)
    orbit_copy(STEPS - 2).wait_recv()
    force(STEPS - 2, second_ref)
    flux_ref[...] = jnp.zeros_like(flux_ref)
    halo_ref[...] = jnp.zeros_like(halo_ref)

    def mix(packed):
        for a in tiles:
            low, high = max(a - 1, 0), min(a + 9, levels)
            forced = forced_ref[low:high]
            up = vertical_ref[low:high - 1] * (forced[1:] - forced[:-1])
            if a == 0:
                up = jnp.concatenate([none, up], axis=0)
            if a + 8 == levels:
                up = jnp.concatenate([up, none], axis=0)
            mixed = forced_ref[a:a + 8] + up[1:] - up[:-1]
            mixed_ref[a:a + 8] = mixed
            if packed is not None:
                collect(packed, mixed, a)

    def stencil(a):
        here = slice(a, a + 8)
        mixed = mixed_ref[here]
        return (diagonal_ref[here] * mixed
                + weight_ref[0, here] * pltpu.roll(mixed, 1, 1)
                + weight_ref[1, here] * pltpu.roll(mixed, last, 1)
                + weight_ref[2, here] * pltpu.roll(mixed, 1, 2)
                + weight_ref[3, here] * pltpu.roll(mixed, CLAT - 1, 2))

    outer = (lane == 0) | (lane == CLAT - 1)

    def weave(rows):
        south = pltpu.roll(rows[1], CLAT - 1, 1)
        return jnp.where(even, rows[0], south), jnp.where(even, south, rows[0])

    def near(woven, a):
        both = jnp.stack([pltpu.roll(woven[l % 2], -l % CLAT, 1) for l in range(a, a + 8)])
        return jnp.where(outer, both, 0.0)

    wide = (levels, CLAT)
    wide_lane = lax.broadcasted_iota(jnp.int32, wide, 1)
    wide_level = lax.broadcasted_iota(jnp.int32, wide, 0)
    blank = jnp.zeros((1, CLAT), F32)

    def level_row(column):
        return jnp.sum(jnp.where(wide_lane == wide_level, jnp.broadcast_to(column, wide), 0.0),
                       axis=0, keepdims=True)

    def corners(first, second):
        return jnp.where(flat_sub == 0, first, jnp.where(flat_sub == last, second, 0.0))

    def mix_rows(rows, weight):
        up = weight * (pltpu.roll(rows, CLAT - 1, 1) - rows)
        return rows + up - pltpu.roll(up, 1, 1)

    def advance(p, _):
        packed = gather()
        mix(packed)
        packed = rows_of(packed)
        shed = []
        for side in range(2):
            out = pack_ref[side, 0] * packed[side]
            shed.append(out)
            lat_out[side, p, 0] = out
            mingled = pack_ref[side, 1] * packed[side]
            for turn_to in range(2):
                far = (last, 0)[turn_to]
                diag_out[side, turn_to, p, 0:1] = out[far:far + 1]
                diag_out[side, turn_to, p, 1:2] = mingled[far:far + 1]

            @pl.when(towards[side])
            def _():
                diag_copy(p, side, 0).start()
                diag_copy(p, side, 1).start()

        def send_lon(which):
            @pl.when(lon == 0)
            def _():
                lon_copy(p, 1, which).start()
                lon_copy(p, 0, which).start()

            @pl.when(lon > 0)
            def _():
                lon_copy(p, 0, which).start()
                lon_copy(p, 1, which).start()

        for side in range(2):
            edge = (last, 0)[side]
            lon_out[side, p, 0] = horizontal_ref[side, :, edge, :] * mixed_ref[:, edge, :]
        send_lon(0)
        for side in range(2):
            edge, inner = ((last, last - 1), (0, 1))[side]
            mixed = mixed_ref[:, edge, :]
            lon_out[side, p, 1] = (
                diagonal_ref[:, edge, :] * mixed
                + weight_ref[side, :, edge, :] * mixed_ref[:, inner, :]
                + weight_ref[2, :, edge, :] * pltpu.roll(mixed, 1, 1)
                + weight_ref[3, :, edge, :] * pltpu.roll(mixed, CLAT - 1, 1)
                + second_ref[:, edge, :])
        send_lon(1)

        partial = gather()
        for a in tiles:
            here = slice(a, a + 8)
            local = stencil(a)
            if a == 0:
                flux_ref[...] += local[0]
            local = local + second_ref[here]
            forced_ref[here] = local
            collect(partial, local, a)
        partial = rows_of(partial)
        for side in range(2):
            lat_out[side, p, 1] = partial[side]

            @pl.when(towards[side])
            def _():
                lat_copy(p, side).start()

        @pl.when(p < pairs - 1)
        def _():
            j = jnp.maximum(STEPS - 3 - 2 * p, 1)
            orbit_copy(j).wait_recv()
            force(j, first_ref)
            orbit_copy(j - 1).wait_recv()
            force(j - 1, second_ref)

        @pl.when(p == 0)
        def _():
            for side in range(2):
                lon_copy(pairs, side, 0).wait_recv()
                lon_copy(pairs, side, 1).wait_recv()

                @pl.when(comes[side])
                def _():
                    lat_copy(pairs, side).wait_recv()
            for side in range(2):
                end = (0, CLAT - 1)[side]
                for which in range(2):
                    corner_ref[side, which] = corners(*(
                        level_row(lon_in[turn, pairs, which, :, end:end + 1]) for turn in range(2)))

        for side in range(2):
            @pl.when(comes[side])
            def _():
                lat_copy(p, side).wait_recv()

        for side in range(2):
            lon_copy(p, side, 0).wait_recv()
            halo_ref[0, :, (0, last)[side], :] = lon_in[side, p, 0]

        rows = weave([lat_in[side, p, 0] for side in range(2)])
        for a in tiles:
            here = slice(a, a + 8)
            more = halo_ref[0, here] + near(rows, a)
            if a == 0:
                flux_ref[...] += more[0]
            forced_ref[here] += more
        mix(None)
        for side in range(2):
            lon_copy(p, side, 1).wait_recv()
            beside = lon_in[side, p, 1] + lon_out[1 - side, p, 0]
            up = lon_in[side, pairs, 0, 0:levels - 1] * (beside[1:] - beside[:-1])
            mixed = (beside + jnp.concatenate([up, blank], axis=0)
                     - jnp.concatenate([blank, up], axis=0))
            halo_ref[1, :, (0, last)[side], :] = lon_in[side, pairs, 1] * mixed

        for side in range(2):
            @pl.when(comes[side])
            def _():
                diag_copy(p, side, 0).wait_recv()
                diag_copy(p, side, 1).wait_recv()

        later = []
        for side in range(2):
            turned = [corners(diag_in[side, 0, p, which:which + 1],
                              diag_in[side, 1, p, which:which + 1]) for which in range(2)]
            beside = lat_in[side, p, 1] + shed[1 - side] + turned[1]
            later.append(lat_in[side, pairs, 1] * mix_rows(beside, lat_in[side, pairs, 0])
                         + corner_ref[side, 1] * mix_rows(turned[0], corner_ref[side, 0]))
        later = weave(later)
        for a in tiles:
            here = slice(a, a + 8)
            result = stencil(a) + (halo_ref[1, here] + near(later, a))
            if a == 0:
                flux_ref[...] += result[0]
            adjoint_ref[here] = result
            forced_ref[here] = result + first_ref[here]
        return 0

    first_ref[...] = jnp.zeros_like(first_ref)
    lax.fori_loop(0, pairs, advance, 0)

    def finish(p, _):
        for side in range(2):
            lon_copy(p, side, 0).wait_send()
            lon_copy(p, side, 1).wait_send()

            @pl.when(towards[side])
            def _():
                lat_copy(p, side).wait_send()

            @pl.when(towards[side] & (p < pairs))
            def _():
                diag_copy(p, side, 0).wait_send()
                diag_copy(p, side, 1).wait_send()
        return 0

    lax.fori_loop(0, pairs + 1, finish, 0)

    def done(t, _):
        orbit_copy(t).wait_send()
        return 0

    lax.fori_loop(0, STEPS, done, 0)

    def parted(d, _):
        slot_copy(d).wait_send()
        return 0

    lax.fori_loop(1, owners, parted, 0)


def per_device(kernel, residual, owner_block, column, time_step, horizontal, vertical):
    orbits, lons, lats = (lax.axis_size(name) for name in ("orbit", "lon", "lat"))
    owners = lons * lats
    klevels, count = kernel.shape
    levels = horizontal.shape[1]
    slot_rows = 4 * count // owners // CLAT
    heights = -(-(count // CLAT + slot_rows + 1) // 8) * 8
    chunks = count // CHUNK
    block, flat = (levels, CLON, CLAT), (CLON, CLAT)
    turns = STEPS // 2 + 1
    slots = (owners, klevels + 1, slot_rows, CLAT)
    bins = (STEPS, klevels, CLON, CLAT)
    width = slot_rows * CLAT
    dma, row = pltpu.SemaphoreType.DMA, pltpu.VMEM((1, count), jnp.int32)
    inputs = (kernel, residual.reshape(1, count), owner_block.reshape(1, count),
              column.reshape(1, count), time_step.reshape(1, count), horizontal, vertical)
    vmem = pl.BlockSpec(memory_space=pltpu.VMEM)
    return pl.pallas_call(
        functools.partial(whole_kernel, orbits, lons, lats, level_weights(levels, klevels)),
        out_shape=(jax.ShapeDtypeStruct(block, F32), jax.ShapeDtypeStruct(flat, F32)),
        in_specs=[pl.BlockSpec(memory_space=pltpu.HBM)] * 7,
        out_specs=(vmem, vmem),
        scratch_shapes=[
            pltpu.VMEM(kernel.shape, F32), pltpu.VMEM((1, count), F32), row, row, row,
            pltpu.VMEM(horizontal.shape, F32), pltpu.VMEM(vertical.shape, F32),
            pltpu.VMEM((chunks * owners, CHUNK), BF16),
            pltpu.VMEM((2 * ROWS, count), BF16),
            row,
            pltpu.VMEM((2 * ROWS * chunks, min(count, 4 * CHUNK)), BF16),
            pltpu.VMEM((ROWS, heights, CLAT), F32),
            pltpu.VMEM(slots, F32), pltpu.VMEM(slots, F32),
            pltpu.VMEM((2 * STEPS * ROWS, CELLS), F32),
            pltpu.VMEM((2 * STEPS * ROWS, width), BF16),
            pltpu.VMEM((CELLS, width), BF16),
            pltpu.VMEM(bins, F32), pltpu.VMEM(bins, F32),
            pltpu.VMEM(block, F32), pltpu.VMEM(block, F32), pltpu.VMEM(block, F32),
            pltpu.VMEM((4,) + block, F32),
            pltpu.VMEM(block, F32), pltpu.VMEM(block, F32), pltpu.VMEM((2,) + block, F32),
            pltpu.VMEM((2, 2) + flat, F32),
            pltpu.VMEM((2, 2) + flat, F32),
            pltpu.VMEM((2, turns, 2, levels, CLAT), F32),
            pltpu.VMEM((2, turns, 2, levels, CLAT), F32),
            pltpu.VMEM((2, turns, 2) + flat, F32),
            pltpu.VMEM((2, turns, 2) + flat, F32),
            pltpu.VMEM((2, 2, turns, 2, CLAT), F32),
            pltpu.VMEM((2, 2, turns, 2, CLAT), F32),
            dma((7,)), dma((owners,)), dma((owners,)), dma((STEPS,)), dma((STEPS,)),
            dma((2, turns, 2)), dma((2, turns, 2)), dma((2, turns)), dma((2, turns)),
            dma((2, 2, turns)), dma((2, 2, turns)),
        ],
        compiler_params=pltpu.CompilerParams(
            collective_id=0, has_side_effects=True, vmem_limit_bytes=VMEM_LIMIT),
    )(*(pltpu.with_memory_space_constraint(x, pltpu.HBM) for x in inputs))


def solution(mesh):
    placed = (
        P(None, ("orbit", "lon", "lat")),
        P(("orbit", "lon", "lat")),
        P(("orbit", "lon", "lat"), None),
        P(("orbit", "lon", "lat")),
        P(("orbit", "lon", "lat")),
        P(None, None, "lon", "lat"),
        P(None, "lon", "lat"),
    )
    return jax.shard_map(
        per_device,
        mesh=mesh,
        in_specs=placed,
        out_specs=(P(None, "lon", "lat"), P("lon", "lat")),
        check_vma=False,
    )
```

```python
import functools

import jax
import jax.numpy as jnp
import numpy as np
from jax import lax
from jax.experimental import pallas as pl
from jax.experimental.pallas import tpu as pltpu
from jax.sharding import PartitionSpec as P

STEPS = 8
CLON = 8
CLAT = 128
CELLS = CLON * CLAT
ROWS = 24
CHUNK = 256
F32 = jnp.float32
BF16 = jnp.bfloat16
VMEM_LIMIT = 48 * 1024 * 1024
NT = (((1,), (1,)), ((), ()))


def level_weights(levels, kernel_levels):
    one = np.float32
    heights = np.arange(levels, dtype=np.float32)
    centre = np.clip((heights + one(0.5)) * one(kernel_levels) / one(levels) - one(0.5),
                     one(0), one(kernel_levels - 1))
    knots = np.arange(kernel_levels, dtype=np.float32)
    return np.maximum(one(0), one(1) - np.abs(centre[:, None] - knots[None, :]))


def split(values):
    high = values.astype(BF16)
    return high, (values - high.astype(F32)).astype(BF16)


def whole_kernel(orbits, lons, lats, weights, kernel_hbm, residual_hbm, owner_hbm, column_hbm, time_hbm,
                 horizontal_hbm, vertical_hbm, adjoint_ref, flux_ref,
                 kernel_ref, residual_ref, owner_ref, column_ref, time_ref, horizontal_ref, vertical_ref,
                 own_ref, data_ref, place_ref, left_ref, sorted_ref, bound_ref,
                 slots_ref, got_ref, total_ref, taken_ref, chosen_ref,
                 bins_ref, other_ref, forced_ref, mixed_ref, diagonal_ref, weight_ref,
                 first_ref, second_ref, halo_ref, pack_ref, corner_ref, lon_out, lon_in, lat_out, lat_in,
                 diag_out, diag_in, load_sem, slot_send, slot_recv, orbit_send, orbit_recv,
                 lon_send, lon_recv, lat_send, lat_recv, diag_send, diag_recv):
    klevels, count = kernel_hbm.shape
    owners, _, slot_rows, _ = slots_ref.shape
    chunks = count // CHUNK
    loads = [pltpu.make_async_copy(source, target, load_sem.at[i]) for i, (source, target) in enumerate(
        ((owner_hbm, owner_ref), (column_hbm, column_ref), (time_hbm, time_ref),
         (residual_hbm, residual_ref), (kernel_hbm, kernel_ref),
         (vertical_hbm, vertical_ref), (horizontal_hbm, horizontal_ref)))]
    for load in loads:
        load.start()
    heights = sorted_ref.shape[1]
    filled = count // CLAT
    sorted_ref[:, filled:, :] = jnp.zeros((ROWS, heights - filled, CLAT), F32)
    earlier = (lax.broadcasted_iota(jnp.int32, (CHUNK, CHUNK), 0)
               < lax.broadcasted_iota(jnp.int32, (CHUNK, CHUNK), 1)).astype(F32).astype(BF16)
    names = lax.broadcasted_iota(jnp.int32, (owners, CHUNK), 0)
    ones = jnp.ones((CHUNK, CLAT), F32).astype(BF16)
    before = (lax.broadcasted_iota(jnp.int32, (owners, owners), 1)
              < lax.broadcasted_iota(jnp.int32, (owners, owners), 0)).astype(F32)

    levels = adjoint_ref.shape[0]
    lon, lat, orbit = lax.axis_index("lon"), lax.axis_index("lat"), lax.axis_index("orbit")
    east, west = lax.rem(lon + 1, lons), lax.rem(lon + lons - 1, lons)
    partner = 1 - orbit
    mesh_id = pl.DeviceIdType.MESH
    pairs = STEPS // 2
    last = CLON - 1
    below, above = lat < lats - 1, lat > 0
    def peer(d):
        return lax.rem(lon + d // lats, lons), lax.rem(lat + lax.rem(d, lats), lats)

    def slot_copy(d):
        to_lon, to_lat = peer(d)
        return pltpu.make_async_remote_copy(
            src_ref=slots_ref.at[to_lon * lats + to_lat], dst_ref=got_ref.at[d],
            send_sem=slot_send.at[d], recv_sem=slot_recv.at[d],
            device_id={"lon": to_lon, "lat": to_lat}, device_id_type=mesh_id)

    barrier = pltpu.get_barrier_semaphore()
    pl.semaphore_signal(barrier, inc=1, device_id={"orbit": partner}, device_id_type=mesh_id)

    def greet(d, _):
        to_lon, to_lat = peer(d)
        pl.semaphore_signal(barrier, inc=1, device_id={"lon": to_lon, "lat": to_lat},
                            device_id_type=mesh_id)
        return 0

    lax.fori_loop(1, owners, greet, 0)

    def orbit_copy(j):
        return pltpu.make_async_remote_copy(
            src_ref=bins_ref.at[j], dst_ref=other_ref.at[j],
            send_sem=orbit_send.at[j], recv_sem=orbit_recv.at[j],
            device_id={"orbit": partner}, device_id_type=mesh_id)

    def lon_copy(p, side, which):
        return pltpu.make_async_remote_copy(
            src_ref=lon_out.at[side, p, which], dst_ref=lon_in.at[side, p, which],
            send_sem=lon_send.at[side, p, which], recv_sem=lon_recv.at[side, p, which],
            device_id={"lon": (east, west)[side]}, device_id_type=mesh_id)

    def lat_copy(p, side):
        return pltpu.make_async_remote_copy(
            src_ref=lat_out.at[side, p], dst_ref=lat_in.at[side, p],
            send_sem=lat_send.at[side, p], recv_sem=lat_recv.at[side, p],
            device_id={"lat": (lat + 1, lat - 1)[side]}, device_id_type=mesh_id)

    def diag_copy(p, side, turn):
        return pltpu.make_async_remote_copy(
            src_ref=diag_out.at[side, turn, p], dst_ref=diag_in.at[side, turn, p],
            send_sem=diag_send.at[side, turn, p], recv_sem=diag_recv.at[side, turn, p],
            device_id={"lon": (east, west)[turn], "lat": (lat + 1, lat - 1)[side]},
            device_id_type=mesh_id)

    towards = (below, above)
    comes = (above, below)

    loads[0].wait()
    for c in range(chunks):
        own_ref[c * owners:(c + 1) * owners] = (
            owner_ref[:, c * CHUNK:(c + 1) * CHUNK] == names).astype(F32).astype(BF16)
    inside = jnp.dot(own_ref[...], earlier, preferred_element_type=F32)
    counts = jnp.dot(own_ref[...], ones, preferred_element_type=F32)
    parts = [counts[c * owners:(c + 1) * owners] for c in range(chunks)]
    totals = functools.reduce(lambda x, y: x + y, parts)
    starts = jnp.dot(before, totals, precision=lax.Precision.HIGHEST, preferred_element_type=F32)
    carry = starts
    for c in range(chunks):
        own = own_ref[c * owners:(c + 1) * owners].astype(F32)
        wide = jnp.concatenate([carry] * (CHUNK // CLAT), axis=1)
        place_ref[:, c * CHUNK:(c + 1) * CHUNK] = jnp.sum(
            own * (inside[c * owners:(c + 1) * owners] + wide), axis=0,
            keepdims=True).astype(jnp.int32)
        carry = carry + parts[c]


    pl.semaphore_wait(barrier, owners)
    loads[5].wait()
    loads[6].wait()
    for side in range(2):
        edge = (last, 0)[side]
        lon_out[side, pairs, 0, 0:levels - 1] = vertical_ref[:, edge, :]
        lon_out[side, pairs, 0, levels - 1:] = jnp.zeros((1, CLAT), F32)
        lon_out[side, pairs, 1] = horizontal_ref[side, :, edge, :]
        lon_copy(pairs, side, 0).start()
        lon_copy(pairs, side, 1).start()

    for load in loads[1:5]:
        load.wait()
    high, low = split(kernel_ref[...] * residual_ref[...])
    seg_high = (time_ref[...] * CLON + column_ref[...] // CLAT).astype(F32)
    seg_low = (column_ref[...] % CLAT).astype(F32)
    spare = jnp.zeros((ROWS - klevels - 1, count), F32)
    data_ref[...] = jnp.concatenate(
        [high.astype(F32), seg_high * float(CLAT), spare, low.astype(F32), seg_low, spare],
        axis=0).astype(BF16)

    groups = count // CHUNK
    span = min(count, 4 * CHUNK)
    inner = lax.broadcasted_iota(jnp.int32, (CHUNK, span), 0).astype(F32).astype(BF16)
    none = jnp.zeros((2 * ROWS, span), BF16)
    product = None
    for c in range(count // span):
        here = slice(c * span, (c + 1) * span)
        place = place_ref[:, here]
        outer = jnp.broadcast_to((place // CHUNK).astype(F32), (2 * ROWS, span)).astype(BF16)
        offset = jnp.broadcast_to((place % CHUNK).astype(F32), (CHUNK, span)).astype(BF16)
        data = data_ref[:, here]
        for g in range(groups):
            left_ref[g * 2 * ROWS:(g + 1) * 2 * ROWS] = jnp.where(
                outer == jnp.asarray(g, BF16), data, none)
        chosen = jnp.where(offset == inner, jnp.ones((), BF16), jnp.zeros((), BF16))
        got = lax.dot_general(left_ref[...], chosen, NT, preferred_element_type=F32)
        product = got if product is None else product + got
    for g in range(groups):
        both = product[2 * ROWS * g:2 * ROWS * g + ROWS] + product[2 * ROWS * g + ROWS:2 * ROWS * (g + 1)]
        for p in range(CHUNK // CLAT):
            sorted_ref[:, g * (CHUNK // CLAT) + p, :] = both[:, p * CLAT:(p + 1) * CLAT]

    shape = (klevels + 1, slot_rows, CLAT)
    slot_lane = lax.broadcasted_iota(jnp.int32, shape, 2)
    slot = (lax.broadcasted_iota(jnp.int32, (1, slot_rows, CLAT), 1) * CLAT
            + lax.broadcasted_iota(jnp.int32, (1, slot_rows, CLAT), 2))
    first = [jnp.clip(jnp.max(starts[o:o + 1]).astype(jnp.int32), 0, count)
             for o in range(owners)] + [count]
    for o in range(owners + 1):
        bound_ref[o] = first[o]

    def hand_out(o, into):
        begins = bound_ref[o]
        row, shift = begins // CLAT, lax.rem(begins, CLAT)
        back = lax.rem(CLAT - shift, CLAT)
        one = pltpu.roll(sorted_ref[0:klevels + 1, pl.ds(row, slot_rows), :], back, 2)
        two = pltpu.roll(sorted_ref[0:klevels + 1, pl.ds(row + 1, slot_rows), :], back, 2)
        run = jnp.where(slot_lane < CLAT - shift, one, two)
        into[0:klevels] = run[0:klevels]
        into[klevels:] = jnp.where(slot < bound_ref[o + 1] - begins, run[klevels:], -1.0)

    even_lon = lax.rem(lon, 2) == 0

    def send_turn(i):
        m = jnp.where(lax.rem(i, 2) == 1, i // 2, owners // 2 + i // 2 - 1)
        ring = m // lats
        right = (lax.rem(ring, 2) == 1) == even_lon
        offset = lons // 2 + (ring + 1) // 2 * jnp.where(right, 1, -1)
        return lax.rem(m, lats) + jnp.where(ring == lons - 1, 1, offset * lats)

    def turn(i):
        ring = i // lats
        offset = jnp.where(even_lon, lax.rem(lons - ring, lons), ring)
        return offset * lats + lax.rem(i, lats)

    def begin(i, _):
        d = send_turn(i)
        to_lon, to_lat = peer(d)
        o = to_lon * lats + to_lat
        hand_out(o, slots_ref.at[o])
        slot_copy(d).start()
        return 0

    lax.fori_loop(1, owners, begin, 0)
    total_ref[...] = jnp.zeros_like(total_ref)
    hand_out(lon * lats + lat, got_ref.at[0])

    for side in range(2):
        @pl.when(jnp.logical_not(comes[side]))
        def _():
            lat_in[side] = jnp.zeros(lat_in.shape[1:], F32)
            diag_in[side] = jnp.zeros(diag_in.shape[1:], F32)

    part = (8, CLON, CLAT)
    lane = lax.broadcasted_iota(jnp.int32, part, 2)
    sub = lax.broadcasted_iota(jnp.int32, part, 1)
    level = lax.broadcasted_iota(jnp.int32, part, 0)
    tiles = range(0, levels, 8)
    flat = (CLON, CLAT)
    flat_lane = lax.broadcasted_iota(jnp.int32, flat, 1)
    flat_sub = lax.broadcasted_iota(jnp.int32, flat, 0)
    even = (flat_lane & 1) == 0

    def collect(total, values, first):
        for i in range(8):
            l = first + i
            pair = (flat_lane >= l) & (flat_lane <= l + 1)
            total[l % 2] = jnp.where(pair, pltpu.roll(values[i], l + 1, 1), total[l % 2])

    def gather():
        return [jnp.zeros(flat, F32), jnp.zeros(flat, F32)]

    def rows_of(total):
        return (jnp.where(even, total[0], total[1]),
                pltpu.roll(jnp.where(even, total[1], total[0]), CLAT - 1, 1))

    none = jnp.zeros((1, CLON, CLAT), F32)
    packs = [gather(), gather(), gather()]
    for a in tiles:
        here = slice(a, a + 8)
        h = [horizontal_ref[d, here] for d in range(4)]
        v = (jnp.concatenate([vertical_ref[a:levels - 1], none], axis=0) if a + 8 == levels
             else vertical_ref[here])
        mingled = jnp.where(sub == last, h[0], h[1])
        for i, values in enumerate((v, jnp.where(lane == 0, h[3], h[2]), mingled)):
            collect(packs[i], values, a)
        diagonal_ref[here] = 1.0 - h[0] - h[1] - h[2] - h[3]
        weight_ref[0, here] = jnp.where(sub == 0, 0.0, pltpu.roll(h[0], 1, 1))
        weight_ref[1, here] = jnp.where(sub == last, 0.0, pltpu.roll(h[1], last, 1))
        weight_ref[2, here] = jnp.where(lane == 0, 0.0, pltpu.roll(h[2], 1, 2))
        weight_ref[3, here] = jnp.where(lane == CLAT - 1, 0.0, pltpu.roll(h[3], CLAT - 1, 2))
    packs = [rows_of(total) for total in packs]
    for side in range(2):
        lat_out[side, pairs, 0] = packs[0][side]
        lat_out[side, pairs, 1] = packs[1][side]
        pack_ref[side, 0] = packs[1][side]
        pack_ref[side, 1] = packs[2][side]

        @pl.when(towards[side])
        def _():
            lat_copy(pairs, side).start()

    def take(i):
        d = turn(i)

        @pl.when(i > 0)
        def _():
            slot_copy(d).wait_recv()

        rows = jnp.concatenate([got_ref[d, :, i, :] for i in range(slot_rows)], axis=1)
        width = rows.shape[1]
        segment = rows[klevels:klevels + 1].astype(jnp.int32)
        values = rows[0:klevels]
        high = values.astype(BF16).astype(F32)
        spare = jnp.zeros((ROWS - klevels, width), F32)
        data = jnp.concatenate([high, spare, values - high, spare], axis=0).astype(BF16)
        step = jnp.broadcast_to((segment >> 10).astype(F32), data.shape).astype(BF16)
        for j in range(STEPS):
            taken_ref[j * 2 * ROWS:(j + 1) * 2 * ROWS] = jnp.where(
                step == jnp.asarray(j, BF16), data, jnp.zeros(data.shape, BF16))
        cell = lax.broadcasted_iota(jnp.int32, (CLAT, width), 0).astype(F32).astype(BF16)
        for i in range(CLON):
            key = jnp.where(((segment >> 7) & (CLON - 1)) == i, segment & (CLAT - 1), -1).astype(F32)
            key = jnp.broadcast_to(key, (CLAT, width)).astype(BF16)
            chosen_ref[i * CLAT:(i + 1) * CLAT] = jnp.where(
                key == cell, jnp.ones((), BF16), jnp.zeros((), BF16))

    def gain(i, _):
        take(i)
        total_ref[...] += lax.dot_general(
            taken_ref[...], chosen_ref[...], NT, preferred_element_type=F32)
        return 0

    lax.fori_loop(0, owners - 1, gain, 0)
    take(owners - 1)
    for j in range(STEPS - 1, -1, -1):
        top = j * 2 * ROWS
        if j >= STEPS - 2 or j == STEPS - 3:
            low = top if j >= STEPS - 2 else 0
            total_ref[low:top + 2 * ROWS] += lax.dot_general(
                taken_ref[low:top + 2 * ROWS], chosen_ref[...], NT, preferred_element_type=F32)
        cells = total_ref[top:top + klevels] + total_ref[top + ROWS:top + ROWS + klevels]
        for i in range(CLON):
            bins_ref[j, :, i, :] = cells[:, i * CLAT:(i + 1) * CLAT]
        orbit_copy(j).start()

    def force(j, target_ref):
        bins = bins_ref[j] + other_ref[j]
        for a in tiles:
            forcing = []
            for l in range(a, a + 8):
                parts = [bins[k:k + 1] * float(weights[l, k]) for k in np.nonzero(weights[l])[0]]
                forcing.append(functools.reduce(lambda x, y: x + y, parts))
            target_ref[a:a + 8] = jnp.concatenate(forcing, axis=0)

    orbit_copy(STEPS - 1).wait_recv()
    force(STEPS - 1, forced_ref)
    orbit_copy(STEPS - 2).wait_recv()
    force(STEPS - 2, second_ref)
    flux_ref[...] = jnp.zeros_like(flux_ref)
    halo_ref[...] = jnp.zeros_like(halo_ref)

    def mix(packed):
        for a in tiles:
            low, high = max(a - 1, 0), min(a + 9, levels)
            forced = forced_ref[low:high]
            up = vertical_ref[low:high - 1] * (forced[1:] - forced[:-1])
            if a == 0:
                up = jnp.concatenate([none, up], axis=0)
            if a + 8 == levels:
                up = jnp.concatenate([up, none], axis=0)
            mixed = forced_ref[a:a + 8] + up[1:] - up[:-1]
            mixed_ref[a:a + 8] = mixed
            if packed is not None:
                collect(packed, mixed, a)

    def stencil(a):
        here = slice(a, a + 8)
        mixed = mixed_ref[here]
        return (diagonal_ref[here] * mixed
                + weight_ref[0, here] * pltpu.roll(mixed, 1, 1)
                + weight_ref[1, here] * pltpu.roll(mixed, last, 1)
                + weight_ref[2, here] * pltpu.roll(mixed, 1, 2)
                + weight_ref[3, here] * pltpu.roll(mixed, CLAT - 1, 2))

    outer = (lane == 0) | (lane == CLAT - 1)

    def weave(rows):
        south = pltpu.roll(rows[1], CLAT - 1, 1)
        return jnp.where(even, rows[0], south), jnp.where(even, south, rows[0])

    def near(woven, a):
        both = jnp.stack([pltpu.roll(woven[l % 2], -l % CLAT, 1) for l in range(a, a + 8)])
        return jnp.where(outer, both, 0.0)

    wide = (levels, CLAT)
    wide_lane = lax.broadcasted_iota(jnp.int32, wide, 1)
    wide_level = lax.broadcasted_iota(jnp.int32, wide, 0)
    blank = jnp.zeros((1, CLAT), F32)

    def level_row(column):
        return jnp.sum(jnp.where(wide_lane == wide_level, jnp.broadcast_to(column, wide), 0.0),
                       axis=0, keepdims=True)

    def corners(first, second):
        return jnp.where(flat_sub == 0, first, jnp.where(flat_sub == last, second, 0.0))

    def mix_rows(rows, weight):
        up = weight * (pltpu.roll(rows, CLAT - 1, 1) - rows)
        return rows + up - pltpu.roll(up, 1, 1)

    def advance(p, _):
        packed = gather()
        mix(packed)
        packed = rows_of(packed)
        shed = []
        for side in range(2):
            out = pack_ref[side, 0] * packed[side]
            shed.append(out)
            lat_out[side, p, 0] = out
            mingled = pack_ref[side, 1] * packed[side]
            for turn_to in range(2):
                far = (last, 0)[turn_to]
                diag_out[side, turn_to, p, 0:1] = out[far:far + 1]
                diag_out[side, turn_to, p, 1:2] = mingled[far:far + 1]

            @pl.when(towards[side])
            def _():
                diag_copy(p, side, 0).start()
                diag_copy(p, side, 1).start()

        def send_lon(which):
            @pl.when(lon == 0)
            def _():
                lon_copy(p, 1, which).start()
                lon_copy(p, 0, which).start()

            @pl.when(lon > 0)
            def _():
                lon_copy(p, 0, which).start()
                lon_copy(p, 1, which).start()

        for side in range(2):
            edge = (last, 0)[side]
            lon_out[side, p, 0] = horizontal_ref[side, :, edge, :] * mixed_ref[:, edge, :]
        send_lon(0)
        for side in range(2):
            edge, inner = ((last, last - 1), (0, 1))[side]
            mixed = mixed_ref[:, edge, :]
            lon_out[side, p, 1] = (
                diagonal_ref[:, edge, :] * mixed
                + weight_ref[side, :, edge, :] * mixed_ref[:, inner, :]
                + weight_ref[2, :, edge, :] * pltpu.roll(mixed, 1, 1)
                + weight_ref[3, :, edge, :] * pltpu.roll(mixed, CLAT - 1, 1)
                + second_ref[:, edge, :])
        send_lon(1)

        partial = gather()
        for a in tiles:
            here = slice(a, a + 8)
            local = stencil(a)
            if a == 0:
                flux_ref[...] += local[0]
            local = local + second_ref[here]
            forced_ref[here] = local
            collect(partial, local, a)
        partial = rows_of(partial)
        for side in range(2):
            lat_out[side, p, 1] = partial[side]

            @pl.when(towards[side])
            def _():
                lat_copy(p, side).start()

        @pl.when(p < pairs - 1)
        def _():
            j = jnp.maximum(STEPS - 3 - 2 * p, 1)
            orbit_copy(j).wait_recv()
            force(j, first_ref)
            orbit_copy(j - 1).wait_recv()
            force(j - 1, second_ref)

        @pl.when(p == 0)
        def _():
            for side in range(2):
                lon_copy(pairs, side, 0).wait_recv()
                lon_copy(pairs, side, 1).wait_recv()

                @pl.when(comes[side])
                def _():
                    lat_copy(pairs, side).wait_recv()
            for side in range(2):
                end = (0, CLAT - 1)[side]
                for which in range(2):
                    corner_ref[side, which] = corners(*(
                        level_row(lon_in[turn, pairs, which, :, end:end + 1]) for turn in range(2)))

        for side in range(2):
            @pl.when(comes[side])
            def _():
                lat_copy(p, side).wait_recv()

        for side in range(2):
            lon_copy(p, side, 0).wait_recv()
            halo_ref[0, :, (0, last)[side], :] = lon_in[side, p, 0]

        rows = weave([lat_in[side, p, 0] for side in range(2)])
        for a in tiles:
            here = slice(a, a + 8)
            more = halo_ref[0, here] + near(rows, a)
            if a == 0:
                flux_ref[...] += more[0]
            forced_ref[here] += more
        mix(None)
        for side in range(2):
            lon_copy(p, side, 1).wait_recv()
            beside = lon_in[side, p, 1] + lon_out[1 - side, p, 0]
            up = lon_in[side, pairs, 0, 0:levels - 1] * (beside[1:] - beside[:-1])
            mixed = (beside + jnp.concatenate([up, blank], axis=0)
                     - jnp.concatenate([blank, up], axis=0))
            halo_ref[1, :, (0, last)[side], :] = lon_in[side, pairs, 1] * mixed

        for side in range(2):
            @pl.when(comes[side])
            def _():
                diag_copy(p, side, 0).wait_recv()
                diag_copy(p, side, 1).wait_recv()

        later = []
        for side in range(2):
            turned = [corners(diag_in[side, 0, p, which:which + 1],
                              diag_in[side, 1, p, which:which + 1]) for which in range(2)]
            beside = lat_in[side, p, 1] + shed[1 - side] + turned[1]
            later.append(lat_in[side, pairs, 1] * mix_rows(beside, lat_in[side, pairs, 0])
                         + corner_ref[side, 1] * mix_rows(turned[0], corner_ref[side, 0]))
        later = weave(later)
        for a in tiles:
            here = slice(a, a + 8)
            result = stencil(a) + (halo_ref[1, here] + near(later, a))
            if a == 0:
                flux_ref[...] += result[0]
            adjoint_ref[here] = result
            forced_ref[here] = result + first_ref[here]
        return 0

    first_ref[...] = jnp.zeros_like(first_ref)
    lax.fori_loop(0, pairs, advance, 0)

    def finish(p, _):
        for side in range(2):
            lon_copy(p, side, 0).wait_send()
            lon_copy(p, side, 1).wait_send()

            @pl.when(towards[side])
            def _():
                lat_copy(p, side).wait_send()

            @pl.when(towards[side] & (p < pairs))
            def _():
                diag_copy(p, side, 0).wait_send()
                diag_copy(p, side, 1).wait_send()
        return 0

    lax.fori_loop(0, pairs + 1, finish, 0)

    def done(t, _):
        orbit_copy(t).wait_send()
        return 0

    lax.fori_loop(0, STEPS, done, 0)

    def parted(d, _):
        slot_copy(d).wait_send()
        return 0

    lax.fori_loop(1, owners, parted, 0)


def per_device(kernel, residual, owner_block, column, time_step, horizontal, vertical):
    orbits, lons, lats = (lax.axis_size(name) for name in ("orbit", "lon", "lat"))
    owners = lons * lats
    klevels, count = kernel.shape
    levels = horizontal.shape[1]
    slot_rows = 4 * count // owners // CLAT
    heights = -(-(count // CLAT + slot_rows + 1) // 8) * 8
    chunks = count // CHUNK
    block, flat = (levels, CLON, CLAT), (CLON, CLAT)
    turns = STEPS // 2 + 1
    slots = (owners, klevels + 1, slot_rows, CLAT)
    bins = (STEPS, klevels, CLON, CLAT)
    width = slot_rows * CLAT
    dma, row = pltpu.SemaphoreType.DMA, pltpu.VMEM((1, count), jnp.int32)
    inputs = (kernel, residual.reshape(1, count), owner_block.reshape(1, count),
              column.reshape(1, count), time_step.reshape(1, count), horizontal, vertical)
    vmem = pl.BlockSpec(memory_space=pltpu.VMEM)
    return pl.pallas_call(
        functools.partial(whole_kernel, orbits, lons, lats, level_weights(levels, klevels)),
        out_shape=(jax.ShapeDtypeStruct(block, F32), jax.ShapeDtypeStruct(flat, F32)),
        in_specs=[pl.BlockSpec(memory_space=pltpu.HBM)] * 7,
        out_specs=(vmem, vmem),
        scratch_shapes=[
            pltpu.VMEM(kernel.shape, F32), pltpu.VMEM((1, count), F32), row, row, row,
            pltpu.VMEM(horizontal.shape, F32), pltpu.VMEM(vertical.shape, F32),
            pltpu.VMEM((chunks * owners, CHUNK), BF16),
            pltpu.VMEM((2 * ROWS, count), BF16),
            row,
            pltpu.VMEM((2 * ROWS * chunks, min(count, 4 * CHUNK)), BF16),
            pltpu.VMEM((ROWS, heights, CLAT), F32),
            pltpu.SMEM((owners + 1,), jnp.int32),
            pltpu.VMEM(slots, F32), pltpu.VMEM(slots, F32),
            pltpu.VMEM((2 * STEPS * ROWS, CELLS), F32),
            pltpu.VMEM((2 * STEPS * ROWS, width), BF16),
            pltpu.VMEM((CELLS, width), BF16),
            pltpu.VMEM(bins, F32), pltpu.VMEM(bins, F32),
            pltpu.VMEM(block, F32), pltpu.VMEM(block, F32), pltpu.VMEM(block, F32),
            pltpu.VMEM((4,) + block, F32),
            pltpu.VMEM(block, F32), pltpu.VMEM(block, F32), pltpu.VMEM((2,) + block, F32),
            pltpu.VMEM((2, 2) + flat, F32),
            pltpu.VMEM((2, 2) + flat, F32),
            pltpu.VMEM((2, turns, 2, levels, CLAT), F32),
            pltpu.VMEM((2, turns, 2, levels, CLAT), F32),
            pltpu.VMEM((2, turns, 2) + flat, F32),
            pltpu.VMEM((2, turns, 2) + flat, F32),
            pltpu.VMEM((2, 2, turns, 2, CLAT), F32),
            pltpu.VMEM((2, 2, turns, 2, CLAT), F32),
            dma((7,)), dma((owners,)), dma((owners,)), dma((STEPS,)), dma((STEPS,)),
            dma((2, turns, 2)), dma((2, turns, 2)), dma((2, turns)), dma((2, turns)),
            dma((2, 2, turns)), dma((2, 2, turns)),
        ],
        compiler_params=pltpu.CompilerParams(
            collective_id=0, has_side_effects=True, vmem_limit_bytes=VMEM_LIMIT),
    )(*(pltpu.with_memory_space_constraint(x, pltpu.HBM) for x in inputs))


def solution(mesh):
    placed = (
        P(None, ("orbit", "lon", "lat")),
        P(("orbit", "lon", "lat")),
        P(("orbit", "lon", "lat"), None),
        P(("orbit", "lon", "lat")),
        P(("orbit", "lon", "lat")),
        P(None, None, "lon", "lat"),
        P(None, "lon", "lat"),
    )
    return jax.shard_map(
        per_device,
        mesh=mesh,
        in_specs=placed,
        out_specs=(P(None, "lon", "lat"), P("lon", "lat")),
        check_vma=False,
    )
```
